32 devices in a mesh: row: 4 (over x, core), col: 8 (over z, y).
Axes of the slice: x: 2, y: 2, z: 4, core: 2. Of those that a mesh axis runs over, the one named last changes fastest.
Arguments:
- sample_heights: float32 [32, 512, 1024], P(None, 'row', 'col'), may hold values from -6 to 6
- depth: int32 [512, 1024], P('row', 'col'), may hold values from 5 to 200
- land_sea: int32 [512, 1024], P('row', 'col'), may hold values 0 or 1
- batch_order: int32 [4], replicated, may hold values from 0 to 3, each once
- obs_value: float32 [4, 2048], P(None, ('row', 'col')), may hold values from -8 to 8
- obs_error: float32 [4, 2048], P(None, ('row', 'col')), may hold values from 50 to 900
- obs_tile: int32 [4, 2048, 1], P(None, ('row', 'col')), may hold values from 0 to 7; in each aligned block of 64 rows (0 to 63, 64 to 127, ..., all dimensions but the last counted through in order) at most 16 rows name the same one
- obs_cell: int32 [4, 2048], P(None, ('row', 'col')), may hold values from 0 to 16383
- loc_level: int32 [4, 512, 8, 32], P(None, 'row', 'col'), may hold values from 1 to 8
Outputs:
- analysis: float32 [32, 512, 1024], P(None, 'row', 'col')
The draws below stay inside these ranges and needn't reach their ends.
Inputs may be any that keep to these rules, and one draw needn't show every extreme that they name: `obs_tile`: for each batch, of the 64 observations of one owner at most 16 lie in one column tile, and in every draw some owner has exactly 16 in some tile.
All inputs are finite; a program needn't handle non-finite values. No bound on the sum of `land_sea` on one device may be relied on, other than what follows from the above.
Results may differ from the reference program's by a relative error of at most 0.0001.
Values sent between devices are 32-bit elements; how exact they have to be, the bound alone decides.
No kernel may reach another device: no remote copies, remote signals or barrier semaphores. Data moves between devices by JAX's collectives and lax.ppermute only.
A program may use at most 128 MiB of HBM per device.

```python
import math
import jax
import jax.numpy as jnp
import numpy as np
from jax import lax

M = 32
CX = 128
CY = 128
OBS_B = 64
BATCH_COUNT = 4
STEPS = 2
SWEEPS = 2
CAP = 16
NX = 512
NY = 1024
NOBS = 2048
N_COL = 8
DEVICES = 32


def draw_obs_error(key, part):
    key = jax.random.fold_in(key, 7)
    position = jnp.arange(NOBS, dtype=jnp.float32) // OBS_B / max(DEVICES - 1, 1)
    base = jnp.exp(jax.random.uniform(key, (BATCH_COUNT, NOBS), jnp.float32, jnp.log(200.0), jnp.log(800.0)))
    scale = jnp.exp(-jnp.log(3.0) * position)
    return (base * scale[None, :]).astype(jnp.float32)


def place_ends(values, rng, least, largest):
    longest = values.shape.index(max(values.shape))
    spots = []
    for shift in (0, 1):
        where = [jax.random.randint(jax.random.fold_in(rng, axis), (), 0, length) for axis, length in enumerate(values.shape)]
        where[longest] = (where[longest] + shift) % values.shape[longest]
        spots.append(tuple(where))
    return values.at[spots[0]].set(least).at[spots[1]].set(largest)


def steps_of(rng, shape, shards, low, high):
    def one(axis_at, parts):
        draws = jax.random.uniform(jax.random.fold_in(jax.random.fold_in(rng, 6), axis_at), (parts,), jnp.float32, low / len(shards), high / len(shards))
        return jnp.repeat(jnp.exp(draws), shape[axis_at] // parts).reshape((-1,) + (1,) * (len(shape) - axis_at - 1))

    level = one(*shards[0])
    for cut in shards[1:]:
        level = level * one(*cut)
    return level


def assign_block(rng, own, number, rows, number_of, top, most, skew):
    order = jax.random.permutation(rng, number_of)
    packed, ordinary = load_shares(number_of, rows * top, most, skew, True), load_shares(number_of, rows * top, most, skew, False)
    places = jnp.arange(number_of)

    def named(lengths, rotation):
        used = int((lengths > 0).sum())
        fixed = max(1, used // 4)
        moved = fixed + (places - fixed + rotation * (used - fixed)) % max(1, number_of - fixed)
        return jnp.zeros((number_of,), jnp.int32).at[order[jnp.where(places < fixed, places, moved)]].set(jnp.asarray(lengths, jnp.int32))

    lengths = jnp.where(number % 4 == 0, named(packed, number // 4), named(ordinary, number - number // 4 - 1))
    mixed = jax.random.permutation(jax.random.fold_in(own, 3), number_of)
    donor, receiver = mixed[0:number_of // 2 * 2:2], mixed[1:number_of // 2 * 2:2]
    margin = jnp.minimum(lengths[donor] - 1, most - lengths[receiver]) // 2
    margin = jnp.where((donor == order[0]) | (receiver == order[0]) | (lengths[receiver] == 0), 0, jnp.maximum(margin, 0))
    moved = jax.random.randint(jax.random.fold_in(own, 4), (number_of // 2,), 0, 1 << 20) % (margin + 1)
    lengths = lengths.at[donor].add(-moved).at[receiver].add(moved)
    items = jnp.searchsorted(jnp.cumsum(lengths), jnp.arange(rows * top), side="right").astype(jnp.int32)
    listing = items.reshape(top, rows).T
    listing = listing[jax.random.permutation(jax.random.fold_in(own, 1), rows)]
    rotation = jax.random.randint(jax.random.fold_in(own, 2), (rows, 1), 0, top)
    return jnp.take_along_axis(listing, (jnp.arange(top)[None, :] + rotation) % top, axis=1)


def load_shares(number_of, total, reach, skew, full):
    portions = [(1 << 20) // math.isqrt(grade ** skew) + 1 for grade in range(1, number_of + 1)]
    largest = reach if full else min(reach, max(-(-total // number_of), total * portions[0] // sum(portions)))
    least = 1 if total - largest >= number_of - 1 else 0
    counts, surplus = [largest] + [least] * (number_of - 1), total - largest - least * (number_of - 1)
    while surplus > 0:
        free = [i for i in range(1, number_of) if counts[i] < largest] or [i for i in range(1, number_of) if counts[i] < reach]
        mass, left = sum([portions[i] for i in free]), surplus
        for i in free:
            more = min(reach - counts[i], max(1, left * portions[i] // mass), surplus)
            counts[i] = counts[i] + more
            surplus = surplus - more
    return np.array(counts)


def gaussian(rng, extent, spread, most, split=(), held_as=jnp.bfloat16):
    array = spread * jax.random.normal(rng, extent, jnp.float32)
    if split:
        array = array * steps_of(rng, extent, split, -0.22, 0.18)
    return jnp.clip(array, -most, most).astype(held_as)


def setup_inputs(seed: int = 0) -> dict:
    key_of = jax.random.split(jax.random.key(seed), 10)
    sample_heights = gaussian(key_of[0], (M, NX, NY), 1.0, 6.0, ((1, 4), (2, 8)), jnp.float32)
    depth = place_ends(jax.random.randint(key_of[1], (NX, NY), 5, 201), jax.random.fold_in(key_of[1], 1), 5, 200).astype(jnp.int32)
    land_sea = place_ends((jax.random.randint(key_of[2], (NX, NY), 0, 5) < 4).astype(jnp.int32), jax.random.fold_in(key_of[2], 1), 0, 1)
    batch_order = jax.random.permutation(key_of[3], BATCH_COUNT).astype(jnp.int32)
    obs_value = gaussian(key_of[4], (BATCH_COUNT, NOBS), 1.5, 8.0, ((1, 32),), jnp.float32)
    obs_error = draw_obs_error(jax.random.fold_in(key_of[9], 71), 0)
    obs_tile_keys = jax.random.split(jax.random.fold_in(key_of[6], 1), BATCH_COUNT * NOBS // OBS_B)
    obs_tile_turns = jax.random.permutation(jax.random.fold_in(key_of[6], 3), BATCH_COUNT * NOBS // OBS_B)
    obs_tile = jax.vmap(lambda own, number: assign_block(jax.random.fold_in(key_of[6], 2), own, number, OBS_B, N_COL, 1, CAP, 2))(obs_tile_keys, obs_tile_turns).reshape((BATCH_COUNT, NOBS, 1))
    obs_cell = place_ends(jax.random.randint(key_of[7], (BATCH_COUNT, NOBS), 0, CX * CY), jax.random.fold_in(key_of[7], 1), 0, (CX * CY) - 1).astype(jnp.int32)
    loc_level = place_ends(jax.random.randint(key_of[8], (BATCH_COUNT, NX, N_COL, DEVICES), 1, 9), jax.random.fold_in(key_of[8], 1), 1, 8).astype(jnp.int32)
    return {"sample_heights": sample_heights, "depth": depth, "land_sea": land_sea, "batch_order": batch_order, "obs_value": obs_value, "obs_error": obs_error, "obs_tile": obs_tile, "obs_cell": obs_cell, "loc_level": loc_level}


def face_weights(kappa, sea):
    kap_pad = jnp.pad(kappa, 1)
    sea_pad = jnp.pad(sea, 1)
    centre = kap_pad[1:-1, 1:-1]
    centre_sea = sea_pad[1:-1, 1:-1]
    filter_result = []
    for pick in (lambda a: a[:-2, 1:-1], lambda a: a[2:, 1:-1], lambda a: a[1:-1, :-2], lambda a: a[1:-1, 2:]):
        filter_result.append(0.5 * (centre + pick(kap_pad)) * centre_sea * pick(sea_pad))
    return filter_result

def neighbour_list(field):
    padded = jnp.pad(field, ((0, 0), (1, 1), (1, 1)))
    return [padded[:, :-2, 1:-1], padded[:, 2:, 1:-1], padded[:, 1:-1, :-2], padded[:, 1:-1, 2:]]

def predicted_fields(sample_collection, sample_mixing_matrix):
    wsum = sample_mixing_matrix[0] + sample_mixing_matrix[1] + sample_mixing_matrix[2] + sample_mixing_matrix[3]
    for step in range(STEPS):
        near = neighbour_list(sample_collection)
        lap = sample_mixing_matrix[0] * (near[0] - sample_collection) + sample_mixing_matrix[1] * (near[1] - sample_collection) + sample_mixing_matrix[2] * (near[2] - sample_collection) + sample_mixing_matrix[3] * (near[3] - sample_collection)
        rhs = sample_collection + 0.5 * lap
        sample_collection = rhs
        for sweep in range(SWEEPS):
            near = neighbour_list(sample_collection)
            pull = sample_mixing_matrix[0] * near[0] + sample_mixing_matrix[1] * near[1] + sample_mixing_matrix[2] * near[2] + sample_mixing_matrix[3] * near[3]
            sample_collection = (rhs + 0.5 * pull) / (1.0 + 0.5 * wsum)
    return sample_collection

def member_solve(cmat, rhs):
    cholesky_factor = jnp.linalg.cholesky(cmat)
    lower = lax.linalg.triangular_solve(cholesky_factor, rhs, left_side=True, lower=True)
    return lax.linalg.triangular_solve(cholesky_factor, lower, left_side=True, lower=True, transpose_a=True)

def reference(sample_heights, depth, land_sea, batch_order, obs_value, obs_error, obs_tile, obs_cell, loc_level):
    high = lax.Precision.HIGHEST
    sea = land_sea.astype(jnp.float32)
    kappa = 0.01 * depth.astype(jnp.float32) * sea
    sample_mixing_matrix = face_weights(kappa, sea)
    sample_collection = predicted_fields(sample_heights, sample_mixing_matrix)
    owner_row = jnp.arange(NOBS, dtype=jnp.int32) // OBS_B // N_COL
    for batch_step in range(BATCH_COUNT):
        batch_id = batch_order[batch_step]
        tiles = jnp.take(obs_tile[:, :, 0], batch_id, axis=0)
        cells = jnp.take(obs_cell, batch_id, axis=0)
        numeric_entries = jnp.take(obs_value, batch_id, axis=0)
        errors = jnp.take(obs_error, batch_id, axis=0)
        grid_row = owner_row * CX + cells // CY
        grid_col = tiles * CY + cells % CY
        prior = sample_collection[:, grid_row, grid_col].T
        ybar = jnp.mean(prior, axis=1)
        anomaly = prior - ybar[:, None]
        innov = numeric_entries - ybar
        inverse = 1.0 / errors
        cmat = jnp.einsum('jm,jn->mn', anomaly * inverse[:, None], anomaly, precision=high)
        cmat = cmat + (M - 1) * jnp.eye(M, dtype=jnp.float32)
        gvec = jnp.einsum('jm,j->m', anomaly, inverse * innov, precision=high)
        solved = member_solve(cmat, jnp.concatenate([gvec[:, None], anomaly.T], axis=1))
        zval = inverse * (innov - jnp.dot(anomaly, solved[:, 0], precision=high))
        gains = (M - 1) * inverse[:, None] * solved[:, 1:].T
        quant = jnp.concatenate([zval[:, None], gains], axis=1)
        block = jnp.einsum('ojm,ojk->omk', anomaly.reshape(DEVICES, OBS_B, M), quant.reshape(DEVICES, OBS_B, M + 1), precision=high) / (M - 1)
        levels = jnp.take(loc_level, batch_id, axis=0).astype(jnp.float32) / 8.0
        bmat = jnp.dot(levels.reshape(NX * N_COL, DEVICES), block.reshape(DEVICES, M * (M + 1)), precision=high)
        bmat = bmat.reshape(NX, N_COL, M, M + 1)
        centre = jnp.mean(sample_collection, axis=0)
        anom = sample_collection - centre[None]
        inc = jnp.einsum('mrtc,rtmk->krtc', anom.reshape(M, NX, N_COL, CY), bmat, precision=high).reshape(M + 1, NX, NY)
        sample_collection = (centre + inc[0])[None] + (anom - 0.5 * inc[1:])
    return sample_collection
```

```python
import functools

import jax
import jax.numpy as jnp
from jax import lax
from jax.experimental import pallas as pl
from jax.experimental.pallas import tpu as pltpu
from jax.sharding import PartitionSpec as P

BATCH_COUNT = 4
STEPS = 2
SWEEPS = 2
HALO = 8
SEG = 2 * HALO
LANES = 128
FIELDS = 4
HIGH = lax.Precision.HIGHEST
F32 = jnp.float32
BF16 = jnp.bfloat16
SMEM = pl.BlockSpec(memory_space=pltpu.SMEM)
VMEM = pl.BlockSpec(memory_space=pltpu.VMEM)
PARAMS = pltpu.CompilerParams(vmem_limit_bytes=48 * 1024 * 1024)


def iota(shape, dim):
    return lax.broadcasted_iota(jnp.int32, shape, dim)


def strides_of(n):
    out = []
    while n > 1:
        n //= 2
        out.append(n)
    return out


def offset_at(position, strides):
    out = position * 0
    for bit, stride in enumerate(strides):
        out = out + ((position >> bit) & 1) * stride
    return out


def position_of(offset, strides):
    out = offset * 0
    for bit, stride in enumerate(strides):
        out = out + ((offset // stride) & 1) * (1 << bit)
    return out


def gather_over(block, axis):
    n = lax.axis_size(axis)
    held = block[None]
    for stride in strides_of(n):
        other = lax.ppermute(held, axis, [(i, i ^ stride) for i in range(n)])
        held = jnp.concatenate([held, other], axis=0)
    return held


def shift_pair(low_send, high_send, axis):
    n = lax.axis_size(axis)
    forward = [(i, i + 1) for i in range(n - 1)]
    backward = [(b, a) for a, b in forward]
    return lax.ppermute(high_send, axis, forward), lax.ppermute(low_send, axis, backward)


def nt(a, b, precision=HIGH):
    return lax.dot_general(
        a, b, (((1,), (1,)), ((), ())), precision=precision, preferred_element_type=F32
    )


def split3(x):
    hi = x.astype(BF16).astype(F32)
    rest = x - hi
    mid = rest.astype(BF16).astype(F32)
    return hi, mid, rest - mid


def prep_kernel(
    order_ref, h_ref, depth_ref, sea_ref, loc_ref, val_ref, err_ref, tile_ref, cell_ref,
    to_right_ref, to_left_ref, record_ref, coef_ref,
):
    members, rows, lanes = h_ref.shape
    groups = members // 8
    seg = iota((rows, lanes), 1) // SEG
    first = iota((rows, lanes), 1) % SEG < HALO
    sea = sea_ref[...].astype(F32)
    kappa = 0.01 * depth_ref[...].astype(F32) * sea
    coef_ref[0] = kappa
    coef_ref[1] = sea

    def pack(pick):
        out = None
        for q in range(8):
            rolled = pltpu.roll(pick(q), q * SEG + HALO, axis=1)
            out = rolled if out is None else jnp.where(seg == q, rolled, out)
        return out

    half = groups // 2
    for g in range(half + 1):
        if g < half:
            a = pack(lambda q: h_ref[8 * g + q])
            b = pack(lambda q: h_ref[8 * (g + half) + q])
        else:
            a = pack(lambda q: kappa)
            b = pack(lambda q: sea)
        to_right_ref[g] = jnp.where(first, a, pltpu.roll(b, HALO, axis=1))
        to_left_ref[g] = jnp.where(first, pltpu.roll(b, lanes - HALO, axis=1), a)

    devices = loc_ref.shape[2]
    base = BATCH_COUNT * devices
    record_ref[base:, :] = jnp.zeros((record_ref.shape[0] - base, lanes), F32)
    for k in range(BATCH_COUNT):
        batch = order_ref[k]
        record_ref[k * devices : (k + 1) * devices, :] = loc_ref[batch].astype(F32).T
        width = val_ref.shape[1]
        for f, ref in enumerate((tile_ref, cell_ref, val_ref, err_ref)):
            row = base + f * BATCH_COUNT + k
            record_ref[row : row + 1, 0:width] = ref[pl.ds(batch, 1), :].astype(F32)


def forecast_kernel(
    h_ref, coef_ref, left_ref, right_ref, up_ref, down_ref, out_ref,
    a_ref, b_ref, rhs_ref, sa_ref, sb_ref, srhs_ref, k_ref, sk_ref, w_ref, sw_ref,
):
    members, rows, lanes = h_ref.shape
    groups = members // 8
    half = groups // 2
    ext = rows + 2 * HALO
    pad = HALO
    inner = pad + HALO
    block = 16
    starts = list(range(0, ext, block))

    def fill(ref, index, upper, centre, lower):
        ref[index, pl.ds(pad, HALO), :] = upper
        ref[index, pl.ds(inner, rows), :] = centre
        ref[index, pl.ds(inner + rows, HALO), :] = lower

    for ref in (k_ref, sk_ref):
        for i in range(ref.shape[0]):
            ref[i, pl.ds(0, pad), :] = jnp.zeros((pad, lanes), F32)
            ref[i, pl.ds(pad + ext, pad), :] = jnp.zeros((pad, lanes), F32)
    for i in range(2):
        fill(k_ref, i, up_ref[members + i], coef_ref[i], down_ref[members + i])

    @pl.loop(0, members)
    def _(m):
        fill(a_ref, m, up_ref[m], h_ref[m], down_ref[m])

    def strips(start, pick, at, number):
        shape = (block, lanes)
        seg = iota(shape, 1) // SEG
        first = iota(shape, 1) % SEG < HALO

        def incoming(which, g):
            base = members + 2 + which * (half + 1) + g
            ref = (left_ref, right_ref)[which]
            parts = []
            for s in range(start, start + block, HALO):
                if s < HALO:
                    parts.append(up_ref[base])
                elif s >= rows + HALO:
                    parts.append(down_ref[base])
                else:
                    parts.append(ref[g, pl.ds(s - HALO, HALO), :])
            return jnp.concatenate(parts, axis=0)

        own = None
        for q in range(8):
            rolled = pltpu.roll(pick(q), q * SEG + HALO, axis=1)
            own = rolled if own is None else jnp.where(seg == q, rolled, own)
        source = at % half if number else half
        from_left = incoming(0, source)
        from_right = incoming(1, source)
        if at >= half if number else at:
            from_left = pltpu.roll(from_left, lanes - HALO, axis=1)
            from_right = pltpu.roll(from_right, HALO, axis=1)
        return jnp.where(first, from_left, own), jnp.where(first, own, from_right)

    for start in starts:
        rows_here = pl.ds(pad + start, block)
        for i in range(2):
            lo, hi = strips(start, lambda q: k_ref[i, rows_here, :], i, 0)
            sk_ref[2 * i, rows_here, :] = lo
            sk_ref[2 * i + 1, rows_here, :] = hi
        for g in range(groups):
            lo, hi = strips(start, lambda q: a_ref[8 * g + q, rows_here, :], g, groups)
            sa_ref[g, rows_here, :] = lo
            sa_ref[groups + g, rows_here, :] = hi

    lane = iota((block, lanes), 1)
    is_last = lane == lanes - 1
    is_first = lane == 0
    at_seven = lane % SEG == HALO - 1

    def sides(centre, edge):
        if edge is None:
            return pltpu.roll(centre, 1, axis=1), pltpu.roll(centre, lanes - 1, axis=1)
        return (
            pltpu.roll(jnp.where(is_last, edge, centre), 1, axis=1),
            pltpu.roll(jnp.where(is_first, edge, centre), lanes - 1, axis=1),
        )

    def weights(ref, at, kap, sea, edges, start):
        here = pl.ds(pad + start, block)

        def four(src, i, edge):
            centre = src[i, here, :]
            return centre, [
                src[i, pl.ds(pad + start - 1, block), :],
                src[i, pl.ds(pad + start + 1, block), :],
                *sides(centre, edge),
            ]

        src = k_ref if edges is not None else sk_ref
        kc, kn = four(src, kap, None if edges is None else edges[0])
        sc, sn = four(src, sea, None if edges is None else edges[1])
        w = [0.5 * (kc + kn[i]) * sc * sn[i] for i in range(4)]
        wsum = w[0] + w[1] + w[2] + w[3]
        inverse = 1.0 / (1.0 + 0.5 * wsum)
        values = [1.0 - 0.5 * wsum] + [0.5 * v for v in w]
        values += [inverse] + [0.5 * v * inverse for v in w]
        for i, value in enumerate(values):
            if at is None:
                ref[i, pl.ds(start, block), :] = value
            else:
                ref[at, i, pl.ds(start, block), :] = value

    for start in starts:
        here = pl.ds(pad + start, block)
        edges = [
            pltpu.roll(
                jnp.where(at_seven, sk_ref[2 * i, here, :], sk_ref[2 * i + 1, here, :]),
                lanes - HALO,
                axis=1,
            )
            for i in range(2)
        ]
        weights(w_ref, None, 0, 1, edges, start)
        weights(sw_ref, 0, 0, 2, None, start)
        weights(sw_ref, 1, 1, 3, None, start)

    def update(src, dst, rhs, m, start, coef, edge, explicit, store):
        centre = src[m, pl.ds(pad + start, block), :]
        upper = src[m, pl.ds(pad + start - 1, block), :]
        lower = src[m, pl.ds(pad + start + 1, block), :]
        west, east = sides(centre, edge)
        if explicit:
            c0, h0, h1, h2, h3, inverse = coef
            total = c0 * centre + (h0 * upper + h1 * lower) + (h2 * west + h3 * east)
            rhs[m, pl.ds(start, block), :] = total * inverse
        else:
            v0, v1, v2, v3 = coef
            total = rhs[m, pl.ds(start, block), :] + (v0 * upper + v1 * lower)
            total = total + (v2 * west + v3 * east)
        store(m, start, total)

    def sweep(src, dst, ssrc, sdst, explicit, last):
        chosen = range(6) if explicit else range(6, 10)

        def to(ref):
            def store(m, start, value):
                ref[m, pl.ds(pad + start, block), :] = value

            return store

        def to_out(m, start, value):
            out_ref[m, pl.ds(start - HALO, block), :] = value

        if not last:

            @pl.loop(0, 2 * groups)
            def _(g):
                side = g // groups
                for start in starts:
                    coef = [sw_ref[side, i, pl.ds(start, block), :] for i in chosen]
                    update(ssrc, sdst, srhs_ref, g, start, coef, None, explicit, to(sdst))

        @pl.loop(0, groups)
        def _(g):
            for start in range(HALO, HALO + rows, block) if last else starts:
                here = pl.ds(pad + start, block)
                coef = [w_ref[i, pl.ds(start, block), :] for i in chosen]
                edge = jnp.where(at_seven, ssrc[g, here, :], ssrc[groups + g, here, :])
                for q in range(8):
                    rolled = pltpu.roll(edge, (lanes - HALO - SEG * q) % lanes, axis=1)
                    update(
                        src, dst, rhs_ref, 8 * g + q, start, coef, rolled, explicit,
                        to_out if last else to(dst),
                    )

    now, later = (a_ref, sa_ref), (b_ref, sb_ref)
    for step in range(STEPS):
        for stage in range(SWEEPS + 1):
            last = step == STEPS - 1 and stage == SWEEPS
            sweep(now[0], later[0], now[1], later[1], stage == 0, last)
            now, later = later, now


def extract_kernel(owner_share, me_ref, record_ref, state_ref, out_ref, meta_ref):
    members, rows, lanes = state_ref.shape
    ncol, height, _ = record_ref.shape
    fields = FIELDS * BATCH_COUNT
    base = height - fields
    capacity = lanes // ncol
    me = me_ref[1]
    stacked = jnp.concatenate([record_ref[p, base:, :] for p in range(ncol)], axis=0)
    pieces = [
        stacked[i * lanes : (i + 1) * lanes, :].T for i in range(ncol * fields // lanes)
    ]
    lane = iota((lanes, lanes), 1)
    triangle = (lane < iota((lanes, lanes), 0)).astype(BF16)
    valid = iota((lanes, lanes), 0) < owner_share
    slot = (lane % capacity).astype(F32)

    def spread(f, k):
        index = (lane // capacity) * fields + f * BATCH_COUNT + k
        out = None
        for i, piece in enumerate(pieces):
            got = jnp.take_along_axis(piece, jnp.clip(index - i * lanes, 0, lanes - 1), axis=1)
            out = got if out is None else jnp.where(index >= i * lanes, got, out)
        return out

    meta_ref[...] = jnp.zeros(meta_ref.shape, F32)
    for k in range(BATCH_COUNT):
        mine = valid & (spread(0, k) == me.astype(F32))
        rank = jnp.dot(triangle, mine.astype(BF16), preferred_element_type=F32)
        hot = mine & (rank == slot)

        def slotted(values):
            return jnp.sum(jnp.where(hot, values, 0.0), axis=0, keepdims=True)

        cell = spread(1, k).astype(jnp.int32)
        x = cell // lanes
        error = jnp.where(hot, spread(3, k), 1.0)
        out_ref[k, pl.ds(members, 1), :] = slotted(1.0 / error)
        out_ref[k, pl.ds(members + 1, 1), :] = slotted(spread(2, k))
        place = slotted((x + 1).astype(F32)) - 1.0
        out_ref[k, pl.ds(members + 2, 1), :] = place
        out_ref[k, pl.ds(members + 3, 5), :] = jnp.zeros((5, lanes), F32)
        meta_ref[k, pl.ds(0, 1), :] = place
        meta_ref[k, pl.ds(1, 1), :] = slotted((cell - x * lanes).astype(F32))

    level = iota((8, lanes), 0)
    for k in range(BATCH_COUNT):
        xs = jnp.broadcast_to(meta_ref[k, pl.ds(0, 1), :], (8, lanes)).astype(jnp.int32)
        ys = jnp.broadcast_to(meta_ref[k, pl.ds(1, 1), :], (8, lanes)).astype(jnp.int32)

        @pl.loop(0, members // 8)
        def _(g):
            totals = []
            for q in range(8):
                total = jnp.zeros((8, lanes), F32)
                for s in range(0, rows, 8):
                    block = state_ref[8 * g + q, pl.ds(s, 8), :]
                    got = jnp.take_along_axis(block, ys, axis=1)
                    total = total + jnp.where(xs == level + s, got, 0.0)
                totals.append(jnp.sum(total, axis=0, keepdims=True))
            out_ref[k, pl.ds(pl.multiple_of(8 * g, 8), 8), :] = jnp.concatenate(totals, axis=0)


def band_sums(strides, me, ncol, parts):
    lanes = LANES
    capacity = lanes // ncol
    segment = iota((ncol, lanes), 1) // capacity
    far = offset_at(segment, strides)
    row = iota((8, lanes), 0)
    lefts, rights = [], []
    for p, (z, w, value) in enumerate(parts):
        members = z.shape[0]
        mean = jnp.mean(z, axis=0, keepdims=True)
        anomaly = z - mean
        innov = value - mean
        scaled = anomaly * w
        offset = sum(((p >> bit) & 1) * stride for bit, stride in enumerate(strides))
        owner = jnp.bitwise_xor(far, jnp.bitwise_xor(me, offset))
        mask = (owner == iota((ncol, lanes), 0)).astype(F32)
        lefts.append(
            jnp.concatenate([scaled[m : m + 1, :] * mask for m in range(members)], axis=0)
        )
        rights.append(
            jnp.concatenate([anomaly, jnp.where(row == 0, innov, 0.0)], axis=0)
        )
    return nt(jnp.concatenate(rights, axis=1), jnp.concatenate(lefts, axis=1))


def first_kernel(strides, me_ref, seen_ref, out_ref):
    ncol = seen_ref.shape[0]
    members = seen_ref.shape[2] - 8
    parts = [
        (
            seen_ref[p, 0, 0:members, :],
            seen_ref[p, 0, members : members + 1, :],
            seen_ref[p, 0, members + 1 : members + 2, :],
        )
        for p in range(ncol)
    ]
    out_ref[...] = band_sums(strides, me_ref[1], ncol, parts)


def spread_sums(row_strides, me, sums_ref, spread_ref, ncol):
    nrow, height, width = sums_ref.shape
    members = width // ncol
    devices = nrow * ncol
    lanes = LANES
    wide = max(devices, lanes)
    copies = max(1, lanes // devices)
    bands = [
        sums_ref.at[position_of(jnp.bitwise_xor(me, r), row_strides)] for r in range(nrow)
    ]
    for m in range(members):
        tile, start = divmod(m * ncol, lanes)
        chunks = []
        for c in range(wide // lanes):
            lane = iota((height, lanes), 1) + c * lanes
            owner = lane % devices
            index = start + owner % ncol
            out = None
            for r in range(nrow):
                if (c * lanes) // ncol > r and devices >= lanes:
                    continue
                piece = bands[r][:, pl.ds(tile * lanes, lanes)]
                got = jnp.take_along_axis(piece, index, axis=1)
                out = got if out is None else jnp.where(owner // ncol == r, got, out)
            chunks.append(out)
        if copies > 1:
            hi, mid, lo = split3(chunks[0])
            which = iota((height, lanes), 1) // devices
            value = jnp.where(which == 0, hi, jnp.where(which == 1, mid, jnp.where(which == 2, lo, 0.0)))
            spread_ref[pl.ds(m * height, height), :] = value.astype(BF16)
        else:
            pieces = [split3(v) for v in chunks]
            value = jnp.concatenate([part[i] for i in range(3) for part in pieces], axis=1)
            spread_ref[pl.ds(m * height, height), :] = value.astype(BF16)


def copies_of(levels):
    devices = levels.shape[0]
    copies = max(3, LANES // devices)
    return jnp.concatenate([(levels * 0.125).astype(BF16)] * copies, axis=0)


def solve_sums(sums_ref, ncol):
    nrow, height, width = sums_ref.shape
    members = width // ncol
    lanes = LANES
    total = sums_ref[0]
    for r in range(1, nrow):
        total = total + sums_ref[r]
    pick = (iota((width, lanes), 0) // ncol == iota((width, lanes), 1)).astype(F32)
    a = jnp.dot(total, pick, precision=HIGH, preferred_element_type=F32)
    row = iota((height, lanes), 0)
    lane = iota((height, lanes), 1)
    a = a + jnp.where((row == lane) & (row < members), members - 1.0, 0.0)
    lane1 = iota((1, lanes), 1)
    for k in range(members):
        column = a[:, k : k + 1]
        pivot = a[k : k + 1, :]
        inverse = 1.0 / a[k : k + 1, k : k + 1]
        scaled = jnp.where(lane1 == k, inverse, pivot * inverse)
        kept = jnp.where(lane == k, 0.0, a)
        a = jnp.where(row == k, scaled, kept - column * scaled)
    gain = a[members : members + 1, :] * (1.0 / (members - 1))
    out = jnp.where(lane1 < members, -0.5 * a[0:members, :] + gain, 0.0)
    return jnp.where(lane1 == members, 1.0 / (members - 1), out)


def apply_sums(spread, levels, z, height):
    at = jnp.dot(spread, levels, preferred_element_type=F32)
    total = None
    for m in range(z.shape[0]):
        term = at[m * height : (m + 1) * height, :] * z[m : m + 1, :]
        total = term if total is None else total + term
    return total


def levels_at(record_ref, p, batch, devices, place):
    lanes = LANES
    hot = (iota((lanes, lanes), 0) == place.astype(jnp.int32)).astype(BF16)
    table = record_ref[p, batch * devices : (batch + 1) * devices, :].astype(BF16)
    return jnp.dot(table, hot, preferred_element_type=F32)


def moved(record_ref, seen_ref, spread, solved, batch, target, devices, read):
    ncol = seen_ref.shape[0]
    members = seen_ref.shape[2] - 8
    height = members + 8
    out = []
    for p in range(0, ncol, 2):
        pair = (p, p + 1)
        levels = jnp.concatenate(
            [
                copies_of(
                    levels_at(
                        record_ref, i, batch, devices,
                        seen_ref[i, target, members + 2 : members + 3, :],
                    )
                )
                for i in pair
            ],
            axis=1,
        )
        z = jnp.concatenate([read(i) for i in pair], axis=1)
        sums = apply_sums(spread, levels, z, height)
        z = z + jnp.dot(
            solved[:, 0:height], sums, precision=HIGH, preferred_element_type=F32
        )
        out += [z[:, 0:LANES], z[:, LANES:]]
    return out


def next_kernel(
    strides, row_strides, batch, me_ref, sums_ref, record_ref, seen_ref, z_ref,
    out_ref, spread_ref, solved_ref,
):
    ncol = seen_ref.shape[0]
    members = seen_ref.shape[2] - 8
    devices = ncol * sums_ref.shape[0]
    spread_sums(row_strides, me_ref[0], sums_ref, spread_ref, ncol)
    solved = solve_sums(sums_ref, ncol)
    solved_ref[...] = solved
    target = batch + 1
    zs = moved(
        record_ref, seen_ref, spread_ref[...], solved, batch, target, devices,
        lambda i: z_ref[i, 0, 0:members, :],
    )
    parts = [
        (
            zs[p],
            seen_ref[p, target, members : members + 1, :],
            seen_ref[p, target, members + 1 : members + 2, :],
        )
        for p in range(ncol)
    ]
    out_ref[...] = band_sums(strides, me_ref[1], ncol, parts)


def compose(spread, solved, levels, batch, trans_ref, dst_ref, height):
    members = solved.shape[0]
    at = jnp.dot(spread, levels, preferred_element_type=F32)
    lanes = LANES
    gain = solved[:, 0:height]
    for j in range(0, members, 2):
        sums = []
        for i in (j, j + 1):
            if batch == 0:
                sums.append(at[i * height : (i + 1) * height, :])
            else:
                total = None
                for m in range(members):
                    term = at[m * height : (m + 1) * height, :] * trans_ref[i, m : m + 1, :]
                    total = term if total is None else total + term
                sums.append(total)
        change = jnp.dot(
            gain, jnp.concatenate(sums, axis=1), precision=HIGH, preferred_element_type=F32
        )
        for n, i in enumerate((j, j + 1)):
            part = change[:, n * lanes : (n + 1) * lanes]
            if batch == 0:
                dst_ref[i] = part + (iota((members, lanes), 0) == i).astype(F32)
            else:
                dst_ref[i] = part + trans_ref[i]


def later_kernel(batch, *refs):
    if batch == 0:
        spread_ref, solved_ref, record_ref, seen_ref, z_ref = refs[:5]
        trans_ref, rest = None, refs[5:]
    else:
        spread_ref, solved_ref, record_ref, seen_ref, z_ref, trans_ref = refs[:6]
        rest = refs[6:]
    ncol = seen_ref.shape[0]
    members = seen_ref.shape[2] - 8
    devices = (record_ref.shape[1] - FIELDS * BATCH_COUNT) // BATCH_COUNT
    spread = spread_ref[...]
    solved = solved_ref[...]
    levels = copies_of(record_ref[0, batch * devices : (batch + 1) * devices, :])
    compose(spread, solved, levels, batch, trans_ref, rest[0], members + 8)
    for target in range(batch + 2, BATCH_COUNT):
        at = target - batch - 1
        zs = moved(
            record_ref, seen_ref, spread, solved, batch, target, devices,
            lambda i: z_ref[i, at, 0:members, :],
        )
        for p in range(ncol):
            rest[1][p, at - 1] = zs[p]


def final_kernel(
    row_strides, me_ref, sums_ref, record_ref, trans_ref, state_ref, out_ref,
    spread_ref, whole_ref, turned_ref,
):
    members, rows, lanes = state_ref.shape
    nrow, height, width = sums_ref.shape
    ncol = width // members
    devices = nrow * ncol
    batch = BATCH_COUNT - 1
    spread_sums(row_strides, me_ref[0], sums_ref, spread_ref, ncol)
    solved = solve_sums(sums_ref, ncol)
    levels = copies_of(record_ref[0, batch * devices : (batch + 1) * devices, :])
    compose(spread_ref[...], solved, levels, batch, trans_ref, whole_ref, height)
    for i in range(members):
        piece = whole_ref[:, i, :]
        hi, lo, _ = split3(piece)
        stack = jnp.concatenate([hi, hi, lo, jnp.zeros_like(hi)], axis=0)
        turned_ref[:, i, :] = stack.T

    @pl.loop(0, rows, unroll=4)
    def _(x):
        z = state_ref[:, x, :]
        hi, lo, _ = split3(z)
        right = jnp.concatenate([hi, lo, hi, jnp.zeros_like(hi)], axis=0).astype(BF16)
        out_ref[:, x, :] = jnp.dot(
            turned_ref[x].astype(BF16), right, preferred_element_type=F32
        )


def call(kernel, out_shape, in_specs, scratch=(), flops=10**6):
    return pl.pallas_call(
        kernel,
        out_shape=out_shape,
        in_specs=in_specs,
        out_specs=jax.tree.map(lambda _: VMEM, out_shape),
        scratch_shapes=list(scratch),
        compiler_params=PARAMS,
    )


def body(
    sample_heights, depth, land_sea, batch_order, obs_value, obs_error, obs_tile, obs_cell, loc_level
):
    members, rows, cols = sample_heights.shape
    ncol = lax.axis_size("col")
    nrow = lax.axis_size("row")
    devices = nrow * ncol
    strides, row_strides = strides_of(ncol), strides_of(nrow)
    groups = members // 8
    half = groups // 2
    height = members + 8
    me = jnp.stack([lax.axis_index("row"), lax.axis_index("col")]).astype(jnp.int32)

    def out(*shape, dtype=F32):
        return jax.ShapeDtypeStruct(shape, dtype)

    record_rows = BATCH_COUNT * devices + FIELDS * BATCH_COUNT
    to_right, to_left, record, coef = call(
        prep_kernel,
        (out(half + 1, rows, cols), out(half + 1, rows, cols), out(record_rows, cols), out(2, rows, cols)),
        [SMEM] + [VMEM] * 8,
    )(
        batch_order, sample_heights, depth, land_sea, loc_level[:, :, 0, :],
        obs_value, obs_error, obs_tile[:, :, 0], obs_cell,
    )
    left, right = shift_pair(to_left, to_right, "col")

    def slab(start):
        cut = lambda a: lax.slice_in_dim(a, start, start + HALO, axis=1)
        return jnp.concatenate([cut(a) for a in (sample_heights, coef, left, right)], axis=0)

    up, down = shift_pair(slab(0), slab(rows - HALO), "row")
    records = gather_over(record, "col")

    ext = rows + 2 * HALO
    tall = ext + 2 * HALO
    state = call(
        forecast_kernel,
        out(members, rows, cols),
        [VMEM] * 6,
        [
            pltpu.VMEM((members, tall, cols), F32),
            pltpu.VMEM((members, tall, cols), F32),
            pltpu.VMEM((members, ext, cols), F32),
            pltpu.VMEM((2 * groups, tall, cols), F32),
            pltpu.VMEM((2 * groups, tall, cols), F32),
            pltpu.VMEM((2 * groups, ext, cols), F32),
            pltpu.VMEM((2, tall, cols), F32),
            pltpu.VMEM((4, tall, cols), F32),
            pltpu.VMEM((10, ext, cols), F32),
            pltpu.VMEM((2, 10, ext, cols), F32),
        ],
    )(sample_heights, coef, left, right, up, down)

    mine = call(
        functools.partial(extract_kernel, obs_cell.shape[1]),
        out(BATCH_COUNT, height, cols),
        [SMEM, VMEM, VMEM],
        [pltpu.VMEM((BATCH_COUNT, 8, cols), F32)],
    )(me, records, state)
    seen = gather_over(mine, "col")

    sums = call(
        functools.partial(first_kernel, strides), out(height, members * ncol), [SMEM, VMEM]
    )(me, seen)
    wide = max(LANES, 3 * devices)
    z = seen[:, 1:]
    trans = None
    for batch in range(BATCH_COUNT - 1):
        every = gather_over(sums, "row")
        sums, spread, solved = call(
            functools.partial(next_kernel, strides, row_strides, batch),
            (
                out(height, members * ncol),
                out(members * height, wide, dtype=BF16),
                out(members, LANES),
            ),
            [SMEM] + [VMEM] * 4,
        )(me, every, records, seen, z)
        left_over = BATCH_COUNT - 2 - batch
        outs = (out(members, members, cols),)
        if left_over:
            outs += (out(ncol, left_over, members, cols),)
        given = (spread, solved, records, seen, z) + (() if trans is None else (trans,))
        got = call(
            functools.partial(later_kernel, batch), outs, [VMEM] * len(given)
        )(*given)
        trans = got[0]
        if left_over:
            z = got[1]
    every = gather_over(sums, "row")
    return call(
        functools.partial(final_kernel, row_strides),
        out(members, rows, cols),
        [SMEM] + [VMEM] * 4,
        [
            pltpu.VMEM((members * height, wide), BF16),
            pltpu.VMEM((members, members, cols), F32),
            pltpu.VMEM((rows, members, cols), F32),
        ],
    )(me, every, records, trans, state)


def solution(mesh):
    return jax.shard_map(
        body,
        mesh=mesh,
        in_specs=(
            P(None, "row", "col"),
            P("row", "col"),
            P("row", "col"),
            P(),
            P(None, ("row", "col")),
            P(None, ("row", "col")),
            P(None, ("row", "col"), None),
            P(None, ("row", "col")),
            P(None, "row", "col", None),
        ),
        out_specs=P(None, "row", "col"),
        check_vma=False,
    )
```

```python
import functools

import jax
import jax.numpy as jnp
from jax import lax
from jax.experimental import pallas as pl
from jax.experimental.pallas import tpu as pltpu
from jax.sharding import PartitionSpec as P

BATCH_COUNT = 4
STEPS = 2
SWEEPS = 2
HALO = 8
SEG = 2 * HALO
LANES = 128
FIELDS = 4
HIGH = lax.Precision.HIGHEST
F32 = jnp.float32
BF16 = jnp.bfloat16
SMEM = pl.BlockSpec(memory_space=pltpu.SMEM)
VMEM = pl.BlockSpec(memory_space=pltpu.VMEM)
PARAMS = pltpu.CompilerParams(vmem_limit_bytes=48 * 1024 * 1024)


def iota(shape, dim):
    return lax.broadcasted_iota(jnp.int32, shape, dim)


def strides_of(n):
    out = []
    while n > 1:
        n //= 2
        out.append(n)
    return out


def offset_at(position, strides):
    out = position * 0
    for bit, stride in enumerate(strides):
        out = out + ((position >> bit) & 1) * stride
    return out


def position_of(offset, strides):
    out = offset * 0
    for bit, stride in enumerate(strides):
        out = out + ((offset // stride) & 1) * (1 << bit)
    return out


def gather_over(block, axis, beside=None):
    n = lax.axis_size(axis)
    held = block[None]
    strides = strides_of(n)
    for stride in strides:
        if stride == strides[-1] and beside is not None:
            held, beside = lax.optimization_barrier((held, beside))
        other = lax.ppermute(held, axis, [(i, i ^ stride) for i in range(n)])
        if stride != strides[-1]:
            held = jnp.concatenate([held, other], axis=0)
    return (held, other) if beside is None else ((held, other), beside)


def shift_pair(low_send, high_send, axis):
    n = lax.axis_size(axis)
    forward = [(i, i + 1) for i in range(n - 1)]
    backward = [(b, a) for a, b in forward]
    return lax.ppermute(high_send, axis, forward), lax.ppermute(low_send, axis, backward)


def nt(a, b, precision=HIGH):
    return lax.dot_general(
        a, b, (((1,), (1,)), ((), ())), precision=precision, preferred_element_type=F32
    )


def split3(x):
    hi = x.astype(BF16).astype(F32)
    rest = x - hi
    mid = rest.astype(BF16).astype(F32)
    return hi, mid, rest - mid


def prep_kernel(h_ref, coef_ref, loc_ref, obs_ref, to_right_ref, to_left_ref, record_ref):
    members, rows, lanes = h_ref.shape
    groups = members // 8
    half = groups // 2
    seg = iota((rows, lanes), 1) // SEG
    first = iota((rows, lanes), 1) % SEG < HALO
    kappa, sea = coef_ref[0], coef_ref[1]

    devices = loc_ref.shape[2]
    base = BATCH_COUNT * devices
    fields = FIELDS * BATCH_COUNT
    width = obs_ref.shape[1]
    record_ref[base:, :] = jnp.zeros((fields, lanes), F32)

    def chosen(k, values):
        order = obs_ref[fields : fields + 1, k : k + 1]
        out = values[0]
        for b in range(1, BATCH_COUNT):
            out = jnp.where(order == b, values[b], out)
        return out

    for k in range(BATCH_COUNT):
        level = chosen(k, [loc_ref[b].astype(F32) for b in range(BATCH_COUNT)])
        record_ref[k * devices : (k + 1) * devices, :] = level.T
        for f in range(FIELDS):
            row = f * BATCH_COUNT
            record_ref[base + row + k : base + row + k + 1, 0:width] = chosen(
                k, [obs_ref[row + b : row + b + 1, :] for b in range(BATCH_COUNT)]
            )

    def pack(pick):
        out = None
        for q in range(8):
            rolled = pltpu.roll(pick(q), q * SEG + HALO, axis=1)
            out = rolled if out is None else jnp.where(seg == q, rolled, out)
        return out

    def send(g, a, b):
        to_right_ref[g] = jnp.where(first, a, pltpu.roll(b, HALO, axis=1))
        to_left_ref[g] = jnp.where(first, pltpu.roll(b, lanes - HALO, axis=1), a)

    send(half, pack(lambda q: kappa), pack(lambda q: sea))
    for g in range(half):
        send(g, pack(lambda q: h_ref[8 * g + q]), pack(lambda q: h_ref[8 * (g + half) + q]))


def forecast_kernel(
    h_ref, coef_ref, left_ref, right_ref, up_ref, down_ref, out_ref,
    a_ref, b_ref, rhs_ref, sa_ref, sb_ref, srhs_ref, k_ref, sk_ref, w_ref, sw_ref, edge_ref,
):
    members, rows, lanes = h_ref.shape
    groups = members // 8
    half = groups // 2
    ext = rows + 2 * HALO
    pad = HALO
    inner = pad + HALO
    block = 16
    starts = list(range(0, ext, block))

    def fill(ref, index, upper, centre, lower):
        ref[index, pl.ds(pad, HALO), :] = upper
        ref[index, pl.ds(inner, rows), :] = centre
        ref[index, pl.ds(inner + rows, HALO), :] = lower

    for ref in (k_ref, sk_ref):
        for i in range(ref.shape[0]):
            ref[i, pl.ds(0, pad), :] = jnp.zeros((pad, lanes), F32)
            ref[i, pl.ds(pad + ext, pad), :] = jnp.zeros((pad, lanes), F32)
    for i in range(2):
        fill(k_ref, i, up_ref[members + i], coef_ref[i], down_ref[members + i])

    @pl.loop(0, members)
    def _(m):
        fill(a_ref, m, up_ref[m], h_ref[m], down_ref[m])

    def strips(start, pick, at, number):
        shape = (block, lanes)
        seg = iota(shape, 1) // SEG
        first = iota(shape, 1) % SEG < HALO

        def incoming(which, g):
            base = members + 2 + which * (half + 1) + g
            ref = (left_ref, right_ref)[which]
            parts = []
            for s in range(start, start + block, HALO):
                if s < HALO:
                    parts.append(up_ref[base])
                elif s >= rows + HALO:
                    parts.append(down_ref[base])
                else:
                    parts.append(ref[g, pl.ds(s - HALO, HALO), :])
            return jnp.concatenate(parts, axis=0)

        own = None
        for q in range(8):
            rolled = pltpu.roll(pick(q), q * SEG + HALO, axis=1)
            own = rolled if own is None else jnp.where(seg == q, rolled, own)
        source = at % half if number else half
        from_left = incoming(0, source)
        from_right = incoming(1, source)
        if at >= half if number else at:
            from_left = pltpu.roll(from_left, lanes - HALO, axis=1)
            from_right = pltpu.roll(from_right, HALO, axis=1)
        return jnp.where(first, from_left, own), jnp.where(first, own, from_right)

    for start in starts:
        rows_here = pl.ds(pad + start, block)
        for i in range(2):
            lo, hi = strips(start, lambda q: k_ref[i, rows_here, :], i, 0)
            sk_ref[2 * i, rows_here, :] = lo
            sk_ref[2 * i + 1, rows_here, :] = hi
        for g in range(groups):
            lo, hi = strips(start, lambda q: a_ref[8 * g + q, rows_here, :], g, groups)
            sa_ref[g, rows_here, :] = lo
            sa_ref[groups + g, rows_here, :] = hi

    lane = iota((block, lanes), 1)
    is_last = lane == lanes - 1
    is_first = lane == 0
    at_seven = lane % SEG == HALO - 1

    def sides(centre, edge):
        if edge is None:
            return pltpu.roll(centre, 1, axis=1), pltpu.roll(centre, lanes - 1, axis=1)
        return (
            jnp.where(is_first, edge, pltpu.roll(centre, 1, axis=1)),
            jnp.where(is_last, edge, pltpu.roll(centre, lanes - 1, axis=1)),
        )

    def edges_of(low, high):
        return jnp.where(
            at_seven, pltpu.roll(high, lanes - 1, axis=1), pltpu.roll(low, 1, axis=1)
        )

    def weights(ref, at, kap, sea, edges, start):
        here = pl.ds(pad + start, block)

        def four(src, i, edge):
            centre = src[i, here, :]
            return centre, [
                src[i, pl.ds(pad + start - 1, block), :],
                src[i, pl.ds(pad + start + 1, block), :],
                *sides(centre, edge),
            ]

        src = k_ref if edges is not None else sk_ref
        kc, kn = four(src, kap, None if edges is None else edges[0])
        sc, sn = four(src, sea, None if edges is None else edges[1])
        w = [0.5 * (kc + kn[i]) * sc * sn[i] for i in range(4)]
        wsum = w[0] + w[1] + w[2] + w[3]
        inverse = 1.0 / (1.0 + 0.5 * wsum)
        values = [1.0 - 0.5 * wsum] + [0.5 * v for v in w]
        values += [inverse] + [0.5 * v * inverse for v in w]
        for i, value in enumerate(values):
            if at is None:
                ref[i, pl.ds(start, block), :] = value
            else:
                ref[at, i, pl.ds(start, block), :] = value

    for start in starts:
        here = pl.ds(pad + start, block)
        edges = [
            pltpu.roll(
                edges_of(sk_ref[2 * i, here, :], sk_ref[2 * i + 1, here, :]), lanes - HALO, axis=1
            )
            for i in range(2)
        ]
        weights(w_ref, None, 0, 1, edges, start)
        weights(sw_ref, 0, 0, 2, None, start)
        weights(sw_ref, 1, 1, 3, None, start)

    def update(src, dst, rhs, m, start, coef, edge, explicit, store):
        centre = src[m, pl.ds(pad + start, block), :]
        upper = src[m, pl.ds(pad + start - 1, block), :]
        lower = src[m, pl.ds(pad + start + 1, block), :]
        west, east = sides(centre, edge)
        if explicit:
            c0, h0, h1, h2, h3, inverse = coef
            total = c0 * centre + (h0 * upper + h1 * lower) + (h2 * west + h3 * east)
            rhs[m, pl.ds(start, block), :] = total * inverse
        else:
            v0, v1, v2, v3 = coef
            total = rhs[m, pl.ds(start, block), :] + (v0 * upper + v1 * lower)
            total = total + (v2 * west + v3 * east)
        store(m, start, total)

    def sweep(src, dst, ssrc, sdst, explicit, last):
        chosen = range(6) if explicit else range(6, 10)

        def to(ref):
            def store(m, start, value):
                ref[m, pl.ds(pad + start, block), :] = value

            return store

        def to_out(m, start, value):
            out_ref[m, pl.ds(start - HALO, block), :] = value

        @pl.loop(0, groups)
        def _(g):
            for start in starts:
                here = pl.ds(pad + start, block)
                edge_ref[g, pl.ds(start, block), :] = edges_of(
                    ssrc[g, here, :], ssrc[groups + g, here, :]
                )
                for side in (0, 1) if not last else ():
                    coef = [sw_ref[side, i, pl.ds(start, block), :] for i in chosen]
                    update(
                        ssrc, sdst, srhs_ref, side * groups + g, start, coef, None, explicit,
                        to(sdst),
                    )

        @pl.loop(0, groups)
        def _(g):
            for start in range(HALO, HALO + rows, block) if last else starts:
                coef = [w_ref[i, pl.ds(start, block), :] for i in chosen]
                edge = edge_ref[g, pl.ds(start, block), :]
                for q in range(8):
                    rolled = pltpu.roll(edge, (lanes - HALO - SEG * q) % lanes, axis=1)
                    update(
                        src, dst, rhs_ref, 8 * g + q, start, coef, rolled, explicit,
                        to_out if last else to(dst),
                    )

    now, later = (a_ref, sa_ref), (b_ref, sb_ref)
    for step in range(STEPS):
        for stage in range(SWEEPS + 1):
            last = step == STEPS - 1 and stage == SWEEPS
            sweep(now[0], later[0], now[1], later[1], stage == 0, last)
            now, later = later, now


def extract_kernel(owner_share, me_ref, record_ref, state_ref, out_ref, meta_ref):
    members, rows, lanes = state_ref.shape
    ncol, height, _ = record_ref.shape
    fields = FIELDS * BATCH_COUNT
    base = height - fields
    capacity = lanes // ncol
    me = me_ref[1]
    stacked = jnp.concatenate([record_ref[p, base:, :] for p in range(ncol)], axis=0)
    pieces = [
        stacked[i * lanes : (i + 1) * lanes, :].T for i in range(ncol * fields // lanes)
    ]
    lane = iota((lanes, lanes), 1)
    triangle = (lane < iota((lanes, lanes), 0)).astype(BF16)
    valid = iota((lanes, lanes), 0) < owner_share
    slot = (lane % capacity).astype(F32)

    def spread(f, k):
        index = (lane // capacity) * fields + f * BATCH_COUNT + k
        out = None
        for i, piece in enumerate(pieces):
            got = jnp.take_along_axis(piece, jnp.clip(index - i * lanes, 0, lanes - 1), axis=1)
            out = got if out is None else jnp.where(index >= i * lanes, got, out)
        return out

    base = BATCH_COUNT * members
    out_ref[base + 3 * BATCH_COUNT :, :] = jnp.zeros((BATCH_COUNT, lanes), F32)
    for k in range(BATCH_COUNT):
        mine = valid & (spread(0, k) == me.astype(F32))
        rank = jnp.dot(triangle, mine.astype(BF16), preferred_element_type=F32)
        hot = mine & (rank == slot)

        def slotted(values):
            return jnp.sum(jnp.where(hot, values, 0.0), axis=0, keepdims=True)

        cell = spread(1, k).astype(jnp.int32)
        x = cell // lanes
        error = jnp.where(hot, spread(3, k), 1.0)
        for n, values in enumerate((1.0 / error, spread(2, k), (x + 1).astype(F32))):
            row = base + n * BATCH_COUNT + k
            out_ref[row : row + 1, :] = slotted(values) - (1.0 if n == 2 else 0.0)
        meta_ref[k : k + 1, :] = slotted((cell - x * lanes).astype(F32))

    level = iota((8, lanes), 0)
    place = base + 2 * BATCH_COUNT
    for k in range(BATCH_COUNT):
        xs = jnp.broadcast_to(out_ref[place + k : place + k + 1, :], (8, lanes)).astype(jnp.int32)
        ys = jnp.broadcast_to(meta_ref[k : k + 1, :], (8, lanes)).astype(jnp.int32)

        @pl.loop(0, members // 8)
        def _(g):
            totals = []
            for q in range(8):
                total = jnp.zeros((8, lanes), F32)
                for s in range(0, rows, 8):
                    block = state_ref[8 * g + q, pl.ds(s, 8), :]
                    got = jnp.take_along_axis(block, ys, axis=1)
                    total = total + jnp.where(xs == level + s, got, 0.0)
                totals.append(jnp.sum(total, axis=0, keepdims=True))
            row = pl.multiple_of(k * members + 8 * g, 8)
            out_ref[pl.ds(row, 8), :] = jnp.concatenate(totals, axis=0)


def band_sums(ncol, parts):
    lanes = LANES
    mask = (iota((ncol, lanes), 1) // (lanes // ncol) == iota((ncol, lanes), 0)).astype(F32)
    row = iota((8, lanes), 0)
    lefts, rights = [], []
    for z, w, value in parts:
        members = z.shape[0]
        mean = jnp.mean(z, axis=0, keepdims=True)
        anomaly = z - mean
        innov = value - mean
        scaled = anomaly * w

        def masked(values):
            return jnp.concatenate(
                [values[m : m + 1, :] * mask for m in range(members)], axis=0
            ).astype(BF16)

        hi, lo, _ = split3(scaled)
        hi, lo = masked(hi), masked(lo)
        lefts += [hi, lo, hi]
        right = jnp.concatenate([anomaly, jnp.where(row == 0, innov, 0.0)], axis=0)
        hi, lo, _ = split3(right)
        hi, lo = hi.astype(BF16), lo.astype(BF16)
        rights += [hi, hi, lo]
    return nt(jnp.concatenate(rights, axis=1), jnp.concatenate(lefts, axis=1), None)


def seen_rows(seen_refs, p):
    half = seen_refs[0].shape[0]
    return seen_refs[p // half].at[p % half]


def first_kernel(members, low_ref, high_ref, out_ref):
    seen = (low_ref, high_ref)
    ncol = 2 * low_ref.shape[0]
    parts = []
    for p in range(ncol):
        rows = seen_rows(seen, p)
        meta = BATCH_COUNT * members
        parts.append(
            (
                rows[0:members, :],
                rows[meta : meta + 1, :],
                rows[meta + BATCH_COUNT : meta + BATCH_COUNT + 1, :],
            )
        )
    out_ref[...] = band_sums(ncol, parts)


def bands_of(row_strides, me, low_ref, high_ref):
    half = low_ref.shape[0]
    out = []
    for r in range(2 * half):
        at = position_of(jnp.bitwise_xor(me, r), row_strides)
        out.append(
            jnp.where(at < half, low_ref[at % half], high_ref[at % half])
        )
    return out


def spread_sums(bands, spread_ref, ncol):
    height, width = bands[0].shape
    nrow = len(bands)
    members = width // ncol
    devices = nrow * ncol
    lanes = LANES
    lane = iota((height, lanes), 1)
    owner = lane % devices
    which = lane // devices
    per = max(1, lanes // devices)
    for first in range(0, members, per):
        tile, start = divmod(first * ncol, lanes)
        index = start + which * ncol + owner % ncol
        group = None
        for r in range(nrow):
            piece = bands[r][:, tile * lanes : (tile + 1) * lanes]
            got = jnp.take_along_axis(piece, index, axis=1)
            group = got if group is None else jnp.where(owner // ncol == r, got, group)
        for n in range(per):
            m = first + n
            if per > 1:
                value = jnp.take_along_axis(group, n * devices + owner, axis=1)
                hi, mid, lo = split3(value)
                value = jnp.where(which == 0, hi, jnp.where(which == 1, mid, lo))
            else:
                value = jnp.concatenate(split3(group), axis=1)
            spread_ref[pl.ds(m * height, height), :] = value.astype(BF16)


def copies_of(levels):
    devices = levels.shape[0]
    copies = max(3, LANES // devices)
    scaled = (levels * 0.125).astype(BF16)
    return jnp.concatenate([scaled] * 3 + [jnp.zeros_like(scaled)] * (copies - 3), axis=0)


def solve_sums(bands, ncol):
    height, width = bands[0].shape
    members = width // ncol
    lanes = LANES
    total = bands[0]
    for band in bands[1:]:
        total = total + band
    pick = (iota((width, lanes), 0) // ncol == iota((width, lanes), 1)).astype(BF16)
    a = sum(
        jnp.dot(part.astype(BF16), pick, preferred_element_type=F32)
        for part in reversed(split3(total))
    )
    row = iota((height, lanes), 0)
    lane = iota((height, lanes), 1)
    a = a + jnp.where((row == lane) & (row < members), members - 1.0, 0.0)
    lane1 = iota((1, lanes), 1)
    block = 8
    for start in range(0, members, block):
        columns = [
            jnp.broadcast_to(a[:, k : k + 1], (height, lanes))
            for k in range(start, start + block)
        ]
        for s in range(block):
            k, column = start + s, columns[s]
            inverse = 1.0 / column[k : k + 1, :]
            scaled = jnp.where(lane1 == k, inverse, a[k : k + 1, :] * inverse)
            a = jnp.where(row == k, scaled, jnp.where(lane == k, 0.0, a) - column * scaled)
            for t in range(s + 1, block):
                part = columns[t][k : k + 1, :] * inverse
                columns[t] = jnp.where(row == k, part, columns[t] - column * part)
    gain = a[members : members + 1, :] * (1.0 / (members - 1))
    out = jnp.where(lane1 < members, -0.5 * a[0:members, :] + gain, 0.0)
    return jnp.where(lane1 == members, 1.0 / (members - 1), out)


def apply_sums(spread, levels, z, height):
    at = jnp.dot(spread, levels, preferred_element_type=F32)
    total = None
    for m in range(z.shape[0]):
        term = at[m * height : (m + 1) * height, :] * z[m : m + 1, :]
        total = term if total is None else total + term
    return total


def levels_at(rows, batch, devices, place):
    lanes = LANES
    hot = (iota((lanes, lanes), 0) == place.astype(jnp.int32)).astype(BF16)
    table = rows[batch * devices : (batch + 1) * devices, :].astype(BF16)
    return jnp.dot(table, hot, preferred_element_type=F32)


def moved(strides, me, record_ref, seen, spread, solved, batch, target, devices, read):
    ncol = 2 * seen[0].shape[0]
    members = solved.shape[0]
    height = members + 8
    place = BATCH_COUNT * members + 2 * BATCH_COUNT + target
    out = []
    for p in range(0, ncol, 2):
        pair = (p, p + 1)
        levels = []
        for i in pair:
            offset = sum(((i >> bit) & 1) * stride for bit, stride in enumerate(strides))
            levels.append(
                copies_of(
                    levels_at(
                        record_ref.at[jnp.bitwise_xor(me, offset)], batch, devices,
                        seen_rows(seen, i)[place : place + 1, :],
                    )
                )
            )
        z = jnp.concatenate([read(i) for i in pair], axis=1)
        sums = apply_sums(spread, jnp.concatenate(levels, axis=1), z, height)
        z = z + jnp.dot(
            solved[:, 0:height], sums, precision=HIGH, preferred_element_type=F32
        )
        out += [z[:, 0:LANES], z[:, LANES:]]
    return out


def reader(seen, z_ref, members, target):
    if z_ref is not None:
        return lambda i: z_ref[i]
    return lambda i: seen_rows(seen, i)[target * members : (target + 1) * members, :]


def next_kernel(strides, row_strides, batch, *refs):
    me_ref, lows_ref, highs_ref, record_ref = refs[:4]
    seen = refs[4:6]
    z_ref = refs[6] if batch else None
    out_ref, spread_ref, solved_ref = refs[-3:]
    ncol = 2 * seen[0].shape[0]
    members = solved_ref.shape[0]
    devices = 2 * ncol * lows_ref.shape[0]
    bands = bands_of(row_strides, me_ref[0], lows_ref, highs_ref)
    spread_sums(bands, spread_ref, ncol)
    solved = solve_sums(bands, ncol)
    solved_ref[...] = solved
    target = batch + 1
    zs = moved(
        strides, me_ref[1], record_ref, seen, spread_ref[...], solved, batch, target, devices,
        reader(seen, z_ref, members, target),
    )
    parts = []
    meta = BATCH_COUNT * members + target
    for p in range(ncol):
        rows = seen_rows(seen, p)
        parts.append(
            (
                zs[p],
                rows[meta : meta + 1, :],
                rows[meta + BATCH_COUNT : meta + BATCH_COUNT + 1, :],
            )
        )
    out_ref[...] = band_sums(ncol, parts)


def moved_kernel(strides, batches, target, *refs):
    me_ref, record_ref = refs[:2]
    seen = refs[2:4]
    given = refs[4 : 4 + 2 * len(batches)]
    z_ref = refs[4 + 2 * len(batches)] if len(refs) == 6 + 2 * len(batches) else None
    out_ref = refs[-1]
    members = given[1].shape[0]
    devices = (record_ref.shape[1] - FIELDS * BATCH_COUNT) // BATCH_COUNT
    read = reader(seen, z_ref, members, target)
    for n, batch in enumerate(batches):
        zs = moved(
            strides, me_ref[1], record_ref, seen, given[2 * n][...], given[2 * n + 1][...],
            batch, target, devices, read,
        )
        read = zs.__getitem__
    for p, z in enumerate(zs):
        out_ref[p] = z


def compose(spread, solved, levels, batch, trans_ref, dst_ref, height):
    members = solved.shape[0]
    at = jnp.dot(spread, levels, preferred_element_type=F32)
    lanes = LANES
    gain = solved[:, 0:height]
    for j in range(0, members, 2):
        sums = []
        for i in (j, j + 1):
            if batch == 0:
                sums.append(at[i * height : (i + 1) * height, :])
            else:
                total = None
                for m in range(members):
                    term = at[m * height : (m + 1) * height, :] * trans_ref[i, m : m + 1, :]
                    total = term if total is None else total + term
                sums.append(total)
        change = jnp.dot(
            gain, jnp.concatenate(sums, axis=1), precision=HIGH, preferred_element_type=F32
        )
        for n, i in enumerate((j, j + 1)):
            part = change[:, n * lanes : (n + 1) * lanes]
            if batch == 0:
                dst_ref[i] = part + (iota((members, lanes), 0) == i).astype(F32)
            else:
                dst_ref[i] = part + trans_ref[i]


def compose_kernel(batches, me_ref, record_ref, *refs):
    given = refs[: 2 * len(batches)]
    trans_ref = refs[2 * len(batches)] if batches[0] else None
    out_ref = refs[-1]
    members = given[1].shape[0]
    devices = (record_ref.shape[1] - FIELDS * BATCH_COUNT) // BATCH_COUNT
    for n, batch in enumerate(batches):
        levels = copies_of(record_ref[me_ref[1], batch * devices : (batch + 1) * devices, :])
        source = trans_ref if n == 0 else out_ref
        compose(
            given[2 * n][...], given[2 * n + 1][...], levels, batch, source, out_ref, members + 8
        )


def final_kernel(
    row_strides, me_ref, lows_ref, highs_ref, record_ref, trans_ref, state_ref, out_ref,
    spread_ref, whole_ref, turned_ref,
):
    members, rows, lanes = state_ref.shape
    height, width = lows_ref.shape[1:]
    ncol = width // members
    devices = 2 * lows_ref.shape[0] * ncol
    batch = BATCH_COUNT - 1
    bands = bands_of(row_strides, me_ref[0], lows_ref, highs_ref)
    spread_sums(bands, spread_ref, ncol)
    solved = solve_sums(bands, ncol)
    levels = copies_of(record_ref[me_ref[1], batch * devices : (batch + 1) * devices, :])
    compose(spread_ref[...], solved, levels, batch, trans_ref, whole_ref, height)
    for i in range(members):
        hi, lo, _ = split3(whole_ref[:, i, :])
        turned_ref[:, i, :] = jnp.concatenate([hi, hi, lo, jnp.zeros_like(hi)], axis=0).T

    @pl.loop(0, rows // 8)
    def _(b):
        start = pl.multiple_of(b * 8, 8)
        turned = jnp.swapaxes(state_ref[:, pl.ds(start, 8), :], 0, 1)
        done = []
        for i in range(8):
            hi, lo, _ = split3(turned[i])
            right = jnp.concatenate([hi, lo, hi, jnp.zeros_like(hi)], axis=0).astype(BF16)
            done.append(
                jnp.dot(
                    turned_ref[start + i].astype(BF16), right, preferred_element_type=F32
                )
            )
        out_ref[:, pl.ds(start, 8), :] = jnp.swapaxes(jnp.stack(done), 0, 1)


def call(kernel, out_shape, in_specs, scratch=(), flops=10**6):
    return pl.pallas_call(
        kernel,
        out_shape=out_shape,
        in_specs=in_specs,
        out_specs=jax.tree.map(lambda _: VMEM, out_shape),
        scratch_shapes=list(scratch),
        compiler_params=PARAMS,
    )


def body(
    sample_heights, depth, land_sea, batch_order, obs_value, obs_error, obs_tile, obs_cell, loc_level
):
    members, rows, cols = sample_heights.shape
    ncol = lax.axis_size("col")
    nrow = lax.axis_size("row")
    devices = nrow * ncol
    strides, row_strides = strides_of(ncol), strides_of(nrow)
    groups = members // 8
    half = groups // 2
    height = members + 8
    me = jnp.stack([lax.axis_index("row"), lax.axis_index("col")]).astype(jnp.int32)

    def out(*shape, dtype=F32):
        return jax.ShapeDtypeStruct(shape, dtype)

    record_rows = BATCH_COUNT * devices + FIELDS * BATCH_COUNT
    sea = land_sea.astype(F32)
    coef = jnp.stack([0.01 * depth.astype(F32) * sea, sea])
    share = obs_cell.shape[1]
    order = jnp.pad(batch_order.astype(F32)[None], ((0, 7), (0, share - BATCH_COUNT)))
    observed = jnp.concatenate(
        [obs_tile[:, :, 0].astype(F32), obs_cell.astype(F32), obs_value, obs_error, order]
    )
    to_right, to_left, record = call(
        prep_kernel,
        (out(half + 1, rows, cols), out(half + 1, rows, cols), out(record_rows, cols)),
        [VMEM] * 4,
    )(sample_heights, coef, loc_level[:, :, 0, :], observed)
    left, right = shift_pair(to_left, to_right, "col")

    def slab(start):
        cut = lambda a: lax.slice_in_dim(a, start, start + HALO, axis=1)
        return jnp.concatenate([cut(a) for a in (sample_heights, coef, left, right)], axis=0)

    up, down = shift_pair(slab(0), slab(rows - HALO), "row")
    records = lax.all_to_all(
        jnp.broadcast_to(record, (ncol, *record.shape)), "col", split_axis=0, concat_axis=0, tiled=True
    )

    ext = rows + 2 * HALO
    tall = ext + 2 * HALO
    state = call(
        forecast_kernel,
        out(members, rows, cols),
        [VMEM] * 6,
        [
            pltpu.VMEM((members, tall, cols), F32),
            pltpu.VMEM((members, tall, cols), F32),
            pltpu.VMEM((members, ext, cols), F32),
            pltpu.VMEM((2 * groups, tall, cols), F32),
            pltpu.VMEM((2 * groups, tall, cols), F32),
            pltpu.VMEM((2 * groups, ext, cols), F32),
            pltpu.VMEM((2, tall, cols), F32),
            pltpu.VMEM((4, tall, cols), F32),
            pltpu.VMEM((10, ext, cols), F32),
            pltpu.VMEM((2, 10, ext, cols), F32),
            pltpu.VMEM((groups, ext, cols), F32),
        ],
    )(sample_heights, coef, left, right, up, down)

    mine = call(
        functools.partial(extract_kernel, obs_cell.shape[1]),
        out(BATCH_COUNT * members + FIELDS * BATCH_COUNT, cols),
        [SMEM, VMEM, VMEM],
        [pltpu.VMEM((8, cols), F32)],
    )(me, records, state)
    seen = gather_over(mine, "col")

    sums = call(
        functools.partial(first_kernel, members), out(height, members * ncol), [VMEM] * 2
    )(*seen)
    wide = max(LANES, 3 * devices)

    def compose_of(batches, given, trans):
        args = (me, records, *given) + (() if trans is None else (trans,))
        return call(
            functools.partial(compose_kernel, batches),
            out(members, members, cols),
            [SMEM] + [VMEM] * (len(args) - 1),
        )(*args)

    def moved_of(batches, target, given, z):
        args = (me, records, *seen, *given) + (() if z is None else (z,))
        return call(
            functools.partial(moved_kernel, strides, batches, target),
            out(ncol, members, cols),
            [SMEM] + [VMEM] * (len(args) - 1),
        )(*args)

    def next_of(batch, every, z):
        args = (me, *every, records, *seen) + (() if z is None else (z,))
        got = call(
            functools.partial(next_kernel, strides, row_strides, batch),
            (
                out(height, members * ncol),
                out(members * height, wide, dtype=BF16),
                out(members, LANES),
            ),
            [SMEM] + [VMEM] * (len(args) - 1),
        )(*args)
        return got[0], got[1:]

    def exchange(sums, beside):
        return gather_over(sums, "row", beside)

    every, _ = exchange(sums, ())
    sums, first = next_of(0, every, None)
    every, (z2, trans) = exchange(
        sums, (moved_of((0,), 2, first, None), compose_of((0,), first, None))
    )
    sums, second = next_of(1, every, z2)
    every, (z3,) = exchange(sums, (moved_of((0, 1), 3, first + second, None),))
    sums, third = next_of(2, every, z3)
    every, (trans,) = exchange(sums, (compose_of((1, 2), second + third, trans),))
    return call(
        functools.partial(final_kernel, row_strides),
        out(members, rows, cols),
        [SMEM] + [VMEM] * 5,
        [
            pltpu.VMEM((members * height, wide), BF16),
            pltpu.VMEM((members, members, cols), F32),
            pltpu.VMEM((rows, members, cols), F32),
        ],
    )(me, *every, records, trans, state)


def solution(mesh):
    return jax.shard_map(
        body,
        mesh=mesh,
        in_specs=(
            P(None, "row", "col"),
            P("row", "col"),
            P("row", "col"),
            P(),
            P(None, ("row", "col")),
            P(None, ("row", "col")),
            P(None, ("row", "col"), None),
            P(None, ("row", "col")),
            P(None, "row", "col", None),
        ),
        out_specs=P(None, "row", "col"),
        check_vma=False,
    )
```

```python
import functools

import jax
import jax.numpy as jnp
from jax import lax
from jax.experimental import pallas as pl
from jax.experimental.pallas import tpu as pltpu
from jax.sharding import PartitionSpec as P

BATCH_COUNT = 4
STEPS = 2
SWEEPS = 2
HALO = 8
SEG = 2 * HALO
LANES = 128
FIELDS = 4
HIGH = lax.Precision.HIGHEST
F32 = jnp.float32
BF16 = jnp.bfloat16
SMEM = pl.BlockSpec(memory_space=pltpu.SMEM)
VMEM = pl.BlockSpec(memory_space=pltpu.VMEM)
ANY = pl.BlockSpec(memory_space=pl.ANY)


def iota(shape, dim):
    return lax.broadcasted_iota(jnp.int32, shape, dim)


def strides_of(n):
    out = []
    while n > 1:
        n //= 2
        out.append(n)
    return out


def offset_at(position, strides):
    out = position * 0
    for bit, stride in enumerate(strides):
        out = out + ((position >> bit) & 1) * stride
    return out


def position_of(offset, strides):
    out = offset * 0
    for bit, stride in enumerate(strides):
        out = out + ((offset // stride) & 1) * (1 << bit)
    return out


def gather_over(block, axis, beside=None):
    n = lax.axis_size(axis)
    held = block[None]
    strides = strides_of(n)
    for stride in strides:
        if stride == strides[-1] and beside is not None:
            held, beside = lax.optimization_barrier((held, beside))
        other = lax.ppermute(held, axis, [(i, i ^ stride) for i in range(n)])
        if stride != strides[-1]:
            held = jnp.concatenate([held, other], axis=0)
    return (held, other) if beside is None else ((held, other), beside)


def shift_pair(low_send, high_send, axis):
    n = lax.axis_size(axis)
    forward = [(i, i + 1) for i in range(n - 1)]
    backward = [(b, a) for a, b in forward]
    return lax.ppermute(high_send, axis, forward), lax.ppermute(low_send, axis, backward)


def nt(a, b, precision=HIGH):
    return lax.dot_general(
        a, b, (((1,), (1,)), ((), ())), precision=precision, preferred_element_type=F32
    )


def split3(x):
    hi = x.astype(BF16).astype(F32)
    rest = x - hi
    mid = rest.astype(BF16).astype(F32)
    return hi, mid, rest - mid


def prep_kernel(
    h_hbm, depth_hbm, sea_hbm, loc_hbm, tile_hbm, cell_hbm, val_hbm, err_hbm, order_hbm,
    to_right_ref, to_left_ref, record_ref, coef_ref,
    h_ref, depth_ref, sea_ref, loc_ref, tile_ref, cell_ref, val_ref, err_ref, order_ref, sems,
):
    members, rows, lanes = h_ref.shape
    groups = members // 8
    half = groups // 2
    pairs = (
        (order_hbm, order_ref),
        (tile_hbm, tile_ref),
        (cell_hbm, cell_ref),
        (val_hbm, val_ref),
        (err_hbm, err_ref),
        (loc_hbm, loc_ref),
        (depth_hbm, depth_ref),
        (sea_hbm, sea_ref),
    )
    small = [
        pltpu.make_async_copy(source, target, sems.at[i])
        for i, (source, target) in enumerate(pairs)
    ]
    large = [
        pltpu.make_async_copy(
            h_hbm.at[pl.ds(8 * g, 8)], h_ref.at[pl.ds(8 * g, 8)], sems.at[len(pairs) + g]
        )
        for g in range(groups)
    ]
    for copy in small + large:
        copy.start()
    seg = iota((rows, lanes), 1) // SEG
    first = iota((rows, lanes), 1) % SEG < HALO
    for copy in small[:6]:
        copy.wait()

    devices = loc_ref.shape[1]
    base = BATCH_COUNT * devices
    fields = FIELDS * BATCH_COUNT
    width = val_ref.shape[1]
    record_ref[base:, :] = jnp.zeros((fields, lanes), F32)
    for k in range(BATCH_COUNT):
        batch = order_ref[k]
        record_ref[k * devices : (k + 1) * devices, :] = loc_ref[batch].astype(F32)
        for f, ref in enumerate((tile_ref, cell_ref, val_ref, err_ref)):
            row = base + f * BATCH_COUNT + k
            record_ref[row : row + 1, 0:width] = ref[pl.ds(batch, 1), :].astype(F32)

    for copy in small[6:]:
        copy.wait()
    sea = sea_ref[...].astype(F32)
    kappa = 0.01 * depth_ref[...].astype(F32) * sea
    coef_ref[0] = kappa
    coef_ref[1] = sea

    def pack(pick):
        out = None
        for q in range(8):
            rolled = pltpu.roll(pick(q), q * SEG + HALO, axis=1)
            out = rolled if out is None else jnp.where(seg == q, rolled, out)
        return out

    def send(g, a, b):
        to_right_ref[g] = jnp.where(first, a, pltpu.roll(b, HALO, axis=1))
        to_left_ref[g] = jnp.where(first, pltpu.roll(b, lanes - HALO, axis=1), a)

    send(half, pack(lambda q: kappa), pack(lambda q: sea))
    for copy in large:
        copy.wait()
    for g in range(half):
        send(g, pack(lambda q: h_ref[8 * g + q]), pack(lambda q: h_ref[8 * (g + half) + q]))


def forecast_kernel(
    h_ref, coef_ref, left_ref, right_ref, up_ref, down_ref, out_ref,
    a_ref, b_ref, rhs_ref, sa_ref, sb_ref, srhs_ref, k_ref, sk_ref, w_ref, sw_ref, edge_ref,
):
    members, rows, lanes = out_ref.shape
    groups = members // 8
    half = groups // 2
    ext = rows + 2 * HALO
    pad = HALO
    inner = pad + HALO
    block = 16
    starts = list(range(0, ext, block))

    for ref in (k_ref, sk_ref):
        for i in range(ref.shape[0]):
            ref[i, pl.ds(0, pad), :] = jnp.zeros((pad, lanes), F32)
            ref[i, pl.ds(pad + ext, pad), :] = jnp.zeros((pad, lanes), F32)
    for i in range(2):
        k_ref[i, pl.ds(pad, HALO), :] = up_ref[members + i]
        k_ref[i, pl.ds(inner, rows), :] = coef_ref[i]
        k_ref[i, pl.ds(inner + rows, HALO), :] = down_ref[members + i]

    @pl.loop(0, members)
    def _(m):
        a_ref[m, pl.ds(pad, HALO), :] = up_ref[m]
        a_ref[m, pl.ds(inner, rows), :] = h_ref[m]
        a_ref[m, pl.ds(inner + rows, HALO), :] = down_ref[m]

    def strips(start, first_row, at, number):
        shape = (block, lanes)
        seg = iota(shape, 1) // SEG
        first = iota(shape, 1) % SEG < HALO

        def incoming(which, g):
            base = members + 2 + which * (half + 1) + g
            ref = (left_ref, right_ref)[which]
            parts = []
            for s in range(start, start + block, HALO):
                if s < HALO:
                    parts.append(up_ref[base])
                elif s >= rows + HALO:
                    parts.append(down_ref[base])
                else:
                    parts.append(ref[g, pl.ds(s - HALO, HALO), :])
            return jnp.concatenate(parts, axis=0)

        own = None
        for q in range(8):
            if number:
                value = a_ref[first_row + q, pl.ds(pad + start, block), :]
            else:
                value = k_ref[first_row, pl.ds(pad + start, block), :]
            rolled = pltpu.roll(value, q * SEG + HALO, axis=1)
            own = rolled if own is None else jnp.where(seg == q, rolled, own)
        source = at % half if number else half
        from_left = incoming(0, source)
        from_right = incoming(1, source)
        if at >= half if number else at:
            from_left = pltpu.roll(from_left, lanes - HALO, axis=1)
            from_right = pltpu.roll(from_right, HALO, axis=1)
        return jnp.where(first, from_left, own), jnp.where(first, own, from_right)

    for start in starts:
        rows_here = pl.ds(pad + start, block)
        for i in range(2):
            lo, hi = strips(start, i, i, 0)
            sk_ref[2 * i, rows_here, :] = lo
            sk_ref[2 * i + 1, rows_here, :] = hi
        for g in range(groups):
            lo, hi = strips(start, 8 * g, g, groups)
            sa_ref[g, rows_here, :] = lo
            sa_ref[groups + g, rows_here, :] = hi

    lane = iota((block, lanes), 1)
    is_last = lane == lanes - 1
    is_first = lane == 0
    at_seven = lane % SEG == HALO - 1

    def sides(centre, edge):
        if edge is None:
            return pltpu.roll(centre, 1, axis=1), pltpu.roll(centre, lanes - 1, axis=1)
        return (
            jnp.where(is_first, edge, pltpu.roll(centre, 1, axis=1)),
            jnp.where(is_last, edge, pltpu.roll(centre, lanes - 1, axis=1)),
        )

    def edges_of(low, high):
        return jnp.where(
            at_seven, pltpu.roll(high, lanes - 1, axis=1), pltpu.roll(low, 1, axis=1)
        )

    def weights(ref, at, kap, sea, edges, start):
        here = pl.ds(pad + start, block)

        def four(src, i, edge):
            centre = src[i, here, :]
            return centre, [
                src[i, pl.ds(pad + start - 1, block), :],
                src[i, pl.ds(pad + start + 1, block), :],
                *sides(centre, edge),
            ]

        src = k_ref if edges is not None else sk_ref
        kc, kn = four(src, kap, None if edges is None else edges[0])
        sc, sn = four(src, sea, None if edges is None else edges[1])
        w = [0.5 * (kc + kn[i]) * sc * sn[i] for i in range(4)]
        wsum = w[0] + w[1] + w[2] + w[3]
        inverse = 1.0 / (1.0 + 0.5 * wsum)
        values = [1.0 - 0.5 * wsum] + [0.5 * v for v in w]
        values += [inverse] + [0.5 * v * inverse for v in w]
        for i, value in enumerate(values):
            if at is None:
                ref[i, pl.ds(start, block), :] = value
            else:
                ref[at, i, pl.ds(start, block), :] = value

    for start in starts:
        here = pl.ds(pad + start, block)
        edges = [
            pltpu.roll(
                edges_of(sk_ref[2 * i, here, :], sk_ref[2 * i + 1, here, :]), lanes - HALO, axis=1
            )
            for i in range(2)
        ]
        weights(w_ref, None, 0, 1, edges, start)
        weights(sw_ref, 0, 0, 2, None, start)
        weights(sw_ref, 1, 1, 3, None, start)

    def update(src, dst, rhs, m, start, coef, edge, explicit, store):
        centre = src[m, pl.ds(pad + start, block), :]
        upper = src[m, pl.ds(pad + start - 1, block), :]
        lower = src[m, pl.ds(pad + start + 1, block), :]
        west, east = sides(centre, edge)
        if explicit:
            c0, h0, h1, h2, h3, inverse = coef
            total = c0 * centre + (h0 * upper + h1 * lower) + (h2 * west + h3 * east)
            rhs[m, pl.ds(start, block), :] = total * inverse
        else:
            v0, v1, v2, v3 = coef
            total = rhs[m, pl.ds(start, block), :] + (v0 * upper + v1 * lower)
            total = total + (v2 * west + v3 * east)
        store(m, start, total)

    def sweep(src, dst, ssrc, sdst, explicit, last):
        chosen = range(6) if explicit else range(6, 10)

        def to(ref):
            def store(m, start, value):
                ref[m, pl.ds(pad + start, block), :] = value

            return store

        def to_out(m, start, value):
            out_ref[m, pl.ds(start - HALO, block), :] = value

        @pl.loop(0, groups)
        def _(g):
            for start in starts:
                here = pl.ds(pad + start, block)
                edge_ref[g, pl.ds(start, block), :] = edges_of(
                    ssrc[g, here, :], ssrc[groups + g, here, :]
                )
                for side in (0, 1) if not last else ():
                    coef = [sw_ref[side, i, pl.ds(start, block), :] for i in chosen]
                    update(
                        ssrc, sdst, srhs_ref, side * groups + g, start, coef, None, explicit,
                        to(sdst),
                    )

        @pl.loop(0, groups)
        def _(g):
            for start in range(HALO, HALO + rows, block) if last else starts:
                coef = [w_ref[i, pl.ds(start, block), :] for i in chosen]
                edge = edge_ref[g, pl.ds(start, block), :]
                for q in range(8):
                    rolled = pltpu.roll(edge, (lanes - HALO - SEG * q) % lanes, axis=1)
                    update(
                        src, dst, rhs_ref, 8 * g + q, start, coef, rolled, explicit,
                        to_out if last else to(dst),
                    )

    now, later = (a_ref, sa_ref), (b_ref, sb_ref)
    for step in range(STEPS):
        for stage in range(SWEEPS + 1):
            last = step == STEPS - 1 and stage == SWEEPS
            sweep(now[0], later[0], now[1], later[1], stage == 0, last)
            now, later = later, now


def extract_kernel(owner_share, me_ref, record_ref, state_ref, out_ref, meta_ref):
    members, rows, lanes = state_ref.shape
    ncol, height, _ = record_ref.shape
    fields = FIELDS * BATCH_COUNT
    base = height - fields
    capacity = lanes // ncol
    me = me_ref[1]
    stacked = jnp.concatenate([record_ref[p, base:, :] for p in range(ncol)], axis=0)
    pieces = [
        stacked[i * lanes : (i + 1) * lanes, :].T for i in range(ncol * fields // lanes)
    ]
    lane = iota((lanes, lanes), 1)
    triangle = (lane < iota((lanes, lanes), 0)).astype(BF16)
    valid = iota((lanes, lanes), 0) < owner_share
    slot = (lane % capacity).astype(F32)

    def spread(f, k):
        index = (lane // capacity) * fields + f * BATCH_COUNT + k
        out = None
        for i, piece in enumerate(pieces):
            got = jnp.take_along_axis(piece, jnp.clip(index - i * lanes, 0, lanes - 1), axis=1)
            out = got if out is None else jnp.where(index >= i * lanes, got, out)
        return out

    base = BATCH_COUNT * members
    out_ref[base + 3 * BATCH_COUNT :, :] = jnp.zeros((BATCH_COUNT, lanes), F32)
    for k in range(BATCH_COUNT):
        mine = valid & (spread(0, k) == me.astype(F32))
        rank = jnp.dot(triangle, mine.astype(BF16), preferred_element_type=F32)
        hot = mine & (rank == slot)

        def slotted(values):
            return jnp.sum(jnp.where(hot, values, 0.0), axis=0, keepdims=True)

        cell = spread(1, k).astype(jnp.int32)
        x = cell // lanes
        error = jnp.where(hot, spread(3, k), 1.0)
        for n, values in enumerate((1.0 / error, spread(2, k), (x + 1).astype(F32))):
            row = base + n * BATCH_COUNT + k
            out_ref[row : row + 1, :] = slotted(values) - (1.0 if n == 2 else 0.0)
        meta_ref[k : k + 1, :] = slotted((cell - x * lanes).astype(F32))

    level = iota((8, lanes), 0)
    place = base + 2 * BATCH_COUNT
    for k in range(BATCH_COUNT):
        xs = jnp.broadcast_to(out_ref[place + k : place + k + 1, :], (8, lanes)).astype(jnp.int32)
        ys = jnp.broadcast_to(meta_ref[k : k + 1, :], (8, lanes)).astype(jnp.int32)

        @pl.loop(0, members // 8)
        def _(g):
            totals = []
            for q in range(8):
                total = jnp.zeros((8, lanes), F32)
                for s in range(0, rows, 8):
                    block = state_ref[8 * g + q, pl.ds(s, 8), :]
                    got = jnp.take_along_axis(block, ys, axis=1)
                    total = total + jnp.where(xs == level + s, got, 0.0)
                totals.append(jnp.sum(total, axis=0, keepdims=True))
            row = pl.multiple_of(k * members + 8 * g, 8)
            out_ref[pl.ds(row, 8), :] = jnp.concatenate(totals, axis=0)


def band_sums(ncol, parts):
    lanes = LANES
    mask = (iota((ncol, lanes), 1) // (lanes // ncol) == iota((ncol, lanes), 0)).astype(F32)
    row = iota((8, lanes), 0)
    lefts, rights = [], []
    for z, w, value in parts:
        members = z.shape[0]
        mean = jnp.mean(z, axis=0, keepdims=True)
        anomaly = z - mean
        innov = value - mean
        scaled = anomaly * w

        def masked(values):
            return jnp.concatenate(
                [values[m : m + 1, :] * mask for m in range(members)], axis=0
            ).astype(BF16)

        hi, lo, _ = split3(scaled)
        hi, lo = masked(hi), masked(lo)
        lefts += [hi, lo, hi]
        right = jnp.concatenate([anomaly, jnp.where(row == 0, innov, 0.0)], axis=0)
        hi, lo, _ = split3(right)
        hi, lo = hi.astype(BF16), lo.astype(BF16)
        rights += [hi, hi, lo]
    return nt(jnp.concatenate(rights, axis=1), jnp.concatenate(lefts, axis=1), None)


def seen_rows(seen_refs, p):
    half = seen_refs[0].shape[0]
    return seen_refs[p // half].at[p % half]


def first_kernel(members, low_ref, high_ref, out_ref):
    seen = (low_ref, high_ref)
    ncol = 2 * low_ref.shape[0]
    parts = []
    for p in range(ncol):
        rows = seen_rows(seen, p)
        meta = BATCH_COUNT * members
        parts.append(
            (
                rows[0:members, :],
                rows[meta : meta + 1, :],
                rows[meta + BATCH_COUNT : meta + BATCH_COUNT + 1, :],
            )
        )
    out_ref[...] = band_sums(ncol, parts)


def bands_of(row_strides, me, low_ref, high_ref):
    half = low_ref.shape[0]
    out = []
    for r in range(2 * half):
        at = position_of(jnp.bitwise_xor(me, r), row_strides)
        out.append(
            jnp.where(at < half, low_ref[at % half], high_ref[at % half])
        )
    return out


def spread_sums(bands, spread_ref, ncol):
    height, width = bands[0].shape
    nrow = len(bands)
    members = width // ncol
    devices = nrow * ncol
    lanes = LANES
    lane = iota((height, lanes), 1)
    owner = lane % devices
    which = lane // devices
    per = max(1, lanes // devices)
    for first in range(0, members, per):
        tile, start = divmod(first * ncol, lanes)
        index = start + which * ncol + owner % ncol
        group = None
        for r in range(nrow):
            piece = bands[r][:, tile * lanes : (tile + 1) * lanes]
            got = jnp.take_along_axis(piece, index, axis=1)
            group = got if group is None else jnp.where(owner // ncol == r, got, group)
        for n in range(per):
            m = first + n
            if per > 1:
                value = jnp.take_along_axis(group, n * devices + owner, axis=1)
                hi, mid, lo = split3(value)
                value = jnp.where(which == 0, hi, jnp.where(which == 1, mid, lo))
            else:
                value = jnp.concatenate(split3(group), axis=1)
            spread_ref[pl.ds(m * height, height), :] = value.astype(BF16)


def copies_of(levels):
    devices = levels.shape[0]
    copies = max(3, LANES // devices)
    scaled = (levels * 0.125).astype(BF16)
    return jnp.concatenate([scaled] * 3 + [jnp.zeros_like(scaled)] * (copies - 3), axis=0)


def solve_sums(bands, ncol):
    height, width = bands[0].shape
    members = width // ncol
    lanes = LANES
    total = bands[0]
    for band in bands[1:]:
        total = total + band
    pick = (iota((width, lanes), 0) // ncol == iota((width, lanes), 1)).astype(BF16)
    a = sum(
        jnp.dot(part.astype(BF16), pick, preferred_element_type=F32)
        for part in reversed(split3(total))
    )
    row = iota((height, lanes), 0)
    lane = iota((height, lanes), 1)
    a = a + jnp.where((row == lane) & (row < members), members - 1.0, 0.0)
    lane1 = iota((1, lanes), 1)
    block = 8
    for start in range(0, members, block):
        columns = [
            jnp.broadcast_to(a[:, k : k + 1], (height, lanes))
            for k in range(start, start + block)
        ]
        for s in range(block):
            k, column = start + s, columns[s]
            inverse = 1.0 / column[k : k + 1, :]
            scaled = jnp.where(lane1 == k, inverse, a[k : k + 1, :] * inverse)
            a = jnp.where(row == k, scaled, jnp.where(lane == k, 0.0, a) - column * scaled)
            for t in range(s + 1, block):
                part = columns[t][k : k + 1, :] * inverse
                columns[t] = jnp.where(row == k, part, columns[t] - column * part)
    gain = a[members : members + 1, :] * (1.0 / (members - 1))
    out = jnp.where(lane1 < members, -0.5 * a[0:members, :] + gain, 0.0)
    return jnp.where(lane1 == members, 1.0 / (members - 1), out)


def product3(left, right):
    lhi, llo, _ = split3(left)
    rhi, rlo, _ = split3(right)
    return jnp.dot(
        jnp.concatenate([lhi, lhi, llo], axis=1).astype(BF16),
        jnp.concatenate([rhi, rlo, rhi], axis=0).astype(BF16),
        preferred_element_type=F32,
    )


def apply_sums(spread, levels, z, height):
    at = jnp.dot(spread, levels, preferred_element_type=F32)
    total = None
    for m in range(z.shape[0]):
        term = at[m * height : (m + 1) * height, :] * z[m : m + 1, :]
        total = term if total is None else total + term
    return total


def levels_at(rows, batch, devices, place):
    lanes = LANES
    hot = (iota((lanes, lanes), 0) == place.astype(jnp.int32)).astype(BF16)
    table = rows[batch * devices : (batch + 1) * devices, :].astype(BF16)
    return jnp.dot(table, hot, preferred_element_type=F32)


def moved(strides, me, record_ref, seen, spread, solved, batch, target, devices, read):
    ncol = 2 * seen[0].shape[0]
    members = solved.shape[0]
    height = members + 8
    place = BATCH_COUNT * members + 2 * BATCH_COUNT + target
    out = []
    for p in range(0, ncol, 2):
        pair = (p, p + 1)
        levels = []
        for i in pair:
            offset = sum(((i >> bit) & 1) * stride for bit, stride in enumerate(strides))
            levels.append(
                copies_of(
                    levels_at(
                        record_ref.at[jnp.bitwise_xor(me, offset)], batch, devices,
                        seen_rows(seen, i)[place : place + 1, :],
                    )
                )
            )
        z = jnp.concatenate([read(i) for i in pair], axis=1)
        sums = apply_sums(spread, jnp.concatenate(levels, axis=1), z, height)
        z = z + product3(solved[:, 0:height], sums)
        out += [z[:, 0:LANES], z[:, LANES:]]
    return out


def reader(seen, z_ref, members, target):
    if z_ref is not None:
        return lambda i: z_ref[i]
    return lambda i: seen_rows(seen, i)[target * members : (target + 1) * members, :]


def next_kernel(strides, row_strides, batch, *refs):
    me_ref, lows_ref, highs_ref, record_ref = refs[:4]
    seen = refs[4:6]
    z_ref = refs[6] if batch else None
    out_ref, spread_ref, solved_ref = refs[-3:]
    ncol = 2 * seen[0].shape[0]
    members = solved_ref.shape[0]
    devices = 2 * ncol * lows_ref.shape[0]
    bands = bands_of(row_strides, me_ref[0], lows_ref, highs_ref)
    spread_sums(bands, spread_ref, ncol)
    solved = solve_sums(bands, ncol)
    solved_ref[...] = solved
    target = batch + 1
    zs = moved(
        strides, me_ref[1], record_ref, seen, spread_ref[...], solved, batch, target, devices,
        reader(seen, z_ref, members, target),
    )
    parts = []
    meta = BATCH_COUNT * members + target
    for p in range(ncol):
        rows = seen_rows(seen, p)
        parts.append(
            (
                zs[p],
                rows[meta : meta + 1, :],
                rows[meta + BATCH_COUNT : meta + BATCH_COUNT + 1, :],
            )
        )
    out_ref[...] = band_sums(ncol, parts)


def moved_kernel(strides, batches, target, *refs):
    me_ref, record_ref = refs[:2]
    seen = refs[2:4]
    given = refs[4 : 4 + 2 * len(batches)]
    z_ref = refs[4 + 2 * len(batches)] if len(refs) == 6 + 2 * len(batches) else None
    out_ref = refs[-1]
    members = given[1].shape[0]
    devices = (record_ref.shape[1] - FIELDS * BATCH_COUNT) // BATCH_COUNT
    read = reader(seen, z_ref, members, target)
    for n, batch in enumerate(batches):
        zs = moved(
            strides, me_ref[1], record_ref, seen, given[2 * n][...], given[2 * n + 1][...],
            batch, target, devices, read,
        )
        read = zs.__getitem__
    for p, z in enumerate(zs):
        out_ref[p] = z


def compose(spread, solved, levels, batch, trans_ref, dst_ref, height):
    members = solved.shape[0]
    at = jnp.dot(spread, levels, preferred_element_type=F32)
    lanes = LANES
    gain = solved[:, 0:height]
    for j in range(0, members, 2):
        sums = []
        for i in (j, j + 1):
            if batch == 0:
                sums.append(at[i * height : (i + 1) * height, :])
            else:
                total = None
                for m in range(members):
                    term = at[m * height : (m + 1) * height, :] * trans_ref[i, m : m + 1, :]
                    total = term if total is None else total + term
                sums.append(total)
        change = product3(gain, jnp.concatenate(sums, axis=1))
        for n, i in enumerate((j, j + 1)):
            part = change[:, n * lanes : (n + 1) * lanes]
            if batch == 0:
                dst_ref[i] = part + (iota((members, lanes), 0) == i).astype(F32)
            else:
                dst_ref[i] = part + trans_ref[i]


def compose_kernel(batches, me_ref, record_ref, *refs):
    given = refs[: 2 * len(batches)]
    trans_ref = refs[2 * len(batches)] if batches[0] else None
    out_ref = refs[-1]
    members = given[1].shape[0]
    devices = (record_ref.shape[1] - FIELDS * BATCH_COUNT) // BATCH_COUNT
    for n, batch in enumerate(batches):
        levels = copies_of(record_ref[me_ref[1], batch * devices : (batch + 1) * devices, :])
        source = trans_ref if n == 0 else out_ref
        compose(
            given[2 * n][...], given[2 * n + 1][...], levels, batch, source, out_ref, members + 8
        )


def split_kernel(state_ref, out_ref):
    members, rows, _ = state_ref.shape

    @pl.loop(0, rows // 8)
    def _(b):
        start = pl.multiple_of(b * 8, 8)
        turned = jnp.swapaxes(state_ref[:, pl.ds(start, 8), :], 0, 1)
        for i in range(8):
            hi, lo, _ = split3(turned[i])
            out_ref[start + i] = jnp.concatenate([hi, lo], axis=0).astype(BF16)


def final_kernel(
    row_strides, me_ref, lows_ref, highs_ref, record_ref, trans_ref, state_ref, out_ref,
    spread_ref, whole_ref, turned_ref,
):
    rows, lanes = state_ref.shape[0], state_ref.shape[2]
    members = state_ref.shape[1] // 2
    height, width = lows_ref.shape[1:]
    ncol = width // members
    devices = 2 * lows_ref.shape[0] * ncol
    batch = BATCH_COUNT - 1
    bands = bands_of(row_strides, me_ref[0], lows_ref, highs_ref)
    spread_sums(bands, spread_ref, ncol)
    solved = solve_sums(bands, ncol)
    levels = copies_of(record_ref[me_ref[1], batch * devices : (batch + 1) * devices, :])
    compose(spread_ref[...], solved, levels, batch, trans_ref, whole_ref, height)
    for i in range(members):
        hi, lo, _ = split3(whole_ref[:, i, :])
        turned_ref[:, i, :] = jnp.concatenate([hi, hi, lo, jnp.zeros_like(hi)], axis=0).T

    @pl.loop(0, rows // 8)
    def _(b):
        start = pl.multiple_of(b * 8, 8)
        done = []
        for i in range(8):
            both = state_ref[start + i]
            right = jnp.concatenate([both, both[0:members]], axis=0)
            left = turned_ref[start + i][:, 0 : 3 * members].astype(BF16)
            done.append(jnp.dot(left, right, preferred_element_type=F32))
        out_ref[:, pl.ds(start, 8), :] = jnp.swapaxes(jnp.stack(done), 0, 1)


def call(kernel, out_shape, in_specs, scratch=(), limit=48, out_specs=None):
    return pl.pallas_call(
        kernel,
        out_shape=out_shape,
        in_specs=in_specs,
        out_specs=out_specs or jax.tree.map(lambda _: VMEM, out_shape),
        scratch_shapes=list(scratch),
        compiler_params=pltpu.CompilerParams(vmem_limit_bytes=limit * 1024 * 1024),
    )


def body(
    sample_heights, depth, land_sea, batch_order, obs_value, obs_error, obs_tile, obs_cell, loc_level
):
    members, rows, cols = sample_heights.shape
    ncol = lax.axis_size("col")
    nrow = lax.axis_size("row")
    devices = nrow * ncol
    strides, row_strides = strides_of(ncol), strides_of(nrow)
    groups = members // 8
    half = groups // 2
    height = members + 8
    me = jnp.stack([lax.axis_index("row"), lax.axis_index("col")]).astype(jnp.int32)

    def out(*shape, dtype=F32):
        return jax.ShapeDtypeStruct(shape, dtype)

    record_rows = BATCH_COUNT * devices + FIELDS * BATCH_COUNT
    share = obs_cell.shape[1]
    to_right, to_left, record, coef = call(
        prep_kernel,
        (out(half + 1, rows, cols), out(half + 1, rows, cols), out(record_rows, cols), out(2, rows, cols)),
        [ANY] * 9,
        [
            pltpu.VMEM((members, rows, cols), F32),
            pltpu.VMEM((rows, cols), jnp.int32),
            pltpu.VMEM((rows, cols), jnp.int32),
            pltpu.VMEM((BATCH_COUNT, devices, rows), jnp.int32),
            pltpu.VMEM((BATCH_COUNT, share), jnp.int32),
            pltpu.VMEM((BATCH_COUNT, share), jnp.int32),
            pltpu.VMEM((BATCH_COUNT, share), F32),
            pltpu.VMEM((BATCH_COUNT, share), F32),
            pltpu.SMEM((BATCH_COUNT,), jnp.int32),
            pltpu.SemaphoreType.DMA((8 + groups,)),
        ],
        limit=58,
    )(
        sample_heights, depth, land_sea, jnp.transpose(loc_level[:, :, 0, :], (0, 2, 1)), obs_tile[:, :, 0], obs_cell,
        obs_value, obs_error, batch_order,
    )
    left, right = shift_pair(to_left, to_right, "col")

    def slab(start):
        cut = lambda a: lax.slice_in_dim(a, start, start + HALO, axis=1)
        return jnp.concatenate([cut(a) for a in (sample_heights, coef, left, right)], axis=0)

    up, down = shift_pair(slab(0), slab(rows - HALO), "row")
    records = lax.all_to_all(
        jnp.broadcast_to(record, (ncol, *record.shape)), "col", split_axis=0, concat_axis=0, tiled=True
    )

    ext = rows + 2 * HALO
    tall = ext + 2 * HALO
    state = call(
        forecast_kernel,
        out(members, rows, cols),
        [VMEM] * 6,
        [
            pltpu.VMEM((members, tall, cols), F32),
            pltpu.VMEM((members, tall, cols), F32),
            pltpu.VMEM((members, ext, cols), F32),
            pltpu.VMEM((2 * groups, tall, cols), F32),
            pltpu.VMEM((2 * groups, tall, cols), F32),
            pltpu.VMEM((2 * groups, ext, cols), F32),
            pltpu.VMEM((2, tall, cols), F32),
            pltpu.VMEM((4, tall, cols), F32),
            pltpu.VMEM((10, ext, cols), F32),
            pltpu.VMEM((2, 10, ext, cols), F32),
            pltpu.VMEM((groups, ext, cols), F32),
        ],
    )(sample_heights, coef, left, right, up, down)
    mine = call(
        functools.partial(extract_kernel, share),
        out(BATCH_COUNT * members + FIELDS * BATCH_COUNT, cols),
        [SMEM, VMEM, VMEM],
        [pltpu.VMEM((8, cols), F32)],
    )(me, records, state)
    seen = gather_over(mine, "col")
    parts = call(split_kernel, out(rows, 2 * members, cols, dtype=BF16), [VMEM])(state)

    sums = call(
        functools.partial(first_kernel, members), out(height, members * ncol), [VMEM] * 2
    )(*seen)
    wide = max(LANES, 3 * devices)

    def compose_of(batches, given, trans):
        args = (me, records, *given) + (() if trans is None else (trans,))
        return call(
            functools.partial(compose_kernel, batches),
            out(members, members, cols),
            [SMEM] + [VMEM] * (len(args) - 1),
        )(*args)

    def moved_of(batches, target, given, z):
        args = (me, records, *seen, *given) + (() if z is None else (z,))
        return call(
            functools.partial(moved_kernel, strides, batches, target),
            out(ncol, members, cols),
            [SMEM] + [VMEM] * (len(args) - 1),
        )(*args)

    def next_of(batch, every, z):
        args = (me, *every, records, *seen) + (() if z is None else (z,))
        got = call(
            functools.partial(next_kernel, strides, row_strides, batch),
            (
                out(height, members * ncol),
                out(members * height, wide, dtype=BF16),
                out(members, LANES),
            ),
            [SMEM] + [VMEM] * (len(args) - 1),
        )(*args)
        return got[0], got[1:]

    def exchange(sums, beside):
        return gather_over(sums, "row", beside)

    every, _ = exchange(sums, ())
    sums, first = next_of(0, every, None)
    every, (z2,) = exchange(sums, (moved_of((0,), 2, first, None),))
    trans = compose_of((0,), first, None)
    sums, second = next_of(1, every, z2)
    every, (z3,) = exchange(sums, (moved_of((0, 1), 3, first + second, None),))
    sums, third = next_of(2, every, z3)
    every, (trans,) = exchange(sums, (compose_of((1,), second, trans),))
    trans = compose_of((2,), third, trans)
    return call(
        functools.partial(final_kernel, row_strides),
        out(members, rows, cols),
        [SMEM] + [VMEM] * 5,
        [
            pltpu.VMEM((members * height, wide), BF16),
            pltpu.VMEM((members, members, cols), F32),
            pltpu.VMEM((rows, members, cols), F32),
        ],
    )(me, *every, records, trans, parts)


def solution(mesh):
    return jax.shard_map(
        body,
        mesh=mesh,
        in_specs=(
            P(None, "row", "col"),
            P("row", "col"),
            P("row", "col"),
            P(),
            P(None, ("row", "col")),
            P(None, ("row", "col")),
            P(None, ("row", "col"), None),
            P(None, ("row", "col")),
            P(None, "row", "col", None),
        ),
        out_specs=P(None, "row", "col"),
        check_vma=False,
    )
```

```python
import functools

import jax
import jax.numpy as jnp
from jax import lax
from jax.experimental import pallas as pl
from jax.experimental.pallas import tpu as pltpu
from jax.sharding import PartitionSpec as P

BATCH_COUNT = 4
STEPS = 2
SWEEPS = 2
HALO = 8
SEG = 2 * HALO
LANES = 128
FIELDS = 4
HIGH = lax.Precision.HIGHEST
F32 = jnp.float32
BF16 = jnp.bfloat16
SMEM = pl.BlockSpec(memory_space=pltpu.SMEM)
VMEM = pl.BlockSpec(memory_space=pltpu.VMEM)
ANY = pl.BlockSpec(memory_space=pl.ANY)


def iota(shape, dim):
    return lax.broadcasted_iota(jnp.int32, shape, dim)


def strides_of(n):
    out = []
    while n > 1:
        n //= 2
        out.append(n)
    return out


def offset_at(position, strides):
    out = position * 0
    for bit, stride in enumerate(strides):
        out = out + ((position >> bit) & 1) * stride
    return out


def position_of(offset, strides):
    out = offset * 0
    for bit, stride in enumerate(strides):
        out = out + ((offset // stride) & 1) * (1 << bit)
    return out


def gather_over(block, axis, early=(), late=()):
    n = lax.axis_size(axis)
    held = block[None]
    strides = strides_of(n)
    for stride in strides:
        if stride == strides[-1]:
            held, early = lax.optimization_barrier((held, early))
        other = lax.ppermute(held, axis, [(i, i ^ stride) for i in range(n)])
        if stride != strides[-1]:
            held = jnp.concatenate([held, other], axis=0)
    other, late = lax.optimization_barrier((other, late))
    return (held, other), early, late


def shift_pair(low_send, high_send, axis):
    n = lax.axis_size(axis)
    forward = [(i, i + 1) for i in range(n - 1)]
    backward = [(b, a) for a, b in forward]
    return lax.ppermute(high_send, axis, forward), lax.ppermute(low_send, axis, backward)


def nt(a, b, precision=HIGH):
    return lax.dot_general(
        a, b, (((1,), (1,)), ((), ())), precision=precision, preferred_element_type=F32
    )


def split3(x):
    hi = x.astype(BF16).astype(F32)
    rest = x - hi
    mid = rest.astype(BF16).astype(F32)
    return hi, mid, rest - mid


def prep_kernel(
    h_hbm, depth_hbm, sea_hbm, loc_hbm, tile_hbm, cell_hbm, val_hbm, err_hbm, order_hbm,
    to_right_ref, to_left_ref, record_ref, coef_ref,
    h_ref, depth_ref, sea_ref, loc_ref, tile_ref, cell_ref, val_ref, err_ref, order_ref, sems,
):
    members, rows, lanes = h_ref.shape
    groups = members // 8
    half = groups // 2
    pairs = (
        (order_hbm, order_ref),
        (tile_hbm, tile_ref),
        (cell_hbm, cell_ref),
        (val_hbm, val_ref),
        (err_hbm, err_ref),
        (loc_hbm, loc_ref),
        (depth_hbm, depth_ref),
        (sea_hbm, sea_ref),
    )
    small = [
        pltpu.make_async_copy(source, target, sems.at[i])
        for i, (source, target) in enumerate(pairs)
    ]
    large = [
        pltpu.make_async_copy(
            h_hbm.at[pl.ds(8 * g, 8)], h_ref.at[pl.ds(8 * g, 8)], sems.at[len(pairs) + g]
        )
        for g in range(groups)
    ]
    for copy in small + large:
        copy.start()
    seg = iota((rows, lanes), 1) // SEG
    first = iota((rows, lanes), 1) % SEG < HALO
    for copy in small[:6]:
        copy.wait()

    devices = loc_ref.shape[1]
    base = BATCH_COUNT * devices
    fields = FIELDS * BATCH_COUNT
    width = val_ref.shape[1]
    record_ref[base:, :] = jnp.zeros((fields, lanes), F32)
    for k in range(BATCH_COUNT):
        batch = order_ref[k]
        record_ref[k * devices : (k + 1) * devices, :] = loc_ref[batch].astype(F32)
        for f, ref in enumerate((tile_ref, cell_ref, val_ref, err_ref)):
            row = base + f * BATCH_COUNT + k
            record_ref[row : row + 1, 0:width] = ref[pl.ds(batch, 1), :].astype(F32)

    for copy in small[6:]:
        copy.wait()
    sea = sea_ref[...].astype(F32)
    kappa = 0.01 * depth_ref[...].astype(F32) * sea
    coef_ref[0] = kappa
    coef_ref[1] = sea

    def pack(pick):
        out = None
        for q in range(8):
            rolled = pltpu.roll(pick(q), q * SEG + HALO, axis=1)
            out = rolled if out is None else jnp.where(seg == q, rolled, out)
        return out

    def send(g, a, b):
        to_right_ref[g] = jnp.where(first, a, pltpu.roll(b, HALO, axis=1))
        to_left_ref[g] = jnp.where(first, pltpu.roll(b, lanes - HALO, axis=1), a)

    send(half, pack(lambda q: kappa), pack(lambda q: sea))
    for copy in large:
        copy.wait()
    for g in range(half):
        send(g, pack(lambda q: h_ref[8 * g + q]), pack(lambda q: h_ref[8 * (g + half) + q]))


def forecast_kernel(
    h_ref, coef_ref, left_ref, right_ref, up_ref, down_ref, out_ref,
    a_ref, b_ref, rhs_ref, sa_ref, sb_ref, srhs_ref, k_ref, sk_ref, w_ref, sw_ref, edge_ref,
):
    members, rows, lanes = out_ref.shape
    groups = members // 8
    half = groups // 2
    ext = rows + 2 * HALO
    pad = HALO
    inner = pad + HALO
    block = 16
    starts = list(range(0, ext, block))

    for ref in (k_ref, sk_ref):
        for i in range(ref.shape[0]):
            ref[i, pl.ds(0, pad), :] = jnp.zeros((pad, lanes), F32)
            ref[i, pl.ds(pad + ext, pad), :] = jnp.zeros((pad, lanes), F32)
    for i in range(2):
        k_ref[i, pl.ds(pad, HALO), :] = up_ref[members + i]
        k_ref[i, pl.ds(inner, rows), :] = coef_ref[i]
        k_ref[i, pl.ds(inner + rows, HALO), :] = down_ref[members + i]

    @pl.loop(0, members)
    def _(m):
        a_ref[m, pl.ds(pad, HALO), :] = up_ref[m]
        a_ref[m, pl.ds(inner, rows), :] = h_ref[m]
        a_ref[m, pl.ds(inner + rows, HALO), :] = down_ref[m]

    def strips(start, first_row, at, number):
        shape = (block, lanes)
        seg = iota(shape, 1) // SEG
        first = iota(shape, 1) % SEG < HALO

        def incoming(which, g):
            base = members + 2 + which * (half + 1) + g
            ref = (left_ref, right_ref)[which]
            parts = []
            for s in range(start, start + block, HALO):
                if s < HALO:
                    parts.append(up_ref[base])
                elif s >= rows + HALO:
                    parts.append(down_ref[base])
                else:
                    parts.append(ref[g, pl.ds(s - HALO, HALO), :])
            return jnp.concatenate(parts, axis=0)

        own = None
        for q in range(8):
            if number:
                value = a_ref[first_row + q, pl.ds(pad + start, block), :]
            else:
                value = k_ref[first_row, pl.ds(pad + start, block), :]
            rolled = pltpu.roll(value, q * SEG + HALO, axis=1)
            own = rolled if own is None else jnp.where(seg == q, rolled, own)
        source = at % half if number else half
        from_left = incoming(0, source)
        from_right = incoming(1, source)
        if at >= half if number else at:
            from_left = pltpu.roll(from_left, lanes - HALO, axis=1)
            from_right = pltpu.roll(from_right, HALO, axis=1)
        return jnp.where(first, from_left, own), jnp.where(first, own, from_right)

    for start in starts:
        rows_here = pl.ds(pad + start, block)
        for i in range(2):
            lo, hi = strips(start, i, i, 0)
            sk_ref[2 * i, rows_here, :] = lo
            sk_ref[2 * i + 1, rows_here, :] = hi
        for g in range(groups):
            lo, hi = strips(start, 8 * g, g, groups)
            sa_ref[g, rows_here, :] = lo
            sa_ref[groups + g, rows_here, :] = hi

    lane = iota((block, lanes), 1)
    is_last = lane == lanes - 1
    is_first = lane == 0
    at_seven = lane % SEG == HALO - 1

    def sides(centre, edge):
        if edge is None:
            return pltpu.roll(centre, 1, axis=1), pltpu.roll(centre, lanes - 1, axis=1)
        return (
            jnp.where(is_first, edge, pltpu.roll(centre, 1, axis=1)),
            jnp.where(is_last, edge, pltpu.roll(centre, lanes - 1, axis=1)),
        )

    def edges_of(low, high):
        return jnp.where(
            at_seven, pltpu.roll(high, lanes - 1, axis=1), pltpu.roll(low, 1, axis=1)
        )

    def weights(ref, at, kap, sea, edges, start):
        here = pl.ds(pad + start, block)

        def four(src, i, edge):
            centre = src[i, here, :]
            return centre, [
                src[i, pl.ds(pad + start - 1, block), :],
                src[i, pl.ds(pad + start + 1, block), :],
                *sides(centre, edge),
            ]

        src = k_ref if edges is not None else sk_ref
        kc, kn = four(src, kap, None if edges is None else edges[0])
        sc, sn = four(src, sea, None if edges is None else edges[1])
        w = [0.5 * (kc + kn[i]) * sc * sn[i] for i in range(4)]
        wsum = w[0] + w[1] + w[2] + w[3]
        inverse = 1.0 / (1.0 + 0.5 * wsum)
        values = [1.0 - 0.5 * wsum] + [0.5 * v for v in w]
        values += [inverse] + [0.5 * v * inverse for v in w]
        for i, value in enumerate(values):
            if at is None:
                ref[i, pl.ds(start, block), :] = value
            else:
                ref[at, i, pl.ds(start, block), :] = value

    for start in starts:
        here = pl.ds(pad + start, block)
        edges = [
            pltpu.roll(
                edges_of(sk_ref[2 * i, here, :], sk_ref[2 * i + 1, here, :]), lanes - HALO, axis=1
            )
            for i in range(2)
        ]
        weights(w_ref, None, 0, 1, edges, start)
        weights(sw_ref, 0, 0, 2, None, start)
        weights(sw_ref, 1, 1, 3, None, start)

    def update(src, dst, rhs, m, start, coef, edge, explicit, store):
        centre = src[m, pl.ds(pad + start, block), :]
        upper = src[m, pl.ds(pad + start - 1, block), :]
        lower = src[m, pl.ds(pad + start + 1, block), :]
        west, east = sides(centre, edge)
        if explicit:
            c0, h0, h1, h2, h3, inverse = coef
            total = c0 * centre + (h0 * upper + h1 * lower) + (h2 * west + h3 * east)
            rhs[m, pl.ds(start, block), :] = total * inverse
        else:
            v0, v1, v2, v3 = coef
            total = rhs[m, pl.ds(start, block), :] + (v0 * upper + v1 * lower)
            total = total + (v2 * west + v3 * east)
        store(m, start, total)

    def sweep(src, dst, ssrc, sdst, explicit, last):
        chosen = range(6) if explicit else range(6, 10)

        def to(ref):
            def store(m, start, value):
                ref[m, pl.ds(pad + start, block), :] = value

            return store

        def to_out(m, start, value):
            out_ref[m, pl.ds(start - HALO, block), :] = value

        @pl.loop(0, groups)
        def _(g):
            for start in starts:
                here = pl.ds(pad + start, block)
                edge_ref[g, pl.ds(start, block), :] = edges_of(
                    ssrc[g, here, :], ssrc[groups + g, here, :]
                )
                for side in (0, 1) if not last else ():
                    coef = [sw_ref[side, i, pl.ds(start, block), :] for i in chosen]
                    update(
                        ssrc, sdst, srhs_ref, side * groups + g, start, coef, None, explicit,
                        to(sdst),
                    )

        @pl.loop(0, groups)
        def _(g):
            for start in range(HALO, HALO + rows, block) if last else starts:
                coef = [w_ref[i, pl.ds(start, block), :] for i in chosen]
                edge = edge_ref[g, pl.ds(start, block), :]
                for q in range(8):
                    rolled = pltpu.roll(edge, (lanes - HALO - SEG * q) % lanes, axis=1)
                    update(
                        src, dst, rhs_ref, 8 * g + q, start, coef, rolled, explicit,
                        to_out if last else to(dst),
                    )

    now, later = (a_ref, sa_ref), (b_ref, sb_ref)
    for step in range(STEPS):
        for stage in range(SWEEPS + 1):
            last = step == STEPS - 1 and stage == SWEEPS
            sweep(now[0], later[0], now[1], later[1], stage == 0, last)
            now, later = later, now


def extract_kernel(owner_share, me_ref, record_ref, state_ref, out_ref, meta_ref):
    members, rows, lanes = state_ref.shape
    ncol, height, _ = record_ref.shape
    fields = FIELDS * BATCH_COUNT
    base = height - fields
    capacity = lanes // ncol
    me = me_ref[1]
    stacked = jnp.concatenate([record_ref[p, base:, :] for p in range(ncol)], axis=0)
    pieces = [
        stacked[i * lanes : (i + 1) * lanes, :].T[0:owner_share]
        for i in range(ncol * fields // lanes)
    ]
    lane = iota((owner_share, lanes), 1)
    square = (owner_share, owner_share)
    triangle = (iota(square, 1) < iota(square, 0)).astype(BF16)
    slot = (lane % capacity).astype(F32)

    def spread(f, k):
        index = (lane // capacity) * fields + f * BATCH_COUNT + k
        out = None
        for i, piece in enumerate(pieces):
            got = jnp.take_along_axis(piece, jnp.clip(index - i * lanes, 0, lanes - 1), axis=1)
            out = got if out is None else jnp.where(index >= i * lanes, got, out)
        return out

    base = BATCH_COUNT * members
    out_ref[base + 3 * BATCH_COUNT :, :] = jnp.zeros((BATCH_COUNT, lanes), F32)
    for k in range(BATCH_COUNT):
        mine = spread(0, k) == me.astype(F32)
        rank = jnp.dot(triangle, mine.astype(BF16), preferred_element_type=F32)
        hot = mine & (rank == slot)

        def slotted(values):
            return jnp.sum(jnp.where(hot, values, 0.0), axis=0, keepdims=True)

        cell = spread(1, k).astype(jnp.int32)
        x = cell // lanes
        error = slotted(spread(3, k))
        taken = error > 0.0
        weight = jnp.where(taken, 1.0 / jnp.where(taken, error, 1.0), 0.0)
        place = slotted((x + 1).astype(F32)) - 1.0
        for n, values in enumerate((weight, slotted(spread(2, k)), place)):
            row = base + n * BATCH_COUNT + k
            out_ref[row : row + 1, :] = values
        meta_ref[k : k + 1, :] = slotted((cell - x * lanes).astype(F32))

    level = iota((8, lanes), 0)
    place = base + 2 * BATCH_COUNT
    for k in range(BATCH_COUNT):
        xs = jnp.broadcast_to(out_ref[place + k : place + k + 1, :], (8, lanes)).astype(jnp.int32)
        ys = jnp.broadcast_to(meta_ref[k : k + 1, :], (8, lanes)).astype(jnp.int32)

        @pl.loop(0, members // 8)
        def _(g):
            totals = []
            for q in range(8):
                total = jnp.zeros((8, lanes), F32)
                for s in range(0, rows, 8):
                    block = state_ref[8 * g + q, pl.ds(s, 8), :]
                    got = jnp.take_along_axis(block, ys, axis=1)
                    total = total + jnp.where(xs == level + s, got, 0.0)
                totals.append(jnp.sum(total, axis=0, keepdims=True))
            row = pl.multiple_of(k * members + 8 * g, 8)
            out_ref[pl.ds(row, 8), :] = jnp.concatenate(totals, axis=0)


def band_sums(ncol, parts):
    lanes = LANES
    mask = (iota((ncol, lanes), 1) // (lanes // ncol) == iota((ncol, lanes), 0)).astype(F32)
    row = iota((8, lanes), 0)
    lefts, rights = [], []
    for z, w, value in parts:
        members = z.shape[0]
        mean = jnp.mean(z, axis=0, keepdims=True)
        anomaly = z - mean
        innov = value - mean
        scaled = anomaly * w

        def masked(values):
            return jnp.concatenate(
                [values[m : m + 1, :] * mask for m in range(members)], axis=0
            ).astype(BF16)

        hi, lo, _ = split3(scaled)
        hi, lo = masked(hi), masked(lo)
        lefts += [hi, lo, hi]
        right = jnp.concatenate([anomaly, jnp.where(row == 0, innov, 0.0)], axis=0)
        hi, lo, _ = split3(right)
        hi, lo = hi.astype(BF16), lo.astype(BF16)
        rights += [hi, hi, lo]
    return nt(jnp.concatenate(rights, axis=1), jnp.concatenate(lefts, axis=1), None)


def seen_rows(seen_refs, p):
    half = seen_refs[0].shape[0]
    return seen_refs[p // half].at[p % half]


def first_kernel(members, low_ref, high_ref, out_ref):
    seen = (low_ref, high_ref)
    ncol = 2 * low_ref.shape[0]
    parts = []
    for p in range(ncol):
        rows = seen_rows(seen, p)
        meta = BATCH_COUNT * members
        parts.append(
            (
                rows[0:members, :],
                rows[meta : meta + 1, :],
                rows[meta + BATCH_COUNT : meta + BATCH_COUNT + 1, :],
            )
        )
    out_ref[...] = band_sums(ncol, parts)


def bands_of(row_strides, me, low_ref, high_ref):
    half = low_ref.shape[0]
    out = []
    for r in range(2 * half):
        at = position_of(jnp.bitwise_xor(me, r), row_strides)
        out.append(
            jnp.where(at < half, low_ref[at % half], high_ref[at % half])
        )
    return out


def spread_sums(bands, spread_ref, ncol):
    height, width = bands[0].shape
    nrow = len(bands)
    members = width // ncol
    devices = nrow * ncol
    lanes = LANES
    lane = iota((height, lanes), 1)
    owner = lane % devices
    which = lane // devices
    per = max(1, lanes // devices)
    for first in range(0, members, per):
        tile, start = divmod(first * ncol, lanes)
        index = start + which * ncol + owner % ncol
        group = None
        for r in range(nrow):
            piece = bands[r][:, tile * lanes : (tile + 1) * lanes]
            got = jnp.take_along_axis(piece, index, axis=1)
            group = got if group is None else jnp.where(owner // ncol == r, got, group)
        for n in range(per):
            m = first + n
            if per > 1:
                value = jnp.take_along_axis(group, n * devices + owner, axis=1)
                hi, mid, lo = split3(value)
                value = jnp.where(which == 0, hi, jnp.where(which == 1, mid, lo))
            else:
                value = jnp.concatenate(split3(group), axis=1)
            spread_ref[pl.ds(m * height, height), :] = value.astype(BF16)


def stacked(scaled):
    devices = scaled.shape[0]
    copies = max(3, LANES // devices)
    return jnp.concatenate([scaled] * 3 + [jnp.zeros_like(scaled)] * (copies - 3), axis=0)


def copies_of(levels):
    return stacked((levels * 0.125).astype(BF16))


def solve_sums(bands, ncol):
    height, width = bands[0].shape
    members = width // ncol
    lanes = LANES
    total = bands[0]
    for band in bands[1:]:
        total = total + band
    pick = (iota((width, lanes), 0) // ncol == iota((width, lanes), 1)).astype(BF16)
    a = sum(
        jnp.dot(part.astype(BF16), pick, preferred_element_type=F32)
        for part in reversed(split3(total))
    )
    row = iota((height, lanes), 0)
    lane = iota((height, lanes), 1)
    a = a + jnp.where((row == lane) & (row < members), members - 1.0, 0.0)
    lane1 = iota((1, lanes), 1)
    block = 8
    for start in range(0, members, block):
        columns = [
            jnp.broadcast_to(a[:, k : k + 1], (height, lanes))
            for k in range(start, start + block)
        ]
        for s in range(block):
            k, column = start + s, columns[s]
            inverse = 1.0 / column[k : k + 1, :]
            scaled = jnp.where(lane1 == k, inverse, a[k : k + 1, :] * inverse)
            a = jnp.where(row == k, scaled, jnp.where(lane == k, 0.0, a) - column * scaled)
            for t in range(s + 1, block):
                part = columns[t][k : k + 1, :] * inverse
                columns[t] = jnp.where(row == k, part, columns[t] - column * part)
    gain = a[members : members + 1, :] * (1.0 / (members - 1))
    out = jnp.where(lane1 < members, -0.5 * a[0:members, :] + gain, 0.0)
    out = jnp.where(lane1 == members, 1.0 / (members - 1), out)
    hi, lo, _ = split3(out)
    deep = height + 8
    stack = jnp.concatenate(
        [hi[:, 0:deep], hi[:, 0:deep], lo[:, 0:deep], jnp.zeros((members, 2 * lanes - 3 * deep), F32)],
        axis=1,
    )
    return stack.astype(BF16)


def product3(stack, right):
    height, width = right.shape
    hi, lo, _ = split3(right)
    zero = jnp.zeros((8, width), F32)
    hi, lo = (jnp.concatenate([part, zero], axis=0).astype(BF16) for part in (hi, lo))
    deep = 3 * (height + 8)
    return jnp.dot(
        stack[:, 0:deep], jnp.concatenate([hi, lo, hi], axis=0), preferred_element_type=F32
    )


def apply_sums(spread, levels, z, height):
    at = jnp.dot(spread, levels, preferred_element_type=F32)
    total = None
    for m in range(z.shape[0]):
        term = at[m * height : (m + 1) * height, :] * z[m : m + 1, :]
        total = term if total is None else total + term
    return total


def levels_kernel(strides, me_ref, record_ref, low_ref, high_ref, *out_refs):
    seen = (low_ref, high_ref)
    ncol, height, lanes = record_ref.shape
    devices = (height - FIELDS * BATCH_COUNT) // BATCH_COUNT
    members = (low_ref.shape[1] - FIELDS * BATCH_COUNT) // BATCH_COUNT
    base = BATCH_COUNT * members + 2 * BATCH_COUNT
    for p in range(ncol):
        offset = sum(((p >> bit) & 1) * stride for bit, stride in enumerate(strides))
        rows = record_ref.at[jnp.bitwise_xor(me_ref[1], offset)]
        at = 0
        for target in range(1, BATCH_COUNT):
            place = seen_rows(seen, p)[base + target : base + target + 1, :]
            hot = (iota((lanes, lanes), 0) == place.astype(jnp.int32)).astype(BF16)
            table = (rows[0 : target * devices, :] * 0.125).astype(BF16)
            found = jnp.dot(table, hot, preferred_element_type=F32)
            for batch in range(target):
                part = found[batch * devices : (batch + 1) * devices, :].astype(BF16)
                out_refs[at][p // 2, :, (p % 2) * lanes : (p % 2 + 1) * lanes] = stacked(part)
                at += 1


def moved(levels_ref, spread, solved, read):
    out = []
    for p in range(levels_ref.shape[0]):
        z = jnp.concatenate([read(2 * p), read(2 * p + 1)], axis=1)
        sums = apply_sums(spread, levels_ref[p], z, z.shape[0] + 8)
        z = z + product3(solved, sums)
        out += [z[:, 0:LANES], z[:, LANES:]]
    return out


def reader(seen, z_ref, members, target):
    if z_ref is not None:
        return lambda i: z_ref[i]
    return lambda i: seen_rows(seen, i)[target * members : (target + 1) * members, :]


def next_kernel(row_strides, batch, *refs):
    me_ref, lows_ref, highs_ref, levels_ref = refs[:4]
    seen = refs[4:6]
    z_ref = refs[6] if batch else None
    out_ref, spread_ref, solved_ref = refs[-3:]
    ncol = 2 * seen[0].shape[0]
    members = solved_ref.shape[0]
    bands = bands_of(row_strides, me_ref[0], lows_ref, highs_ref)
    spread_sums(bands, spread_ref, ncol)
    solved = solve_sums(bands, ncol)
    solved_ref[...] = solved
    target = batch + 1
    zs = moved(levels_ref, spread_ref[...], solved, reader(seen, z_ref, members, target))
    parts = []
    meta = BATCH_COUNT * members + target
    for p in range(ncol):
        rows = seen_rows(seen, p)
        parts.append(
            (
                zs[p],
                rows[meta : meta + 1, :],
                rows[meta + BATCH_COUNT : meta + BATCH_COUNT + 1, :],
            )
        )
    out_ref[...] = band_sums(ncol, parts)


def moved_kernel(target, levels_ref, spread_ref, solved_ref, *refs):
    out_ref = refs[-1]
    z_ref = refs[0] if len(refs) == 2 else None
    read = reader(refs[0:2], z_ref, solved_ref.shape[0], target)
    for p, z in enumerate(moved(levels_ref, spread_ref[...], solved_ref[...], read)):
        out_ref[p] = z


def compose(spread, solved, levels, batch, trans_ref, dst_ref, height):
    members = solved.shape[0]
    at = jnp.dot(spread, levels, preferred_element_type=F32)
    lanes = LANES
    for j in range(0, members, 2):
        sums = []
        for i in (j, j + 1):
            if batch == 0:
                sums.append(at[i * height : (i + 1) * height, :])
            else:
                total = None
                for m in range(members):
                    term = at[m * height : (m + 1) * height, :] * trans_ref[i, m : m + 1, :]
                    total = term if total is None else total + term
                sums.append(total)
        change = product3(solved, jnp.concatenate(sums, axis=1))
        for n, i in enumerate((j, j + 1)):
            part = change[:, n * lanes : (n + 1) * lanes]
            if batch == 0:
                dst_ref[i] = part + (iota((members, lanes), 0) == i).astype(F32)
            else:
                dst_ref[i] = part + trans_ref[i]


def compose_kernel(batches, me_ref, record_ref, *refs):
    given = refs[: 2 * len(batches)]
    trans_ref = refs[2 * len(batches)] if batches[0] else None
    out_ref = refs[-1]
    members = given[1].shape[0]
    devices = (record_ref.shape[1] - FIELDS * BATCH_COUNT) // BATCH_COUNT
    for n, batch in enumerate(batches):
        levels = copies_of(record_ref[me_ref[1], batch * devices : (batch + 1) * devices, :])
        source = trans_ref if n == 0 else out_ref
        compose(
            given[2 * n][...], given[2 * n + 1][...], levels, batch, source, out_ref, members + 8
        )


def split_kernel(state_ref, out_ref):
    members, rows, _ = state_ref.shape

    @pl.loop(0, rows // 8)
    def _(b):
        start = pl.multiple_of(b * 8, 8)
        turned = jnp.swapaxes(state_ref[:, pl.ds(start, 8), :], 0, 1)
        for i in range(8):
            hi, lo, _ = split3(turned[i])
            out_ref[start + i] = jnp.concatenate([hi, lo], axis=0).astype(BF16)


def final_kernel(
    row_strides, me_ref, lows_ref, highs_ref, record_ref, trans_ref, state_ref, out_hbm,
    spread_ref, whole_ref, turned_ref, out_ref, sems,
):
    rows, lanes = state_ref.shape[0], state_ref.shape[2]
    members = state_ref.shape[1] // 2
    height, width = lows_ref.shape[1:]
    ncol = width // members
    devices = 2 * lows_ref.shape[0] * ncol
    batch = BATCH_COUNT - 1
    bands = bands_of(row_strides, me_ref[0], lows_ref, highs_ref)
    spread_sums(bands, spread_ref, ncol)
    solved = solve_sums(bands, ncol)
    levels = copies_of(record_ref[me_ref[1], batch * devices : (batch + 1) * devices, :])
    compose(spread_ref[...], solved, levels, batch, trans_ref, whole_ref, height)
    for i in range(members):
        hi, lo, _ = split3(whole_ref[:, i, :])
        turned_ref[i] = jnp.concatenate([hi, hi, lo, jnp.zeros_like(hi)], axis=0).T

    share = rows // sems.shape[0]
    copies = []
    for c in range(sems.shape[0]):

        @pl.loop(c * share // 8, (c + 1) * share // 8)
        def _(b):
            start = pl.multiple_of(b * 8, 8)
            lefts = jnp.swapaxes(turned_ref[:, pl.ds(start, 8), :], 0, 1).astype(BF16)
            done = []
            for i in range(8):
                both = state_ref[start + i]
                right = jnp.concatenate([both, both[0:members]], axis=0)
                done.append(
                    jnp.dot(lefts[i][:, 0 : 3 * members], right, preferred_element_type=F32)
                )
            out_ref[:, pl.ds(start, 8), :] = jnp.swapaxes(jnp.stack(done), 0, 1)

        part = pl.ds(c * share, share)
        copies.append(
            pltpu.make_async_copy(out_ref.at[:, part, :], out_hbm.at[:, part, :], sems.at[c])
        )
        copies[-1].start()
    for copy in copies:
        copy.wait()


def call(kernel, out_shape, in_specs, scratch=(), limit=48, out_specs=None):
    return pl.pallas_call(
        kernel,
        out_shape=out_shape,
        in_specs=in_specs,
        out_specs=out_specs or jax.tree.map(lambda _: VMEM, out_shape),
        scratch_shapes=list(scratch),
        compiler_params=pltpu.CompilerParams(vmem_limit_bytes=limit * 1024 * 1024),
    )


def body(
    sample_heights, depth, land_sea, batch_order, obs_value, obs_error, obs_tile, obs_cell, loc_level
):
    members, rows, cols = sample_heights.shape
    ncol = lax.axis_size("col")
    nrow = lax.axis_size("row")
    devices = nrow * ncol
    strides, row_strides = strides_of(ncol), strides_of(nrow)
    groups = members // 8
    half = groups // 2
    height = members + 8
    me = jnp.stack([lax.axis_index("row"), lax.axis_index("col")]).astype(jnp.int32)

    def out(*shape, dtype=F32):
        return jax.ShapeDtypeStruct(shape, dtype)

    record_rows = BATCH_COUNT * devices + FIELDS * BATCH_COUNT
    share = obs_cell.shape[1]
    to_right, to_left, record, coef = call(
        prep_kernel,
        (out(half + 1, rows, cols), out(half + 1, rows, cols), out(record_rows, cols), out(2, rows, cols)),
        [ANY] * 9,
        [
            pltpu.VMEM((members, rows, cols), F32),
            pltpu.VMEM((rows, cols), jnp.int32),
            pltpu.VMEM((rows, cols), jnp.int32),
            pltpu.VMEM((BATCH_COUNT, devices, rows), jnp.int32),
            pltpu.VMEM((BATCH_COUNT, share), jnp.int32),
            pltpu.VMEM((BATCH_COUNT, share), jnp.int32),
            pltpu.VMEM((BATCH_COUNT, share), F32),
            pltpu.VMEM((BATCH_COUNT, share), F32),
            pltpu.SMEM((BATCH_COUNT,), jnp.int32),
            pltpu.SemaphoreType.DMA((8 + groups,)),
        ],
        limit=58,
    )(
        sample_heights, depth, land_sea, jnp.transpose(loc_level[:, :, 0, :], (0, 2, 1)), obs_tile[:, :, 0], obs_cell,
        obs_value, obs_error, batch_order,
    )
    left, right = shift_pair(to_left, to_right, "col")

    def slab(start):
        cut = lambda a: lax.slice_in_dim(a, start, start + HALO, axis=1)
        return jnp.concatenate([cut(a) for a in (sample_heights, coef, left, right)], axis=0)

    up, down = shift_pair(slab(0), slab(rows - HALO), "row")
    records = lax.all_to_all(
        jnp.broadcast_to(record, (ncol, *record.shape)), "col", split_axis=0, concat_axis=0, tiled=True
    )

    ext = rows + 2 * HALO
    tall = ext + 2 * HALO
    state = call(
        forecast_kernel,
        out(members, rows, cols),
        [VMEM] * 6,
        [
            pltpu.VMEM((members, tall, cols), F32),
            pltpu.VMEM((members, tall, cols), F32),
            pltpu.VMEM((members, ext, cols), F32),
            pltpu.VMEM((2 * groups, tall, cols), F32),
            pltpu.VMEM((2 * groups, tall, cols), F32),
            pltpu.VMEM((2 * groups, ext, cols), F32),
            pltpu.VMEM((2, tall, cols), F32),
            pltpu.VMEM((4, tall, cols), F32),
            pltpu.VMEM((10, ext, cols), F32),
            pltpu.VMEM((2, 10, ext, cols), F32),
            pltpu.VMEM((groups, ext, cols), F32),
        ],
    )(sample_heights, coef, left, right, up, down)
    mine = call(
        functools.partial(extract_kernel, share),
        out(BATCH_COUNT * members + FIELDS * BATCH_COUNT, cols),
        [SMEM, VMEM, VMEM],
        [pltpu.VMEM((8, cols), F32)],
    )(me, records, state)
    seen, _, _ = gather_over(mine, "col")
    parts = call(split_kernel, out(rows, 2 * members, cols, dtype=BF16), [VMEM])(state)

    sums = call(
        functools.partial(first_kernel, members), out(height, members * ncol), [VMEM] * 2
    )(*seen)
    wide = max(LANES, 3 * devices)

    def compose_of(batches, given, trans):
        args = (me, records, *given) + (() if trans is None else (trans,))
        return call(
            functools.partial(compose_kernel, batches),
            out(members, members, cols),
            [SMEM] + [VMEM] * (len(args) - 1),
        )(*args)

    def moved_of(batch, target, given, z):
        args = (levels[(batch, target)], *given) + (seen if z is None else (z,))
        return call(
            functools.partial(moved_kernel, target),
            out(ncol, members, cols),
            [VMEM] * len(args),
        )(*args)

    def next_of(batch, every, z):
        args = (me, *every, levels[(batch, batch + 1)], *seen) + (() if z is None else (z,))
        got = call(
            functools.partial(next_kernel, row_strides, batch),
            (
                out(height, members * ncol),
                out(members * height, wide, dtype=BF16),
                out(members, 2 * LANES, dtype=BF16),
            ),
            [SMEM] + [VMEM] * (len(args) - 1),
        )(*args)
        return got[0], got[1:]

    pairs = [(b, k) for k in range(1, BATCH_COUNT) for b in range(k)]
    found = call(
        functools.partial(levels_kernel, strides),
        tuple(out(ncol // 2, wide, 2 * LANES, dtype=BF16) for _ in pairs),
        [SMEM] + [VMEM] * 3,
    )(me, records, *seen)
    every, (found, parts), _ = gather_over(sums, "row", (found, parts))
    levels = dict(zip(pairs, found))
    sums, first = next_of(0, every, None)
    every, z2, trans = gather_over(
        sums, "row", moved_of(0, 2, first, None), compose_of((0,), first, None)
    )
    sums, second = next_of(1, every, z2)
    z3 = moved_of(0, 3, first, None)
    every, z3, z3_late = gather_over(sums, "row", z3, moved_of(1, 3, second, z3))
    sums, third = next_of(2, every, z3_late)
    trans = compose_of((1,), second, trans)
    every, _, trans = gather_over(sums, "row", trans, compose_of((2,), third, trans))
    return call(
        functools.partial(final_kernel, row_strides),
        out(members, rows, cols),
        [SMEM] + [VMEM] * 5,
        [
            pltpu.VMEM((members * height, wide), BF16),
            pltpu.VMEM((members, members, cols), F32),
            pltpu.VMEM((members, rows, cols), F32),
            pltpu.VMEM((members, rows, cols), F32),
            pltpu.SemaphoreType.DMA((4,)),
        ],
        out_specs=ANY,
    )(me, *every, records, trans, parts)


def solution(mesh):
    return jax.shard_map(
        body,
        mesh=mesh,
        in_specs=(
            P(None, "row", "col"),
            P("row", "col"),
            P("row", "col"),
            P(),
            P(None, ("row", "col")),
            P(None, ("row", "col")),
            P(None, ("row", "col"), None),
            P(None, ("row", "col")),
            P(None, "row", "col", None),
        ),
        out_specs=P(None, "row", "col"),
        check_vma=False,
    )
```

```python
import functools

import jax
import jax.numpy as jnp
from jax import lax
from jax.experimental import pallas as pl
from jax.experimental.pallas import tpu as pltpu
from jax.sharding import PartitionSpec as P

BATCH_COUNT = 4
STEPS = 2
SWEEPS = 2
HALO = 8
SEG = 2 * HALO
LANES = 128
FIELDS = 4
HIGH = lax.Precision.HIGHEST
F32 = jnp.float32
BF16 = jnp.bfloat16
SMEM = pl.BlockSpec(memory_space=pltpu.SMEM)
VMEM = pl.BlockSpec(memory_space=pltpu.VMEM)
ANY = pl.BlockSpec(memory_space=pl.ANY)


def iota(shape, dim):
    return lax.broadcasted_iota(jnp.int32, shape, dim)


def strides_of(n):
    out = []
    while n > 1:
        n //= 2
        out.append(n)
    return out


def offset_at(position, strides):
    out = position * 0
    for bit, stride in enumerate(strides):
        out = out + ((position >> bit) & 1) * stride
    return out


def position_of(offset, strides):
    out = offset * 0
    for bit, stride in enumerate(strides):
        out = out + ((offset // stride) & 1) * (1 << bit)
    return out


def gather_over(block, axis, early=(), late=()):
    n = lax.axis_size(axis)
    held = block[None]
    strides = strides_of(n)
    for stride in strides:
        if stride == strides[-1]:
            held, early = lax.optimization_barrier((held, early))
        other = lax.ppermute(held, axis, [(i, i ^ stride) for i in range(n)])
        if stride != strides[-1]:
            held = jnp.concatenate([held, other], axis=0)
    other, late = lax.optimization_barrier((other, late))
    return (held, other), early, late


def shift_pair(low_send, high_send, axis):
    n = lax.axis_size(axis)
    forward = [(i, i + 1) for i in range(n - 1)]
    backward = [(b, a) for a, b in forward]
    return lax.ppermute(high_send, axis, forward), lax.ppermute(low_send, axis, backward)


def nt(a, b, precision=HIGH):
    return lax.dot_general(
        a, b, (((1,), (1,)), ((), ())), precision=precision, preferred_element_type=F32
    )


def split3(x):
    hi = x.astype(BF16).astype(F32)
    rest = x - hi
    mid = rest.astype(BF16).astype(F32)
    return hi, mid, rest - mid


def prep_kernel(
    h_hbm, depth_hbm, sea_hbm, loc_hbm, tile_hbm, cell_hbm, val_hbm, err_hbm, order_hbm,
    to_right_ref, to_left_ref, record_ref, coef_ref,
    h_ref, depth_ref, sea_ref, loc_ref, tile_ref, cell_ref, val_ref, err_ref, order_ref, sems,
):
    members, rows, lanes = h_ref.shape
    groups = members // 8
    half = groups // 2
    pairs = (
        (order_hbm, order_ref),
        (tile_hbm, tile_ref),
        (cell_hbm, cell_ref),
        (val_hbm, val_ref),
        (err_hbm, err_ref),
        (loc_hbm, loc_ref),
        (depth_hbm, depth_ref),
        (sea_hbm, sea_ref),
    )
    small = [
        pltpu.make_async_copy(source, target, sems.at[i])
        for i, (source, target) in enumerate(pairs)
    ]
    large = [
        pltpu.make_async_copy(
            h_hbm.at[pl.ds(8 * g, 8)], h_ref.at[pl.ds(8 * g, 8)], sems.at[len(pairs) + g]
        )
        for g in range(groups)
    ]
    for copy in small + large:
        copy.start()
    seg = iota((rows, lanes), 1) // SEG
    first = iota((rows, lanes), 1) % SEG < HALO
    for copy in small[:6]:
        copy.wait()

    devices = loc_ref.shape[1]
    base = BATCH_COUNT * devices
    fields = FIELDS * BATCH_COUNT
    width = val_ref.shape[1]
    record_ref[base:, :] = jnp.zeros((fields, lanes), F32)
    for k in range(BATCH_COUNT):
        batch = order_ref[k]
        record_ref[k * devices : (k + 1) * devices, :] = loc_ref[batch].astype(F32)
        for f, ref in enumerate((tile_ref, cell_ref, val_ref, err_ref)):
            row = base + f * BATCH_COUNT + k
            record_ref[row : row + 1, 0:width] = ref[pl.ds(batch, 1), :].astype(F32)

    for copy in small[6:]:
        copy.wait()
    sea = sea_ref[...].astype(F32)
    kappa = 0.01 * depth_ref[...].astype(F32) * sea
    coef_ref[0] = kappa
    coef_ref[1] = sea

    def pack(pick):
        out = None
        for q in range(8):
            rolled = pltpu.roll(pick(q), q * SEG + HALO, axis=1)
            out = rolled if out is None else jnp.where(seg == q, rolled, out)
        return out

    def send(g, a, b):
        to_right_ref[g] = jnp.where(first, a, pltpu.roll(b, HALO, axis=1))
        to_left_ref[g] = jnp.where(first, pltpu.roll(b, lanes - HALO, axis=1), a)

    send(half, pack(lambda q: kappa), pack(lambda q: sea))
    for copy in large:
        copy.wait()
    for g in range(half):
        send(g, pack(lambda q: h_ref[8 * g + q]), pack(lambda q: h_ref[8 * (g + half) + q]))


def strip_pair(pick, incoming, second):
    values = [pick(q) for q in range(8)]
    shape = values[0].shape
    lanes = shape[1]
    seg = iota(shape, 1) // SEG
    first = iota(shape, 1) % SEG < HALO
    own = None
    for q in range(8):
        rolled = pltpu.roll(values[q], q * SEG + HALO, axis=1)
        own = rolled if own is None else jnp.where(seg == q, rolled, own)
    from_left, from_right = incoming(0), incoming(1)
    if second:
        from_left = pltpu.roll(from_left, lanes - HALO, axis=1)
        from_right = pltpu.roll(from_right, HALO, axis=1)
    return jnp.where(first, from_left, own), jnp.where(first, own, from_right)


def strips_kernel(h_ref, coef_ref, left_ref, right_ref, out_ref, out_k_ref, held_ref):
    members, rows, lanes = h_ref.shape
    groups = members // 8
    half = groups // 2
    block = 32

    @pl.loop(0, members)
    def _(m):
        held_ref[m] = h_ref[m]

    @pl.loop(0, rows // block)
    def _(b):
        here = pl.ds(pl.multiple_of(b * block, block), block)
        for i in range(2):
            out_k_ref[2 * i, here, :], out_k_ref[2 * i + 1, here, :] = strip_pair(
                lambda q: coef_ref[i, here, :],
                lambda w: (left_ref, right_ref)[w][half, here, :],
                i == 1,
            )
        for g in range(groups):
            out_ref[g, here, :], out_ref[groups + g, here, :] = strip_pair(
                lambda q: h_ref[8 * g + q, here, :],
                lambda w: (left_ref, right_ref)[w][g % half, here, :],
                g >= half,
            )


def forecast_kernel(
    h_ref, coef_ref, own_ref, own_k_ref, up_ref, down_ref, out_ref,
    a_ref, b_ref, rhs_ref, sa_ref, sb_ref, srhs_ref, k_ref, sk_ref, w_ref, sw_ref, edge_ref,
):
    members, rows, lanes = out_ref.shape
    groups = members // 8
    half = groups // 2
    ext = rows + 2 * HALO
    pad = HALO
    inner = pad + HALO
    block = 16
    starts = list(range(0, ext, block))

    for ref in (k_ref, sk_ref):
        for i in range(ref.shape[0]):
            ref[i, pl.ds(0, pad), :] = jnp.zeros((pad, lanes), F32)
            ref[i, pl.ds(pad + ext, pad), :] = jnp.zeros((pad, lanes), F32)
    for i in range(2):
        k_ref[i, pl.ds(pad, HALO), :] = up_ref[members + i]
        k_ref[i, pl.ds(inner, rows), :] = coef_ref[i]
        k_ref[i, pl.ds(inner + rows, HALO), :] = down_ref[members + i]

    @pl.loop(0, members)
    def _(m):
        a_ref[m, pl.ds(pad, HALO), :] = up_ref[m]
        a_ref[m, pl.ds(inner, rows), :] = h_ref[m]
        a_ref[m, pl.ds(inner + rows, HALO), :] = down_ref[m]

    for ref, start in ((up_ref, pad), (down_ref, inner + rows)):
        here = pl.ds(start, HALO)
        for i in range(2):
            sk_ref[2 * i, here, :], sk_ref[2 * i + 1, here, :] = strip_pair(
                lambda q: ref[members + i],
                lambda w: ref[members + 2 + w * (half + 1) + half],
                i == 1,
            )
        for g in range(groups):
            sa_ref[g, here, :], sa_ref[groups + g, here, :] = strip_pair(
                lambda q: ref[8 * g + q],
                lambda w: ref[members + 2 + w * (half + 1) + g % half],
                g >= half,
            )
    for i in range(4):
        sk_ref[i, pl.ds(inner, rows), :] = own_k_ref[i]
    for i in range(2 * groups):
        sa_ref[i, pl.ds(inner, rows), :] = own_ref[i]

    lane = iota((block, lanes), 1)
    is_last = lane == lanes - 1
    is_first = lane == 0
    at_seven = lane % SEG == HALO - 1

    def sides(centre, edge):
        if edge is None:
            return pltpu.roll(centre, 1, axis=1), pltpu.roll(centre, lanes - 1, axis=1)
        return (
            jnp.where(is_first, edge, pltpu.roll(centre, 1, axis=1)),
            jnp.where(is_last, edge, pltpu.roll(centre, lanes - 1, axis=1)),
        )

    def edges_of(low, high):
        return jnp.where(
            at_seven, pltpu.roll(high, lanes - 1, axis=1), pltpu.roll(low, 1, axis=1)
        )

    def weights(ref, at, kap, sea, edges, start):
        here = pl.ds(pad + start, block)

        def four(src, i, edge):
            centre = src[i, here, :]
            return centre, [
                src[i, pl.ds(pad + start - 1, block), :],
                src[i, pl.ds(pad + start + 1, block), :],
                *sides(centre, edge),
            ]

        src = k_ref if edges is not None else sk_ref
        kc, kn = four(src, kap, None if edges is None else edges[0])
        sc, sn = four(src, sea, None if edges is None else edges[1])
        w = [0.5 * (kc + kn[i]) * sc * sn[i] for i in range(4)]
        wsum = w[0] + w[1] + w[2] + w[3]
        inverse = 1.0 / (1.0 + 0.5 * wsum)
        values = [1.0 - 0.5 * wsum] + [0.5 * v for v in w]
        values += [inverse] + [0.5 * v * inverse for v in w]
        for i, value in enumerate(values):
            if at is None:
                ref[i, pl.ds(start, block), :] = value
            else:
                ref[at, i, pl.ds(start, block), :] = value

    for start in starts:
        here = pl.ds(pad + start, block)
        edges = [
            pltpu.roll(
                edges_of(sk_ref[2 * i, here, :], sk_ref[2 * i + 1, here, :]), lanes - HALO, axis=1
            )
            for i in range(2)
        ]
        weights(w_ref, None, 0, 1, edges, start)
        weights(sw_ref, 0, 0, 2, None, start)
        weights(sw_ref, 1, 1, 3, None, start)

    def update(src, dst, rhs, m, start, coef, edge, explicit, store):
        centre = src[m, pl.ds(pad + start, block), :]
        upper = src[m, pl.ds(pad + start - 1, block), :]
        lower = src[m, pl.ds(pad + start + 1, block), :]
        west, east = sides(centre, edge)
        if explicit:
            c0, h0, h1, h2, h3, inverse = coef
            total = c0 * centre + (h0 * upper + h1 * lower) + (h2 * west + h3 * east)
            rhs[m, pl.ds(start, block), :] = total * inverse
        else:
            v0, v1, v2, v3 = coef
            total = rhs[m, pl.ds(start, block), :] + (v0 * upper + v1 * lower)
            total = total + (v2 * west + v3 * east)
        store(m, start, total)

    def sweep(src, dst, ssrc, sdst, explicit, last):
        chosen = range(6) if explicit else range(6, 10)

        def to(ref):
            def store(m, start, value):
                ref[m, pl.ds(pad + start, block), :] = value

            return store

        def to_out(m, start, value):
            out_ref[m, pl.ds(start - HALO, block), :] = value

        @pl.loop(0, groups)
        def _(g):
            for start in starts:
                here = pl.ds(pad + start, block)
                edge_ref[g, pl.ds(start, block), :] = edges_of(
                    ssrc[g, here, :], ssrc[groups + g, here, :]
                )
                for side in (0, 1) if not last else ():
                    coef = [sw_ref[side, i, pl.ds(start, block), :] for i in chosen]
                    update(
                        ssrc, sdst, srhs_ref, side * groups + g, start, coef, None, explicit,
                        to(sdst),
                    )

        @pl.loop(0, groups)
        def _(g):
            for start in range(HALO, HALO + rows, block) if last else starts:
                coef = [w_ref[i, pl.ds(start, block), :] for i in chosen]
                edge = edge_ref[g, pl.ds(start, block), :]
                for q in range(8):
                    rolled = pltpu.roll(edge, (lanes - HALO - SEG * q) % lanes, axis=1)
                    update(
                        src, dst, rhs_ref, 8 * g + q, start, coef, rolled, explicit,
                        to_out if last else to(dst),
                    )

    now, later = (a_ref, sa_ref), (b_ref, sb_ref)
    for step in range(STEPS):
        for stage in range(SWEEPS + 1):
            last = step == STEPS - 1 and stage == SWEEPS
            sweep(now[0], later[0], now[1], later[1], stage == 0, last)
            now, later = later, now


def extract_kernel(owner_share, me_ref, record_ref, state_ref, out_ref, meta_ref):
    members, rows, lanes = state_ref.shape
    ncol, height, _ = record_ref.shape
    fields = FIELDS * BATCH_COUNT
    base = height - fields
    capacity = lanes // ncol
    me = me_ref[1]
    stacked = jnp.concatenate([record_ref[p, base:, :] for p in range(ncol)], axis=0)
    pieces = [
        stacked[i * lanes : (i + 1) * lanes, :].T[0:owner_share]
        for i in range(ncol * fields // lanes)
    ]
    lane = iota((owner_share, lanes), 1)
    square = (owner_share, owner_share)
    triangle = (iota(square, 1) < iota(square, 0)).astype(BF16)
    slot = (lane % capacity).astype(F32)

    def spread(f, k):
        index = (lane // capacity) * fields + f * BATCH_COUNT + k
        out = None
        for i, piece in enumerate(pieces):
            got = jnp.take_along_axis(piece, jnp.clip(index - i * lanes, 0, lanes - 1), axis=1)
            out = got if out is None else jnp.where(index >= i * lanes, got, out)
        return out

    base = BATCH_COUNT * members
    out_ref[base + 3 * BATCH_COUNT :, :] = jnp.zeros((BATCH_COUNT, lanes), F32)
    for k in range(BATCH_COUNT):
        mine = spread(0, k) == me.astype(F32)
        rank = jnp.dot(triangle, mine.astype(BF16), preferred_element_type=F32)
        hot = mine & (rank == slot)

        def slotted(values):
            return jnp.sum(jnp.where(hot, values, 0.0), axis=0, keepdims=True)

        cell = spread(1, k).astype(jnp.int32)
        x = cell // lanes
        error = slotted(spread(3, k))
        taken = error > 0.0
        weight = jnp.where(taken, 1.0 / jnp.where(taken, error, 1.0), 0.0)
        place = slotted((x + 1).astype(F32)) - 1.0
        for n, values in enumerate((weight, slotted(spread(2, k)), place)):
            row = base + n * BATCH_COUNT + k
            out_ref[row : row + 1, :] = values
        meta_ref[k : k + 1, :] = slotted((cell - x * lanes).astype(F32))

    level = iota((8, lanes), 0)
    place = base + 2 * BATCH_COUNT
    for k in range(BATCH_COUNT):
        xs = jnp.broadcast_to(out_ref[place + k : place + k + 1, :], (8, lanes)).astype(jnp.int32)
        ys = jnp.broadcast_to(meta_ref[k : k + 1, :], (8, lanes)).astype(jnp.int32)

        @pl.loop(0, members // 8)
        def _(g):
            totals = []
            for q in range(8):
                total = jnp.zeros((8, lanes), F32)
                for s in range(0, rows, 8):
                    block = state_ref[8 * g + q, pl.ds(s, 8), :]
                    got = jnp.take_along_axis(block, ys, axis=1)
                    total = total + jnp.where(xs == level + s, got, 0.0)
                totals.append(jnp.sum(total, axis=0, keepdims=True))
            row = pl.multiple_of(k * members + 8 * g, 8)
            out_ref[pl.ds(row, 8), :] = jnp.concatenate(totals, axis=0)


def band_sums(ncol, parts):
    lanes = LANES
    mask = (iota((ncol, lanes), 1) // (lanes // ncol) == iota((ncol, lanes), 0)).astype(F32)
    row = iota((8, lanes), 0)
    lefts, rights = [], []
    for z, w, value in parts:
        members = z.shape[0]
        mean = jnp.mean(z, axis=0, keepdims=True)
        anomaly = z - mean
        innov = value - mean
        scaled = anomaly * w

        def masked(values):
            return jnp.concatenate(
                [values[m : m + 1, :] * mask for m in range(members)], axis=0
            ).astype(BF16)

        hi, lo, _ = split3(scaled)
        hi, lo = masked(hi), masked(lo)
        lefts += [hi, lo, hi]
        right = jnp.concatenate([anomaly, jnp.where(row == 0, innov, 0.0)], axis=0)
        hi, lo, _ = split3(right)
        hi, lo = hi.astype(BF16), lo.astype(BF16)
        rights += [hi, hi, lo]
    return nt(jnp.concatenate(rights, axis=1), jnp.concatenate(lefts, axis=1), None)


def seen_rows(seen_refs, p):
    half = seen_refs[0].shape[0]
    return seen_refs[p // half].at[p % half]


def first_kernel(members, low_ref, high_ref, out_ref):
    seen = (low_ref, high_ref)
    ncol = 2 * low_ref.shape[0]
    parts = []
    for p in range(ncol):
        rows = seen_rows(seen, p)
        meta = BATCH_COUNT * members
        parts.append(
            (
                rows[0:members, :],
                rows[meta : meta + 1, :],
                rows[meta + BATCH_COUNT : meta + BATCH_COUNT + 1, :],
            )
        )
    out_ref[...] = band_sums(ncol, parts)


def bands_of(row_strides, me, low_ref, high_ref):
    half = low_ref.shape[0]
    out = []
    for r in range(2 * half):
        at = position_of(jnp.bitwise_xor(me, r), row_strides)
        out.append(
            jnp.where(at < half, low_ref[at % half], high_ref[at % half])
        )
    return out


def spread_sums(bands, spread_ref, ncol):
    height, width = bands[0].shape
    nrow = len(bands)
    members = width // ncol
    devices = nrow * ncol
    lanes = LANES
    lane = iota((height, lanes), 1)
    owner = lane % devices
    which = lane // devices
    per = max(1, lanes // devices)
    for first in range(0, members, per):
        tile, start = divmod(first * ncol, lanes)
        index = start + which * ncol + owner % ncol
        group = None
        for r in range(nrow):
            piece = bands[r][:, tile * lanes : (tile + 1) * lanes]
            got = jnp.take_along_axis(piece, index, axis=1)
            group = got if group is None else jnp.where(owner // ncol == r, got, group)
        for n in range(per):
            m = first + n
            if per > 1:
                value = jnp.take_along_axis(group, n * devices + owner, axis=1)
                hi, mid, lo = split3(value)
                value = jnp.where(which == 0, hi, jnp.where(which == 1, mid, lo))
            else:
                value = jnp.concatenate(split3(group), axis=1)
            spread_ref[pl.ds(m * height, height), :] = value.astype(BF16)


def stacked(scaled):
    devices = scaled.shape[0]
    copies = max(3, LANES // devices)
    return jnp.concatenate([scaled] * 3 + [jnp.zeros_like(scaled)] * (copies - 3), axis=0)


def copies_of(levels):
    return stacked((levels * 0.125).astype(BF16))


def solve_sums(bands, ncol):
    height, width = bands[0].shape
    members = width // ncol
    lanes = LANES
    total = bands[0]
    for band in bands[1:]:
        total = total + band
    pick = (iota((width, lanes), 0) // ncol == iota((width, lanes), 1)).astype(BF16)
    a = sum(
        jnp.dot(part.astype(BF16), pick, preferred_element_type=F32)
        for part in reversed(split3(total))
    )
    row = iota((height, lanes), 0)
    lane = iota((height, lanes), 1)
    a = a + jnp.where((row == lane) & (row < members), members - 1.0, 0.0)
    lane1 = iota((1, lanes), 1)
    block = 8
    for start in range(0, members, block):
        columns = [
            jnp.broadcast_to(a[:, k : k + 1], (height, lanes))
            for k in range(start, start + block)
        ]
        for s in range(block):
            k, column = start + s, columns[s]
            inverse = 1.0 / column[k : k + 1, :]
            scaled = jnp.where(lane1 == k, inverse, a[k : k + 1, :] * inverse)
            a = jnp.where(row == k, scaled, jnp.where(lane == k, 0.0, a) - column * scaled)
            for t in range(s + 1, block):
                part = columns[t][k : k + 1, :] * inverse
                columns[t] = jnp.where(row == k, part, columns[t] - column * part)
    gain = a[members : members + 1, :] * (1.0 / (members - 1))
    out = jnp.where(lane1 < members, -0.5 * a[0:members, :] + gain, 0.0)
    out = jnp.where(lane1 == members, 1.0 / (members - 1), out)
    hi, lo, _ = split3(out)
    deep = height + 8
    stack = jnp.concatenate(
        [hi[:, 0:deep], hi[:, 0:deep], lo[:, 0:deep], jnp.zeros((members, 2 * lanes - 3 * deep), F32)],
        axis=1,
    )
    return stack.astype(BF16)


def product3(stack, right):
    height, width = right.shape
    hi, lo, _ = split3(right)
    zero = jnp.zeros((8, width), F32)
    hi, lo = (jnp.concatenate([part, zero], axis=0).astype(BF16) for part in (hi, lo))
    deep = 3 * (height + 8)
    return jnp.dot(
        stack[:, 0:deep], jnp.concatenate([hi, lo, hi], axis=0), preferred_element_type=F32
    )


def apply_sums(spread, levels, z, height):
    at = jnp.dot(spread, levels, preferred_element_type=F32)
    total = None
    for m in range(z.shape[0]):
        term = at[m * height : (m + 1) * height, :] * z[m : m + 1, :]
        total = term if total is None else total + term
    return total


def levels_kernel(strides, me_ref, record_ref, low_ref, high_ref, *out_refs):
    seen = (low_ref, high_ref)
    ncol, height, lanes = record_ref.shape
    devices = (height - FIELDS * BATCH_COUNT) // BATCH_COUNT
    members = (low_ref.shape[1] - FIELDS * BATCH_COUNT) // BATCH_COUNT
    base = BATCH_COUNT * members + 2 * BATCH_COUNT
    for p in range(ncol):
        offset = sum(((p >> bit) & 1) * stride for bit, stride in enumerate(strides))
        rows = record_ref.at[jnp.bitwise_xor(me_ref[1], offset)]
        at = 0
        for target in range(1, BATCH_COUNT):
            place = seen_rows(seen, p)[base + target : base + target + 1, :]
            hot = (iota((lanes, lanes), 0) == place.astype(jnp.int32)).astype(BF16)
            table = (rows[0 : target * devices, :] * 0.125).astype(BF16)
            found = jnp.dot(table, hot, preferred_element_type=F32)
            for batch in range(target):
                part = found[batch * devices : (batch + 1) * devices, :].astype(BF16)
                out_refs[at][p // 2, :, (p % 2) * lanes : (p % 2 + 1) * lanes] = stacked(part)
                at += 1


def moved(levels_ref, spread, solved, read):
    out = []
    for p in range(levels_ref.shape[0]):
        z = jnp.concatenate([read(2 * p), read(2 * p + 1)], axis=1)
        sums = apply_sums(spread, levels_ref[p], z, z.shape[0] + 8)
        z = z + product3(solved, sums)
        out += [z[:, 0:LANES], z[:, LANES:]]
    return out


def reader(seen, z_ref, members, target):
    if z_ref is not None:
        return lambda i: z_ref[i]
    return lambda i: seen_rows(seen, i)[target * members : (target + 1) * members, :]


def next_kernel(row_strides, batch, *refs):
    me_ref, lows_ref, highs_ref, levels_ref = refs[:4]
    seen = refs[4:6]
    z_ref = refs[6] if batch else None
    out_ref, spread_ref, solved_ref = refs[-3:]
    ncol = 2 * seen[0].shape[0]
    members = solved_ref.shape[0]
    bands = bands_of(row_strides, me_ref[0], lows_ref, highs_ref)
    spread_sums(bands, spread_ref, ncol)
    solved = solve_sums(bands, ncol)
    solved_ref[...] = solved
    target = batch + 1
    zs = moved(levels_ref, spread_ref[...], solved, reader(seen, z_ref, members, target))
    parts = []
    meta = BATCH_COUNT * members + target
    for p in range(ncol):
        rows = seen_rows(seen, p)
        parts.append(
            (
                zs[p],
                rows[meta : meta + 1, :],
                rows[meta + BATCH_COUNT : meta + BATCH_COUNT + 1, :],
            )
        )
    out_ref[...] = band_sums(ncol, parts)


def moved_kernel(target, levels_ref, spread_ref, solved_ref, *refs):
    out_ref = refs[-1]
    z_ref = refs[0] if len(refs) == 2 else None
    read = reader(refs[0:2], z_ref, solved_ref.shape[0], target)
    for p, z in enumerate(moved(levels_ref, spread_ref[...], solved_ref[...], read)):
        out_ref[p] = z


def compose(spread, solved, levels, batch, trans_ref, dst_ref, height):
    members = solved.shape[0]
    at = jnp.dot(spread, levels, preferred_element_type=F32)
    lanes = LANES
    for j in range(0, members, 2):
        sums = []
        for i in (j, j + 1):
            if batch == 0:
                sums.append(at[i * height : (i + 1) * height, :])
            else:
                total = None
                for m in range(members):
                    term = at[m * height : (m + 1) * height, :] * trans_ref[i, m : m + 1, :]
                    total = term if total is None else total + term
                sums.append(total)
        change = product3(solved, jnp.concatenate(sums, axis=1))
        for n, i in enumerate((j, j + 1)):
            part = change[:, n * lanes : (n + 1) * lanes]
            if batch == 0:
                dst_ref[i] = part + (iota((members, lanes), 0) == i).astype(F32)
            else:
                dst_ref[i] = part + trans_ref[i]


def compose_kernel(batches, me_ref, record_ref, *refs):
    given = refs[: 2 * len(batches)]
    trans_ref = refs[2 * len(batches)] if batches[0] else None
    out_ref = refs[-1]
    members = given[1].shape[0]
    devices = (record_ref.shape[1] - FIELDS * BATCH_COUNT) // BATCH_COUNT
    for n, batch in enumerate(batches):
        levels = copies_of(record_ref[me_ref[1], batch * devices : (batch + 1) * devices, :])
        source = trans_ref if n == 0 else out_ref
        compose(
            given[2 * n][...], given[2 * n + 1][...], levels, batch, source, out_ref, members + 8
        )


def split_kernel(state_ref, out_ref):
    members, rows, _ = state_ref.shape

    @pl.loop(0, rows // 8)
    def _(b):
        start = pl.multiple_of(b * 8, 8)
        turned = jnp.swapaxes(state_ref[:, pl.ds(start, 8), :], 0, 1)
        for i in range(8):
            hi, lo, _ = split3(turned[i])
            out_ref[start + i] = jnp.concatenate([hi, lo], axis=0).astype(BF16)


def final_kernel(
    row_strides, me_ref, lows_ref, highs_ref, record_ref, trans_ref, state_ref, out_hbm,
    spread_ref, whole_ref, turned_ref, out_ref, sems,
):
    rows, lanes = state_ref.shape[0], state_ref.shape[2]
    members = state_ref.shape[1] // 2
    height, width = lows_ref.shape[1:]
    ncol = width // members
    devices = 2 * lows_ref.shape[0] * ncol
    batch = BATCH_COUNT - 1
    bands = bands_of(row_strides, me_ref[0], lows_ref, highs_ref)
    spread_sums(bands, spread_ref, ncol)
    solved = solve_sums(bands, ncol)
    levels = copies_of(record_ref[me_ref[1], batch * devices : (batch + 1) * devices, :])
    compose(spread_ref[...], solved, levels, batch, trans_ref, whole_ref, height)
    for i in range(members):
        hi, lo, _ = split3(whole_ref[:, i, :])
        turned_ref[i] = jnp.concatenate([hi, hi, lo, jnp.zeros_like(hi)], axis=0).T

    share = rows // sems.shape[0]
    copies = []
    for c in range(sems.shape[0]):

        @pl.loop(c * share // 8, (c + 1) * share // 8)
        def _(b):
            start = pl.multiple_of(b * 8, 8)
            lefts = jnp.swapaxes(turned_ref[:, pl.ds(start, 8), :], 0, 1).astype(BF16)
            done = []
            for i in range(8):
                both = state_ref[start + i]
                right = jnp.concatenate([both, both[0:members]], axis=0)
                done.append(
                    jnp.dot(lefts[i][:, 0 : 3 * members], right, preferred_element_type=F32)
                )
            out_ref[:, pl.ds(start, 8), :] = jnp.swapaxes(jnp.stack(done), 0, 1)

        part = pl.ds(c * share, share)
        copies.append(
            pltpu.make_async_copy(out_ref.at[:, part, :], out_hbm.at[:, part, :], sems.at[c])
        )
        copies[-1].start()
    for copy in copies:
        copy.wait()


def call(kernel, out_shape, in_specs, scratch=(), limit=48, out_specs=None):
    return pl.pallas_call(
        kernel,
        out_shape=out_shape,
        in_specs=in_specs,
        out_specs=out_specs or jax.tree.map(lambda _: VMEM, out_shape),
        scratch_shapes=list(scratch),
        compiler_params=pltpu.CompilerParams(vmem_limit_bytes=limit * 1024 * 1024),
    )


def body(
    sample_heights, depth, land_sea, batch_order, obs_value, obs_error, obs_tile, obs_cell, loc_level
):
    members, rows, cols = sample_heights.shape
    ncol = lax.axis_size("col")
    nrow = lax.axis_size("row")
    devices = nrow * ncol
    strides, row_strides = strides_of(ncol), strides_of(nrow)
    groups = members // 8
    half = groups // 2
    height = members + 8
    me = jnp.stack([lax.axis_index("row"), lax.axis_index("col")]).astype(jnp.int32)

    def out(*shape, dtype=F32):
        return jax.ShapeDtypeStruct(shape, dtype)

    record_rows = BATCH_COUNT * devices + FIELDS * BATCH_COUNT
    share = obs_cell.shape[1]
    to_right, to_left, record, coef = call(
        prep_kernel,
        (out(half + 1, rows, cols), out(half + 1, rows, cols), out(record_rows, cols), out(2, rows, cols)),
        [ANY] * 9,
        [
            pltpu.VMEM((members, rows, cols), F32),
            pltpu.VMEM((rows, cols), jnp.int32),
            pltpu.VMEM((rows, cols), jnp.int32),
            pltpu.VMEM((BATCH_COUNT, devices, rows), jnp.int32),
            pltpu.VMEM((BATCH_COUNT, share), jnp.int32),
            pltpu.VMEM((BATCH_COUNT, share), jnp.int32),
            pltpu.VMEM((BATCH_COUNT, share), F32),
            pltpu.VMEM((BATCH_COUNT, share), F32),
            pltpu.SMEM((BATCH_COUNT,), jnp.int32),
            pltpu.SemaphoreType.DMA((8 + groups,)),
        ],
        limit=58,
    )(
        sample_heights, depth, land_sea, jnp.transpose(loc_level[:, :, 0, :], (0, 2, 1)), obs_tile[:, :, 0], obs_cell,
        obs_value, obs_error, batch_order,
    )
    left, right = shift_pair(to_left, to_right, "col")

    def slab(start):
        cut = lambda a: lax.slice_in_dim(a, start, start + HALO, axis=1)
        return jnp.concatenate([cut(a) for a in (sample_heights, coef, left, right)], axis=0)

    up, down = shift_pair(slab(0), slab(rows - HALO), "row")
    records = lax.all_to_all(
        jnp.broadcast_to(record, (ncol, *record.shape)), "col", split_axis=0, concat_axis=0, tiled=True
    )

    ext = rows + 2 * HALO
    tall = ext + 2 * HALO
    own, own_k, held = call(
        strips_kernel,
        (out(2 * groups, rows, cols), out(4, rows, cols), out(members, rows, cols)),
        [VMEM] * 4,
    )(sample_heights, coef, left, right)
    state = call(
        forecast_kernel,
        out(members, rows, cols),
        [VMEM] * 6,
        [
            pltpu.VMEM((members, tall, cols), F32),
            pltpu.VMEM((members, tall, cols), F32),
            pltpu.VMEM((members, ext, cols), F32),
            pltpu.VMEM((2 * groups, tall, cols), F32),
            pltpu.VMEM((2 * groups, tall, cols), F32),
            pltpu.VMEM((2 * groups, ext, cols), F32),
            pltpu.VMEM((2, tall, cols), F32),
            pltpu.VMEM((4, tall, cols), F32),
            pltpu.VMEM((10, ext, cols), F32),
            pltpu.VMEM((2, 10, ext, cols), F32),
            pltpu.VMEM((groups, ext, cols), F32),
        ],
    )(held, coef, own, own_k, up, down)
    mine = call(
        functools.partial(extract_kernel, share),
        out(BATCH_COUNT * members + FIELDS * BATCH_COUNT, cols),
        [SMEM, VMEM, VMEM],
        [pltpu.VMEM((8, cols), F32)],
    )(me, records, state)
    seen, _, _ = gather_over(mine, "col")
    parts = call(split_kernel, out(rows, 2 * members, cols, dtype=BF16), [VMEM])(state)

    sums = call(
        functools.partial(first_kernel, members), out(height, members * ncol), [VMEM] * 2
    )(*seen)
    wide = max(LANES, 3 * devices)

    def compose_of(batches, given, trans):
        args = (me, records, *given) + (() if trans is None else (trans,))
        return call(
            functools.partial(compose_kernel, batches),
            out(members, members, cols),
            [SMEM] + [VMEM] * (len(args) - 1),
        )(*args)

    def moved_of(batch, target, given, z):
        args = (levels[(batch, target)], *given) + (seen if z is None else (z,))
        return call(
            functools.partial(moved_kernel, target),
            out(ncol, members, cols),
            [VMEM] * len(args),
        )(*args)

    def next_of(batch, every, z):
        args = (me, *every, levels[(batch, batch + 1)], *seen) + (() if z is None else (z,))
        got = call(
            functools.partial(next_kernel, row_strides, batch),
            (
                out(height, members * ncol),
                out(members * height, wide, dtype=BF16),
                out(members, 2 * LANES, dtype=BF16),
            ),
            [SMEM] + [VMEM] * (len(args) - 1),
        )(*args)
        return got[0], got[1:]

    pairs = [(b, k) for k in range(1, BATCH_COUNT) for b in range(k)]
    found = call(
        functools.partial(levels_kernel, strides),
        tuple(out(ncol // 2, wide, 2 * LANES, dtype=BF16) for _ in pairs),
        [SMEM] + [VMEM] * 3,
    )(me, records, *seen)
    every, (found, parts), _ = gather_over(sums, "row", (found, parts))
    levels = dict(zip(pairs, found))
    sums, first = next_of(0, every, None)
    every, z2, trans = gather_over(
        sums, "row", moved_of(0, 2, first, None), compose_of((0,), first, None)
    )
    sums, second = next_of(1, every, z2)
    z3 = moved_of(0, 3, first, None)
    every, z3, z3_late = gather_over(sums, "row", z3, moved_of(1, 3, second, z3))
    sums, third = next_of(2, every, z3_late)
    trans = compose_of((1,), second, trans)
    every, _, trans = gather_over(sums, "row", trans, compose_of((2,), third, trans))
    return call(
        functools.partial(final_kernel, row_strides),
        out(members, rows, cols),
        [SMEM] + [VMEM] * 5,
        [
            pltpu.VMEM((members * height, wide), BF16),
            pltpu.VMEM((members, members, cols), F32),
            pltpu.VMEM((members, rows, cols), F32),
            pltpu.VMEM((members, rows, cols), F32),
            pltpu.SemaphoreType.DMA((4,)),
        ],
        out_specs=ANY,
    )(me, *every, records, trans, parts)


def solution(mesh):
    return jax.shard_map(
        body,
        mesh=mesh,
        in_specs=(
            P(None, "row", "col"),
            P("row", "col"),
            P("row", "col"),
            P(),
            P(None, ("row", "col")),
            P(None, ("row", "col")),
            P(None, ("row", "col"), None),
            P(None, ("row", "col")),
            P(None, "row", "col", None),
        ),
        out_specs=P(None, "row", "col"),
        check_vma=False,
    )
```

```python
import functools
import itertools

import jax
import jax.numpy as jnp
from jax import lax
from jax.experimental import pallas as pl
from jax.experimental.pallas import tpu as pltpu
from jax.sharding import PartitionSpec as P

BATCH_COUNT = 4
STEPS = 2
SWEEPS = 2
HALO = 8
SEG = 2 * HALO
LANES = 128
FIELDS = 4
HIGH = lax.Precision.HIGHEST
F32 = jnp.float32
BF16 = jnp.bfloat16
SMEM = pl.BlockSpec(memory_space=pltpu.SMEM)
VMEM = pl.BlockSpec(memory_space=pltpu.VMEM)
ANY = pl.BlockSpec(memory_space=pl.ANY)


def iota(shape, dim):
    return lax.broadcasted_iota(jnp.int32, shape, dim)


def strides_of(n):
    out = []
    while n > 1:
        n //= 2
        out.append(n)
    return out


def offset_at(position, strides):
    out = position * 0
    for bit, stride in enumerate(strides):
        out = out + ((position >> bit) & 1) * stride
    return out


def position_of(offset, strides):
    out = offset * 0
    for bit, stride in enumerate(strides):
        out = out + ((offset // stride) & 1) * (1 << bit)
    return out


def gather_over(block, axis, early=(), late=()):
    n = lax.axis_size(axis)
    held = block[None]
    strides = strides_of(n)
    for stride in strides:
        if stride == strides[-1]:
            held, early = lax.optimization_barrier((held, early))
        other = lax.ppermute(held, axis, [(i, i ^ stride) for i in range(n)])
        if stride != strides[-1]:
            held = jnp.concatenate([held, other], axis=0)
    other, late = lax.optimization_barrier((other, late))
    return (held, other), early, late


def shift_pair(low_send, high_send, axis):
    n = lax.axis_size(axis)
    forward = [(i, i + 1) for i in range(n - 1)]
    backward = [(b, a) for a, b in forward]
    return lax.ppermute(high_send, axis, forward), lax.ppermute(low_send, axis, backward)


def nt(a, b, precision=HIGH):
    return lax.dot_general(
        a, b, (((1,), (1,)), ((), ())), precision=precision, preferred_element_type=F32
    )


def split3(x):
    hi = x.astype(BF16).astype(F32)
    rest = x - hi
    mid = rest.astype(BF16).astype(F32)
    return hi, mid, rest - mid


def prep_kernel(
    h_hbm, depth_hbm, sea_hbm, loc_hbm, tile_hbm, cell_hbm, val_hbm, err_hbm, order_hbm,
    to_right_ref, to_left_ref, record_ref, coef_ref,
    h_ref, depth_ref, sea_ref, loc_ref, tile_ref, cell_ref, val_ref, err_ref, order_ref, sems,
):
    members, rows, lanes = h_ref.shape
    groups = members // 8
    half = groups // 2
    pairs = (
        (order_hbm, order_ref),
        (tile_hbm, tile_ref),
        (cell_hbm, cell_ref),
        (val_hbm, val_ref),
        (err_hbm, err_ref),
        (loc_hbm, loc_ref),
        (depth_hbm, depth_ref),
        (sea_hbm, sea_ref),
    )
    small = [
        pltpu.make_async_copy(source, target, sems.at[i])
        for i, (source, target) in enumerate(pairs)
    ]
    large = [
        pltpu.make_async_copy(
            h_hbm.at[pl.ds(8 * g, 8)], h_ref.at[pl.ds(8 * g, 8)], sems.at[len(pairs) + g]
        )
        for g in range(groups)
    ]
    for copy in small + large:
        copy.start()
    seg = iota((rows, lanes), 1) // SEG
    first = iota((rows, lanes), 1) % SEG < HALO
    for copy in small[:6]:
        copy.wait()

    devices = loc_ref.shape[1]
    base = BATCH_COUNT * devices
    fields = FIELDS * BATCH_COUNT
    width = val_ref.shape[1]
    record_ref[base:, :] = jnp.zeros((fields, lanes), F32)
    for k in range(BATCH_COUNT):
        batch = order_ref[k]
        record_ref[k * devices : (k + 1) * devices, :] = loc_ref[batch].astype(F32)
        for f, ref in enumerate((tile_ref, cell_ref, val_ref, err_ref)):
            row = base + f * BATCH_COUNT + k
            record_ref[row : row + 1, 0:width] = ref[pl.ds(batch, 1), :].astype(F32)

    for copy in small[6:]:
        copy.wait()
    sea = sea_ref[...].astype(F32)
    kappa = 0.01 * depth_ref[...].astype(F32) * sea
    coef_ref[0] = kappa
    coef_ref[1] = sea

    def pack(pick):
        out = None
        for q in range(8):
            rolled = pltpu.roll(pick(q), q * SEG + HALO, axis=1)
            out = rolled if out is None else jnp.where(seg == q, rolled, out)
        return out

    def send(g, a, b):
        to_right_ref[g] = jnp.where(first, a, pltpu.roll(b, HALO, axis=1))
        to_left_ref[g] = jnp.where(first, pltpu.roll(b, lanes - HALO, axis=1), a)

    send(half, pack(lambda q: kappa), pack(lambda q: sea))
    for copy in large:
        copy.wait()
    for g in range(half):
        send(g, pack(lambda q: h_ref[8 * g + q]), pack(lambda q: h_ref[8 * (g + half) + q]))


def strip_pair(pick, incoming, second):
    values = [pick(q) for q in range(8)]
    shape = values[0].shape
    lanes = shape[1]
    seg = iota(shape, 1) // SEG
    first = iota(shape, 1) % SEG < HALO
    own = None
    for q in range(8):
        rolled = pltpu.roll(values[q], q * SEG + HALO, axis=1)
        own = rolled if own is None else jnp.where(seg == q, rolled, own)
    from_left, from_right = incoming(0), incoming(1)
    if second:
        from_left = pltpu.roll(from_left, lanes - HALO, axis=1)
        from_right = pltpu.roll(from_right, HALO, axis=1)
    return jnp.where(first, from_left, own), jnp.where(first, own, from_right)


def strips_kernel(h_ref, coef_ref, left_ref, right_ref, out_ref, out_k_ref, held_ref):
    members, rows, lanes = h_ref.shape
    groups = members // 8
    half = groups // 2
    block = 32

    @pl.loop(0, members)
    def _(m):
        held_ref[m] = h_ref[m]

    @pl.loop(0, rows // block)
    def _(b):
        here = pl.ds(pl.multiple_of(b * block, block), block)
        for i in range(2):
            out_k_ref[2 * i, here, :], out_k_ref[2 * i + 1, here, :] = strip_pair(
                lambda q: coef_ref[i, here, :],
                lambda w: (left_ref, right_ref)[w][half, here, :],
                i == 1,
            )
        for g in range(groups):
            out_ref[g, here, :], out_ref[groups + g, here, :] = strip_pair(
                lambda q: h_ref[8 * g + q, here, :],
                lambda w: (left_ref, right_ref)[w][g % half, here, :],
                g >= half,
            )


def forecast_kernel(
    h_ref, coef_ref, own_ref, own_k_ref, up_ref, down_ref, out_ref,
    a_ref, b_ref, rhs_ref, sa_ref, sb_ref, srhs_ref, k_ref, sk_ref, w_ref, sw_ref, edge_ref,
):
    members, rows, lanes = out_ref.shape
    groups = members // 8
    half = groups // 2
    ext = rows + 2 * HALO
    pad = HALO
    inner = pad + HALO
    block = 16
    starts = list(range(0, ext, block))

    for ref in (k_ref, sk_ref):
        for i in range(ref.shape[0]):
            ref[i, pl.ds(0, pad), :] = jnp.zeros((pad, lanes), F32)
            ref[i, pl.ds(pad + ext, pad), :] = jnp.zeros((pad, lanes), F32)
    for i in range(2):
        k_ref[i, pl.ds(pad, HALO), :] = up_ref[members + i]
        k_ref[i, pl.ds(inner, rows), :] = coef_ref[i]
        k_ref[i, pl.ds(inner + rows, HALO), :] = down_ref[members + i]

    @pl.loop(0, members)
    def _(m):
        a_ref[m, pl.ds(pad, HALO), :] = up_ref[m]
        a_ref[m, pl.ds(inner, rows), :] = h_ref[m]
        a_ref[m, pl.ds(inner + rows, HALO), :] = down_ref[m]

    for ref, start in ((up_ref, pad), (down_ref, inner + rows)):
        here = pl.ds(start, HALO)
        for i in range(2):
            sk_ref[2 * i, here, :], sk_ref[2 * i + 1, here, :] = strip_pair(
                lambda q: ref[members + i],
                lambda w: ref[members + 2 + w * (half + 1) + half],
                i == 1,
            )
        for g in range(groups):
            sa_ref[g, here, :], sa_ref[groups + g, here, :] = strip_pair(
                lambda q: ref[8 * g + q],
                lambda w: ref[members + 2 + w * (half + 1) + g % half],
                g >= half,
            )
    for i in range(4):
        sk_ref[i, pl.ds(inner, rows), :] = own_k_ref[i]
    for i in range(2 * groups):
        sa_ref[i, pl.ds(inner, rows), :] = own_ref[i]

    lane = iota((block, lanes), 1)
    is_last = lane == lanes - 1
    is_first = lane == 0
    at_seven = lane % SEG == HALO - 1

    def sides(centre, edge):
        if edge is None:
            return pltpu.roll(centre, 1, axis=1), pltpu.roll(centre, lanes - 1, axis=1)
        return (
            jnp.where(is_first, edge, pltpu.roll(centre, 1, axis=1)),
            jnp.where(is_last, edge, pltpu.roll(centre, lanes - 1, axis=1)),
        )

    def edges_of(low, high):
        return jnp.where(
            at_seven, pltpu.roll(high, lanes - 1, axis=1), pltpu.roll(low, 1, axis=1)
        )

    def weights(ref, at, kap, sea, edges, start):
        here = pl.ds(pad + start, block)

        def four(src, i, edge):
            centre = src[i, here, :]
            return centre, [
                src[i, pl.ds(pad + start - 1, block), :],
                src[i, pl.ds(pad + start + 1, block), :],
                *sides(centre, edge),
            ]

        src = k_ref if edges is not None else sk_ref
        kc, kn = four(src, kap, None if edges is None else edges[0])
        sc, sn = four(src, sea, None if edges is None else edges[1])
        w = [0.5 * (kc + kn[i]) * sc * sn[i] for i in range(4)]
        wsum = w[0] + w[1] + w[2] + w[3]
        inverse = 1.0 / (1.0 + 0.5 * wsum)
        values = [1.0 - 0.5 * wsum] + [0.5 * v for v in w]
        values += [inverse] + [0.5 * v * inverse for v in w]
        for i, value in enumerate(values):
            if at is None:
                ref[i, pl.ds(start, block), :] = value
            else:
                ref[at, i, pl.ds(start, block), :] = value

    for start in starts:
        here = pl.ds(pad + start, block)
        edges = [
            pltpu.roll(
                edges_of(sk_ref[2 * i, here, :], sk_ref[2 * i + 1, here, :]), lanes - HALO, axis=1
            )
            for i in range(2)
        ]
        weights(w_ref, None, 0, 1, edges, start)
        weights(sw_ref, 0, 0, 2, None, start)
        weights(sw_ref, 1, 1, 3, None, start)

    def update(src, dst, rhs, m, start, coef, edge, explicit, store):
        centre = src[m, pl.ds(pad + start, block), :]
        upper = src[m, pl.ds(pad + start - 1, block), :]
        lower = src[m, pl.ds(pad + start + 1, block), :]
        west, east = sides(centre, edge)
        if explicit:
            c0, h0, h1, h2, h3, inverse = coef
            total = c0 * centre + (h0 * upper + h1 * lower) + (h2 * west + h3 * east)
            rhs[m, pl.ds(start, block), :] = total * inverse
        else:
            v0, v1, v2, v3 = coef
            total = rhs[m, pl.ds(start, block), :] + (v0 * upper + v1 * lower)
            total = total + (v2 * west + v3 * east)
        store(m, start, total)

    def sweep(src, dst, ssrc, sdst, explicit, last):
        chosen = range(6) if explicit else range(6, 10)

        def to(ref):
            def store(m, start, value):
                ref[m, pl.ds(pad + start, block), :] = value

            return store

        def to_out(m, start, value):
            out_ref[m, pl.ds(start - HALO, block), :] = value

        @pl.loop(0, groups)
        def _(g):
            for start in starts:
                here = pl.ds(pad + start, block)
                edge_ref[g, pl.ds(start, block), :] = edges_of(
                    ssrc[g, here, :], ssrc[groups + g, here, :]
                )
                for side in (0, 1) if not last else ():
                    coef = [sw_ref[side, i, pl.ds(start, block), :] for i in chosen]
                    update(
                        ssrc, sdst, srhs_ref, side * groups + g, start, coef, None, explicit,
                        to(sdst),
                    )

        @pl.loop(0, groups)
        def _(g):
            for start in range(HALO, HALO + rows, block) if last else starts:
                coef = [w_ref[i, pl.ds(start, block), :] for i in chosen]
                edge = edge_ref[g, pl.ds(start, block), :]
                for q in range(8):
                    rolled = pltpu.roll(edge, (lanes - HALO - SEG * q) % lanes, axis=1)
                    update(
                        src, dst, rhs_ref, 8 * g + q, start, coef, rolled, explicit,
                        to_out if last else to(dst),
                    )

    now, later = (a_ref, sa_ref), (b_ref, sb_ref)
    for step in range(STEPS):
        for stage in range(SWEEPS + 1):
            last = step == STEPS - 1 and stage == SWEEPS
            sweep(now[0], later[0], now[1], later[1], stage == 0, last)
            now, later = later, now


def extract_kernel(owner_share, me_ref, record_ref, state_ref, out_ref, meta_ref):
    members, rows, lanes = state_ref.shape
    ncol, height, _ = record_ref.shape
    fields = FIELDS * BATCH_COUNT
    base = height - fields
    capacity = lanes // ncol
    me = me_ref[1]
    stacked = jnp.concatenate([record_ref[p, base:, :] for p in range(ncol)], axis=0)
    pieces = [
        stacked[i * lanes : (i + 1) * lanes, :].T[0:owner_share]
        for i in range(ncol * fields // lanes)
    ]
    lane = iota((owner_share, lanes), 1)
    square = (owner_share, owner_share)
    triangle = (iota(square, 1) < iota(square, 0)).astype(BF16)
    slot = (lane % capacity).astype(F32)

    def spread(f, k):
        index = (lane // capacity) * fields + f * BATCH_COUNT + k
        out = None
        for i, piece in enumerate(pieces):
            got = jnp.take_along_axis(piece, jnp.clip(index - i * lanes, 0, lanes - 1), axis=1)
            out = got if out is None else jnp.where(index >= i * lanes, got, out)
        return out

    base = BATCH_COUNT * members
    out_ref[base + 3 * BATCH_COUNT :, :] = jnp.zeros((BATCH_COUNT, lanes), F32)
    for k in range(BATCH_COUNT):
        mine = spread(0, k) == me.astype(F32)
        rank = jnp.dot(triangle, mine.astype(BF16), preferred_element_type=F32)
        hot = mine & (rank == slot)

        def slotted(values):
            return jnp.sum(jnp.where(hot, values, 0.0), axis=0, keepdims=True)

        cell = spread(1, k).astype(jnp.int32)
        x = cell // lanes
        error = slotted(spread(3, k))
        taken = error > 0.0
        weight = jnp.where(taken, 1.0 / jnp.where(taken, error, 1.0), 0.0)
        place = slotted((x + 1).astype(F32)) - 1.0
        for n, values in enumerate((weight, slotted(spread(2, k)), place)):
            row = base + n * BATCH_COUNT + k
            out_ref[row : row + 1, :] = values
        meta_ref[k : k + 1, :] = slotted((cell - x * lanes).astype(F32))

    level = iota((8, lanes), 0)
    place = base + 2 * BATCH_COUNT
    for k in range(BATCH_COUNT):
        xs = jnp.broadcast_to(out_ref[place + k : place + k + 1, :], (8, lanes)).astype(jnp.int32)
        ys = jnp.broadcast_to(meta_ref[k : k + 1, :], (8, lanes)).astype(jnp.int32)

        @pl.loop(0, members // 8)
        def _(g):
            totals = []
            for q in range(8):
                total = jnp.zeros((8, lanes), F32)
                for s in range(0, rows, 8):
                    block = state_ref[8 * g + q, pl.ds(s, 8), :]
                    got = jnp.take_along_axis(block, ys, axis=1)
                    total = total + jnp.where(xs == level + s, got, 0.0)
                totals.append(jnp.sum(total, axis=0, keepdims=True))
            row = pl.multiple_of(k * members + 8 * g, 8)
            out_ref[pl.ds(row, 8), :] = jnp.concatenate(totals, axis=0)


def band_sums(ncol, parts):
    lanes = LANES
    mask = (iota((ncol, lanes), 1) // (lanes // ncol) == iota((ncol, lanes), 0)).astype(F32)
    row = iota((8, lanes), 0)
    lefts, rights = [], []
    for z, w, value in parts:
        members = z.shape[0]
        mean = jnp.mean(z, axis=0, keepdims=True)
        anomaly = z - mean
        innov = value - mean
        scaled = anomaly * w

        def masked(values):
            return jnp.concatenate(
                [values[m : m + 1, :] * mask for m in range(members)], axis=0
            ).astype(BF16)

        hi, lo, _ = split3(scaled)
        hi, lo = masked(hi), masked(lo)
        lefts += [hi, lo, hi]
        right = jnp.concatenate([anomaly, jnp.where(row == 0, innov, 0.0)], axis=0)
        hi, lo, _ = split3(right)
        hi, lo = hi.astype(BF16), lo.astype(BF16)
        rights += [hi, hi, lo]
    return nt(jnp.concatenate(rights, axis=1), jnp.concatenate(lefts, axis=1), None)


def seen_rows(seen_refs, p):
    half = seen_refs[0].shape[0]
    return seen_refs[p // half].at[p % half]


def first_kernel(members, low_ref, high_ref, out_ref):
    seen = (low_ref, high_ref)
    ncol = 2 * low_ref.shape[0]
    parts = []
    for p in range(ncol):
        rows = seen_rows(seen, p)
        meta = BATCH_COUNT * members
        parts.append(
            (
                rows[0:members, :],
                rows[meta : meta + 1, :],
                rows[meta + BATCH_COUNT : meta + BATCH_COUNT + 1, :],
            )
        )
    out_ref[...] = band_sums(ncol, parts)


def bands_of(row_strides, me, low_ref, high_ref):
    half = low_ref.shape[0]
    out = []
    for r in range(2 * half):
        at = position_of(jnp.bitwise_xor(me, r), row_strides)
        out.append(
            jnp.where(at < half, low_ref[at % half], high_ref[at % half])
        )
    return out


def spread_steps(bands, spread_ref, ncol):
    height, width = bands[0].shape
    nrow = len(bands)
    members = width // ncol
    devices = nrow * ncol
    lanes = LANES
    lane = iota((height, lanes), 1)
    owner = lane % devices
    which = lane // devices
    per = max(1, lanes // devices)
    for first in range(0, members, per):
        tile, start = divmod(first * ncol, lanes)
        index = start + which * ncol + owner % ncol
        group = None
        for r in range(nrow):
            piece = bands[r][:, tile * lanes : (tile + 1) * lanes]
            got = jnp.take_along_axis(piece, index, axis=1)
            group = got if group is None else jnp.where(owner // ncol == r, got, group)
        for n in range(per):
            m = first + n
            if per > 1:
                value = jnp.take_along_axis(group, n * devices + owner, axis=1)
                hi, mid, lo = split3(value)
                value = jnp.where(which == 0, hi, jnp.where(which == 1, mid, lo))
            else:
                value = jnp.concatenate(split3(group), axis=1)
            spread_ref[pl.ds(m * height, height), :] = value.astype(BF16)
        yield


def stacked(scaled):
    devices = scaled.shape[0]
    copies = max(3, LANES // devices)
    return jnp.concatenate([scaled] * 3 + [jnp.zeros_like(scaled)] * (copies - 3), axis=0)


def copies_of(levels):
    return stacked((levels * 0.125).astype(BF16))


def solve_steps(bands, ncol, result):
    height, width = bands[0].shape
    members = width // ncol
    lanes = LANES
    total = bands[0]
    for band in bands[1:]:
        total = total + band
    pick = (iota((width, lanes), 0) // ncol == iota((width, lanes), 1)).astype(BF16)
    a = sum(
        jnp.dot(part.astype(BF16), pick, preferred_element_type=F32)
        for part in reversed(split3(total))
    )
    row = iota((height, lanes), 0)
    lane = iota((height, lanes), 1)
    a = a + jnp.where((row == lane) & (row < members), members - 1.0, 0.0)
    lane1 = iota((1, lanes), 1)
    block = 8
    for start in range(0, members, block):
        columns = [
            jnp.broadcast_to(a[:, k : k + 1], (height, lanes))
            for k in range(start, start + block)
        ]
        for s in range(block):
            k, column = start + s, columns[s]
            inverse = 1.0 / column[k : k + 1, :]
            scaled = jnp.where(lane1 == k, inverse, a[k : k + 1, :] * inverse)
            a = jnp.where(row == k, scaled, jnp.where(lane == k, 0.0, a) - column * scaled)
            for t in range(s + 1, block):
                part = columns[t][k : k + 1, :] * inverse
                columns[t] = jnp.where(row == k, part, columns[t] - column * part)
        yield
    gain = a[members : members + 1, :] * (1.0 / (members - 1))
    out = jnp.where(lane1 < members, -0.5 * a[0:members, :] + gain, 0.0)
    out = jnp.where(lane1 == members, 1.0 / (members - 1), out)
    hi, lo, _ = split3(out)
    deep = height + 8
    stack = jnp.concatenate(
        [hi[:, 0:deep], hi[:, 0:deep], lo[:, 0:deep], jnp.zeros((members, 2 * lanes - 3 * deep), F32)],
        axis=1,
    )
    result.append(stack.astype(BF16))


def together(long, short, every):
    for n, _ in enumerate(long):
        if n % every == every - 1:
            next(short, None)
    for _ in short:
        pass


def product3(stack, right):
    height, width = right.shape
    hi, lo, _ = split3(right)
    zero = jnp.zeros((8, width), F32)
    hi, lo = (jnp.concatenate([part, zero], axis=0).astype(BF16) for part in (hi, lo))
    deep = 3 * (height + 8)
    return jnp.dot(
        stack[:, 0:deep], jnp.concatenate([hi, lo, hi], axis=0), preferred_element_type=F32
    )


def apply_sums(spread, levels, z, height):
    at = jnp.dot(spread, levels, preferred_element_type=F32)
    total = None
    for m in range(z.shape[0]):
        term = at[m * height : (m + 1) * height, :] * z[m : m + 1, :]
        total = term if total is None else total + term
    return total


def levels_kernel(strides, me_ref, record_ref, low_ref, high_ref, *out_refs):
    seen = (low_ref, high_ref)
    ncol, height, lanes = record_ref.shape
    devices = (height - FIELDS * BATCH_COUNT) // BATCH_COUNT
    members = (low_ref.shape[1] - FIELDS * BATCH_COUNT) // BATCH_COUNT
    base = BATCH_COUNT * members + 2 * BATCH_COUNT
    for p in range(ncol):
        offset = sum(((p >> bit) & 1) * stride for bit, stride in enumerate(strides))
        rows = record_ref.at[jnp.bitwise_xor(me_ref[1], offset)]
        at = 0
        for target in range(1, BATCH_COUNT):
            place = seen_rows(seen, p)[base + target : base + target + 1, :]
            hot = (iota((lanes, lanes), 0) == place.astype(jnp.int32)).astype(BF16)
            table = (rows[0 : target * devices, :] * 0.125).astype(BF16)
            found = jnp.dot(table, hot, preferred_element_type=F32)
            for batch in range(target):
                part = found[batch * devices : (batch + 1) * devices, :].astype(BF16)
                out_refs[at][p // 2, :, (p % 2) * lanes : (p % 2 + 1) * lanes] = stacked(part)
                at += 1


def sums_steps(levels_ref, spread_ref, read, found):
    for p in range(levels_ref.shape[0]):
        z = jnp.concatenate([read(2 * p), read(2 * p + 1)], axis=1)
        found.append((z, apply_sums(spread_ref[...], levels_ref[p], z, z.shape[0] + 8)))
        yield


def moved(found, solved):
    out = []
    for z, sums in found:
        z = z + product3(solved, sums)
        out += [z[:, 0:LANES], z[:, LANES:]]
    return out


def reader(seen, z_ref, members, target):
    if z_ref is not None:
        return lambda i: z_ref[i]
    return lambda i: seen_rows(seen, i)[target * members : (target + 1) * members, :]


def next_kernel(row_strides, batch, *refs):
    me_ref, lows_ref, highs_ref, levels_ref = refs[:4]
    seen = refs[4:6]
    z_ref = refs[6] if batch else None
    out_ref, spread_ref, solved_ref = refs[-3:]
    ncol = 2 * seen[0].shape[0]
    members = solved_ref.shape[0]
    bands = bands_of(row_strides, me_ref[0], lows_ref, highs_ref)
    target = batch + 1
    result, found = [], []
    together(
        itertools.chain(
            spread_steps(bands, spread_ref, ncol),
            sums_steps(levels_ref, spread_ref, reader(seen, z_ref, members, target), found),
        ),
        solve_steps(bands, ncol, result),
        3,
    )
    solved = result[0]
    solved_ref[...] = solved
    zs = moved(found, solved)
    parts = []
    meta = BATCH_COUNT * members + target
    for p in range(ncol):
        rows = seen_rows(seen, p)
        parts.append(
            (
                zs[p],
                rows[meta : meta + 1, :],
                rows[meta + BATCH_COUNT : meta + BATCH_COUNT + 1, :],
            )
        )
    out_ref[...] = band_sums(ncol, parts)


def moved_kernel(target, levels_ref, spread_ref, solved_ref, *refs):
    out_ref = refs[-1]
    z_ref = refs[0] if len(refs) == 2 else None
    read = reader(refs[0:2], z_ref, solved_ref.shape[0], target)
    found = []
    for _ in sums_steps(levels_ref, spread_ref, read, found):
        pass
    for p, z in enumerate(moved(found, solved_ref[...])):
        out_ref[p] = z


def compose_sums(spread_ref, levels, batch, trans_ref, height, members, found):
    at = jnp.dot(spread_ref[...], levels, preferred_element_type=F32)
    for j in range(0, members, 2):
        sums = []
        for i in (j, j + 1):
            if batch == 0:
                sums.append(at[i * height : (i + 1) * height, :])
            else:
                total = None
                for m in range(members):
                    term = at[m * height : (m + 1) * height, :] * trans_ref[i, m : m + 1, :]
                    total = term if total is None else total + term
                sums.append(total)
        found.append(jnp.concatenate(sums, axis=1))
        yield


def compose_end(found, solved, batch, trans_ref, dst_ref):
    members, lanes = solved.shape[0], LANES
    for j, sums in enumerate(found):
        change = product3(solved, sums)
        for n in range(2):
            i = 2 * j + n
            part = change[:, n * lanes : (n + 1) * lanes]
            if batch == 0:
                dst_ref[i] = part + (iota((members, lanes), 0) == i).astype(F32)
            else:
                dst_ref[i] = part + trans_ref[i]


def compose_kernel(batches, me_ref, record_ref, *refs):
    given = refs[: 2 * len(batches)]
    trans_ref = refs[2 * len(batches)] if batches[0] else None
    out_ref = refs[-1]
    members = given[1].shape[0]
    devices = (record_ref.shape[1] - FIELDS * BATCH_COUNT) // BATCH_COUNT
    for n, batch in enumerate(batches):
        levels = copies_of(record_ref[me_ref[1], batch * devices : (batch + 1) * devices, :])
        source = trans_ref if n == 0 else out_ref
        found = []
        for _ in compose_sums(given[2 * n], levels, batch, source, members + 8, members, found):
            pass
        compose_end(found, given[2 * n + 1][...], batch, source, out_ref)


def split_kernel(state_ref, out_ref):
    members, rows, _ = state_ref.shape

    @pl.loop(0, rows // 8)
    def _(b):
        start = pl.multiple_of(b * 8, 8)
        turned = jnp.swapaxes(state_ref[:, pl.ds(start, 8), :], 0, 1)
        for i in range(8):
            hi, lo, _ = split3(turned[i])
            out_ref[start + i] = jnp.concatenate([hi, lo], axis=0).astype(BF16)


def final_kernel(
    row_strides, me_ref, lows_ref, highs_ref, record_ref, trans_ref, state_ref, out_hbm,
    spread_ref, whole_ref, turned_ref, out_ref, sems,
):
    rows, lanes = state_ref.shape[0], state_ref.shape[2]
    members = state_ref.shape[1] // 2
    height, width = lows_ref.shape[1:]
    ncol = width // members
    devices = 2 * lows_ref.shape[0] * ncol
    batch = BATCH_COUNT - 1
    bands = bands_of(row_strides, me_ref[0], lows_ref, highs_ref)
    levels = copies_of(record_ref[me_ref[1], batch * devices : (batch + 1) * devices, :])
    result, found = [], []
    together(
        itertools.chain(
            spread_steps(bands, spread_ref, ncol),
            compose_sums(spread_ref, levels, batch, trans_ref, height, members, found),
        ),
        solve_steps(bands, ncol, result),
        6,
    )
    compose_end(found, result[0], batch, trans_ref, whole_ref)
    for i in range(members):
        hi, lo, _ = split3(whole_ref[:, i, :])
        turned_ref[i] = jnp.concatenate([hi, hi, lo, jnp.zeros_like(hi)], axis=0).T

    share = rows // sems.shape[0]
    copies = []
    for c in range(sems.shape[0]):

        @pl.loop(c * share // 8, (c + 1) * share // 8)
        def _(b):
            start = pl.multiple_of(b * 8, 8)
            lefts = jnp.swapaxes(turned_ref[:, pl.ds(start, 8), :], 0, 1).astype(BF16)
            done = []
            for i in range(8):
                both = state_ref[start + i]
                right = jnp.concatenate([both, both[0:members]], axis=0)
                done.append(
                    jnp.dot(lefts[i][:, 0 : 3 * members], right, preferred_element_type=F32)
                )
            out_ref[:, pl.ds(start, 8), :] = jnp.swapaxes(jnp.stack(done), 0, 1)

        part = pl.ds(c * share, share)
        copies.append(
            pltpu.make_async_copy(out_ref.at[:, part, :], out_hbm.at[:, part, :], sems.at[c])
        )
        copies[-1].start()
    for copy in copies:
        copy.wait()


def call(kernel, out_shape, in_specs, scratch=(), limit=48, out_specs=None):
    return pl.pallas_call(
        kernel,
        out_shape=out_shape,
        in_specs=in_specs,
        out_specs=out_specs or jax.tree.map(lambda _: VMEM, out_shape),
        scratch_shapes=list(scratch),
        compiler_params=pltpu.CompilerParams(vmem_limit_bytes=limit * 1024 * 1024),
    )


def body(
    sample_heights, depth, land_sea, batch_order, obs_value, obs_error, obs_tile, obs_cell, loc_level
):
    members, rows, cols = sample_heights.shape
    ncol = lax.axis_size("col")
    nrow = lax.axis_size("row")
    devices = nrow * ncol
    strides, row_strides = strides_of(ncol), strides_of(nrow)
    groups = members // 8
    half = groups // 2
    height = members + 8
    me = jnp.stack([lax.axis_index("row"), lax.axis_index("col")]).astype(jnp.int32)

    def out(*shape, dtype=F32):
        return jax.ShapeDtypeStruct(shape, dtype)

    record_rows = BATCH_COUNT * devices + FIELDS * BATCH_COUNT
    share = obs_cell.shape[1]
    to_right, to_left, record, coef = call(
        prep_kernel,
        (out(half + 1, rows, cols), out(half + 1, rows, cols), out(record_rows, cols), out(2, rows, cols)),
        [ANY] * 9,
        [
            pltpu.VMEM((members, rows, cols), F32),
            pltpu.VMEM((rows, cols), jnp.int32),
            pltpu.VMEM((rows, cols), jnp.int32),
            pltpu.VMEM((BATCH_COUNT, devices, rows), jnp.int32),
            pltpu.VMEM((BATCH_COUNT, share), jnp.int32),
            pltpu.VMEM((BATCH_COUNT, share), jnp.int32),
            pltpu.VMEM((BATCH_COUNT, share), F32),
            pltpu.VMEM((BATCH_COUNT, share), F32),
            pltpu.SMEM((BATCH_COUNT,), jnp.int32),
            pltpu.SemaphoreType.DMA((8 + groups,)),
        ],
        limit=58,
    )(
        sample_heights, depth, land_sea, jnp.transpose(loc_level[:, :, 0, :], (0, 2, 1)), obs_tile[:, :, 0], obs_cell,
        obs_value, obs_error, batch_order,
    )
    left, right = shift_pair(to_left, to_right, "col")

    def slab(start):
        cut = lambda a: lax.slice_in_dim(a, start, start + HALO, axis=1)
        return jnp.concatenate([cut(a) for a in (sample_heights, coef, left, right)], axis=0)

    up, down = shift_pair(slab(0), slab(rows - HALO), "row")
    records = lax.all_to_all(
        jnp.broadcast_to(record, (ncol, *record.shape)), "col", split_axis=0, concat_axis=0, tiled=True
    )

    ext = rows + 2 * HALO
    tall = ext + 2 * HALO
    own, own_k, held = call(
        strips_kernel,
        (out(2 * groups, rows, cols), out(4, rows, cols), out(members, rows, cols)),
        [VMEM] * 4,
    )(sample_heights, coef, left, right)
    state = call(
        forecast_kernel,
        out(members, rows, cols),
        [VMEM] * 6,
        [
            pltpu.VMEM((members, tall, cols), F32),
            pltpu.VMEM((members, tall, cols), F32),
            pltpu.VMEM((members, ext, cols), F32),
            pltpu.VMEM((2 * groups, tall, cols), F32),
            pltpu.VMEM((2 * groups, tall, cols), F32),
            pltpu.VMEM((2 * groups, ext, cols), F32),
            pltpu.VMEM((2, tall, cols), F32),
            pltpu.VMEM((4, tall, cols), F32),
            pltpu.VMEM((10, ext, cols), F32),
            pltpu.VMEM((2, 10, ext, cols), F32),
            pltpu.VMEM((groups, ext, cols), F32),
        ],
    )(held, coef, own, own_k, up, down)
    mine = call(
        functools.partial(extract_kernel, share),
        out(BATCH_COUNT * members + FIELDS * BATCH_COUNT, cols),
        [SMEM, VMEM, VMEM],
        [pltpu.VMEM((8, cols), F32)],
    )(me, records, state)
    seen, _, _ = gather_over(mine, "col")
    parts = call(split_kernel, out(rows, 2 * members, cols, dtype=BF16), [VMEM])(state)

    sums = call(
        functools.partial(first_kernel, members), out(height, members * ncol), [VMEM] * 2
    )(*seen)
    wide = max(LANES, 3 * devices)

    def compose_of(batches, given, trans):
        args = (me, records, *given) + (() if trans is None else (trans,))
        return call(
            functools.partial(compose_kernel, batches),
            out(members, members, cols),
            [SMEM] + [VMEM] * (len(args) - 1),
        )(*args)

    def moved_of(batch, target, given, z):
        args = (levels[(batch, target)], *given) + (seen if z is None else (z,))
        return call(
            functools.partial(moved_kernel, target),
            out(ncol, members, cols),
            [VMEM] * len(args),
        )(*args)

    def next_of(batch, every, z):
        args = (me, *every, levels[(batch, batch + 1)], *seen) + (() if z is None else (z,))
        got = call(
            functools.partial(next_kernel, row_strides, batch),
            (
                out(height, members * ncol),
                out(members * height, wide, dtype=BF16),
                out(members, 2 * LANES, dtype=BF16),
            ),
            [SMEM] + [VMEM] * (len(args) - 1),
        )(*args)
        return got[0], got[1:]

    pairs = [(b, k) for k in range(1, BATCH_COUNT) for b in range(k)]
    found = call(
        functools.partial(levels_kernel, strides),
        tuple(out(ncol // 2, wide, 2 * LANES, dtype=BF16) for _ in pairs),
        [SMEM] + [VMEM] * 3,
    )(me, records, *seen)
    every, (found, parts), _ = gather_over(sums, "row", (found, parts))
    levels = dict(zip(pairs, found))
    sums, first = next_of(0, every, None)
    every, (z2, z3), trans = gather_over(
        sums,
        "row",
        (moved_of(0, 2, first, None), moved_of(0, 3, first, None)),
        compose_of((0,), first, None),
    )
    sums, second = next_of(1, every, z2)
    every, trans, z3 = gather_over(
        sums, "row", compose_of((1,), second, trans), moved_of(1, 3, second, z3)
    )
    sums, third = next_of(2, every, z3)
    every, trans, _ = gather_over(sums, "row", compose_of((2,), third, trans))
    return call(
        functools.partial(final_kernel, row_strides),
        out(members, rows, cols),
        [SMEM] + [VMEM] * 5,
        [
            pltpu.VMEM((members * height, wide), BF16),
            pltpu.VMEM((members, members, cols), F32),
            pltpu.VMEM((members, rows, cols), F32),
            pltpu.VMEM((members, rows, cols), F32),
            pltpu.SemaphoreType.DMA((4,)),
        ],
        out_specs=ANY,
    )(me, *every, records, trans, parts)


def solution(mesh):
    return jax.shard_map(
        body,
        mesh=mesh,
        in_specs=(
            P(None, "row", "col"),
            P("row", "col"),
            P("row", "col"),
            P(),
            P(None, ("row", "col")),
            P(None, ("row", "col")),
            P(None, ("row", "col"), None),
            P(None, ("row", "col")),
            P(None, "row", "col", None),
        ),
        out_specs=P(None, "row", "col"),
        check_vma=False,
    )
```

```python
import functools
import itertools

import jax
import jax.numpy as jnp
from jax import lax
from jax.experimental import pallas as pl
from jax.experimental.pallas import tpu as pltpu
from jax.sharding import PartitionSpec as P

BATCH_COUNT = 4
STEPS = 2
SWEEPS = 2
HALO = 8
SEG = 2 * HALO
LANES = 128
FIELDS = 4
HIGH = lax.Precision.HIGHEST
F32 = jnp.float32
BF16 = jnp.bfloat16
SMEM = pl.BlockSpec(memory_space=pltpu.SMEM)
VMEM = pl.BlockSpec(memory_space=pltpu.VMEM)
ANY = pl.BlockSpec(memory_space=pl.ANY)


def iota(shape, dim):
    return lax.broadcasted_iota(jnp.int32, shape, dim)


def strides_of(n):
    out = []
    while n > 1:
        n //= 2
        out.append(n)
    return out


def offset_at(position, strides):
    out = position * 0
    for bit, stride in enumerate(strides):
        out = out + ((position >> bit) & 1) * stride
    return out


def position_of(offset, strides):
    out = offset * 0
    for bit, stride in enumerate(strides):
        out = out + ((offset // stride) & 1) * (1 << bit)
    return out


def gather_over(block, axis, early=(), late=()):
    n = lax.axis_size(axis)
    held = block[None]
    strides = strides_of(n)
    for stride in strides:
        if stride == strides[-1]:
            held, early = lax.optimization_barrier((held, early))
        other = lax.ppermute(held, axis, [(i, i ^ stride) for i in range(n)])
        if stride != strides[-1]:
            held = jnp.concatenate([held, other], axis=0)
    other, late = lax.optimization_barrier((other, late))
    return (held, other), early, late


def shift_pair(low_send, high_send, axis):
    n = lax.axis_size(axis)
    forward = [(i, i + 1) for i in range(n - 1)]
    backward = [(b, a) for a, b in forward]
    return lax.ppermute(high_send, axis, forward), lax.ppermute(low_send, axis, backward)


def nt(a, b, precision=HIGH):
    return lax.dot_general(
        a, b, (((1,), (1,)), ((), ())), precision=precision, preferred_element_type=F32
    )


def split3(x):
    hi = x.astype(BF16).astype(F32)
    rest = x - hi
    mid = rest.astype(BF16).astype(F32)
    return hi, mid, rest - mid


def prep_kernel(
    h_hbm, depth_hbm, sea_hbm, loc_hbm, tile_hbm, cell_hbm, val_hbm, err_hbm, order_hbm,
    to_right_ref, to_left_ref, record_ref, coef_ref,
    h_ref, depth_ref, sea_ref, loc_ref, tile_ref, cell_ref, val_ref, err_ref, order_ref, sems,
):
    members, rows, lanes = h_ref.shape
    groups = members // 8
    half = groups // 2
    pairs = (
        (order_hbm, order_ref),
        (tile_hbm, tile_ref),
        (cell_hbm, cell_ref),
        (val_hbm, val_ref),
        (err_hbm, err_ref),
        (loc_hbm, loc_ref),
        (depth_hbm, depth_ref),
        (sea_hbm, sea_ref),
    )
    small = [
        pltpu.make_async_copy(source, target, sems.at[i])
        for i, (source, target) in enumerate(pairs)
    ]
    large = [
        pltpu.make_async_copy(
            h_hbm.at[pl.ds(8 * g, 8)], h_ref.at[pl.ds(8 * g, 8)], sems.at[len(pairs) + g]
        )
        for g in range(groups)
    ]
    for copy in small + large:
        copy.start()
    seg = iota((rows, lanes), 1) // SEG
    first = iota((rows, lanes), 1) % SEG < HALO
    for copy in small[:6]:
        copy.wait()

    devices = loc_ref.shape[1]
    base = BATCH_COUNT * devices
    fields = FIELDS * BATCH_COUNT
    width = val_ref.shape[1]
    record_ref[base:, :] = jnp.zeros((fields, lanes), F32)
    for k in range(BATCH_COUNT):
        batch = order_ref[k]
        record_ref[k * devices : (k + 1) * devices, :] = loc_ref[batch].astype(F32)
        for f, ref in enumerate((tile_ref, cell_ref, val_ref, err_ref)):
            row = base + f * BATCH_COUNT + k
            record_ref[row : row + 1, 0:width] = ref[pl.ds(batch, 1), :].astype(F32)

    for copy in small[6:]:
        copy.wait()
    sea = sea_ref[...].astype(F32)
    kappa = 0.01 * depth_ref[...].astype(F32) * sea
    coef_ref[0] = kappa
    coef_ref[1] = sea

    def pack(pick):
        out = None
        for q in range(8):
            rolled = pltpu.roll(pick(q), q * SEG + HALO, axis=1)
            out = rolled if out is None else jnp.where(seg == q, rolled, out)
        return out

    def send(g, a, b):
        to_right_ref[g] = jnp.where(first, a, pltpu.roll(b, HALO, axis=1))
        to_left_ref[g] = jnp.where(first, pltpu.roll(b, lanes - HALO, axis=1), a)

    send(half, pack(lambda q: kappa), pack(lambda q: sea))
    for copy in large:
        copy.wait()
    for g in range(half):
        send(g, pack(lambda q: h_ref[8 * g + q]), pack(lambda q: h_ref[8 * (g + half) + q]))


def strip_pair(pick, incoming, second):
    values = [pick(q) for q in range(8)]
    shape = values[0].shape
    lanes = shape[1]
    seg = iota(shape, 1) // SEG
    first = iota(shape, 1) % SEG < HALO
    own = None
    for q in range(8):
        rolled = pltpu.roll(values[q], q * SEG + HALO, axis=1)
        own = rolled if own is None else jnp.where(seg == q, rolled, own)
    from_left, from_right = incoming(0), incoming(1)
    if second:
        from_left = pltpu.roll(from_left, lanes - HALO, axis=1)
        from_right = pltpu.roll(from_right, HALO, axis=1)
    return jnp.where(first, from_left, own), jnp.where(first, own, from_right)


def strips_kernel(h_ref, coef_ref, left_ref, right_ref, out_ref, out_k_ref, held_ref):
    members, rows, lanes = h_ref.shape
    groups = members // 8
    half = groups // 2
    block = 32

    @pl.loop(0, members)
    def _(m):
        held_ref[m] = h_ref[m]

    @pl.loop(0, rows // block)
    def _(b):
        here = pl.ds(pl.multiple_of(b * block, block), block)
        for i in range(2):
            out_k_ref[2 * i, here, :], out_k_ref[2 * i + 1, here, :] = strip_pair(
                lambda q: coef_ref[i, here, :],
                lambda w: (left_ref, right_ref)[w][half, here, :],
                i == 1,
            )
        for g in range(groups):
            out_ref[g, here, :], out_ref[groups + g, here, :] = strip_pair(
                lambda q: h_ref[8 * g + q, here, :],
                lambda w: (left_ref, right_ref)[w][g % half, here, :],
                g >= half,
            )


def forecast_kernel(
    h_ref, coef_ref, own_ref, own_k_ref, up_ref, down_ref, out_ref,
    a_ref, b_ref, rhs_ref, sa_ref, sb_ref, srhs_ref, k_ref, sk_ref, w_ref, sw_ref, edge_ref,
):
    members, rows, lanes = out_ref.shape
    groups = members // 8
    half = groups // 2
    ext = rows + 2 * HALO
    pad = HALO
    inner = pad + HALO
    block = 16
    starts = list(range(0, ext, block))

    for ref in (k_ref, sk_ref):
        for i in range(ref.shape[0]):
            ref[i, pl.ds(0, pad), :] = jnp.zeros((pad, lanes), F32)
            ref[i, pl.ds(pad + ext, pad), :] = jnp.zeros((pad, lanes), F32)
    for i in range(2):
        k_ref[i, pl.ds(pad, HALO), :] = up_ref[members + i]
        k_ref[i, pl.ds(inner, rows), :] = coef_ref[i]
        k_ref[i, pl.ds(inner + rows, HALO), :] = down_ref[members + i]

    @pl.loop(0, members)
    def _(m):
        a_ref[m, pl.ds(pad, HALO), :] = up_ref[m]
        a_ref[m, pl.ds(inner, rows), :] = h_ref[m]
        a_ref[m, pl.ds(inner + rows, HALO), :] = down_ref[m]

    for ref, start in ((up_ref, pad), (down_ref, inner + rows)):
        here = pl.ds(start, HALO)
        for i in range(2):
            sk_ref[2 * i, here, :], sk_ref[2 * i + 1, here, :] = strip_pair(
                lambda q: ref[members + i],
                lambda w: ref[members + 2 + w * (half + 1) + half],
                i == 1,
            )
        for g in range(groups):
            sa_ref[g, here, :], sa_ref[groups + g, here, :] = strip_pair(
                lambda q: ref[8 * g + q],
                lambda w: ref[members + 2 + w * (half + 1) + g % half],
                g >= half,
            )
    for i in range(4):
        sk_ref[i, pl.ds(inner, rows), :] = own_k_ref[i]
    for i in range(2 * groups):
        sa_ref[i, pl.ds(inner, rows), :] = own_ref[i]

    lane = iota((block, lanes), 1)
    is_last = lane == lanes - 1
    is_first = lane == 0
    at_seven = lane % SEG == HALO - 1

    def sides(centre, edge):
        if edge is None:
            return pltpu.roll(centre, 1, axis=1), pltpu.roll(centre, lanes - 1, axis=1)
        return (
            jnp.where(is_first, edge, pltpu.roll(centre, 1, axis=1)),
            jnp.where(is_last, edge, pltpu.roll(centre, lanes - 1, axis=1)),
        )

    def edges_of(low, high):
        return jnp.where(
            at_seven, pltpu.roll(high, lanes - 1, axis=1), pltpu.roll(low, 1, axis=1)
        )

    def weights(ref, at, kap, sea, edges, start):
        here = pl.ds(pad + start, block)

        def four(src, i, edge):
            centre = src[i, here, :]
            return centre, [
                src[i, pl.ds(pad + start - 1, block), :],
                src[i, pl.ds(pad + start + 1, block), :],
                *sides(centre, edge),
            ]

        src = k_ref if edges is not None else sk_ref
        kc, kn = four(src, kap, None if edges is None else edges[0])
        sc, sn = four(src, sea, None if edges is None else edges[1])
        w = [0.5 * (kc + kn[i]) * sc * sn[i] for i in range(4)]
        wsum = w[0] + w[1] + w[2] + w[3]
        inverse = 1.0 / (1.0 + 0.5 * wsum)
        values = [1.0 - 0.5 * wsum] + [0.5 * v for v in w]
        values += [inverse] + [0.5 * v * inverse for v in w]
        for i, value in enumerate(values):
            if at is None:
                ref[i, pl.ds(start, block), :] = value
            else:
                ref[at, i, pl.ds(start, block), :] = value

    for start in starts:
        here = pl.ds(pad + start, block)
        edges = [
            pltpu.roll(
                edges_of(sk_ref[2 * i, here, :], sk_ref[2 * i + 1, here, :]), lanes - HALO, axis=1
            )
            for i in range(2)
        ]
        weights(w_ref, None, 0, 1, edges, start)
        weights(sw_ref, 0, 0, 2, None, start)
        weights(sw_ref, 1, 1, 3, None, start)

    def update(src, dst, rhs, m, start, coef, edge, explicit, store):
        centre = src[m, pl.ds(pad + start, block), :]
        upper = src[m, pl.ds(pad + start - 1, block), :]
        lower = src[m, pl.ds(pad + start + 1, block), :]
        west, east = sides(centre, edge)
        if explicit:
            c0, h0, h1, h2, h3, inverse = coef
            total = c0 * centre + (h0 * upper + h1 * lower) + (h2 * west + h3 * east)
            rhs[m, pl.ds(start, block), :] = total * inverse
        else:
            v0, v1, v2, v3 = coef
            total = rhs[m, pl.ds(start, block), :] + (v0 * upper + v1 * lower)
            total = total + (v2 * west + v3 * east)
        store(m, start, total)

    def sweep(src, dst, ssrc, sdst, explicit, last):
        chosen = range(6) if explicit else range(6, 10)

        def to(ref):
            def store(m, start, value):
                ref[m, pl.ds(pad + start, block), :] = value

            return store

        def to_out(m, start, value):
            out_ref[m, pl.ds(start - HALO, block), :] = value

        @pl.loop(0, groups)
        def _(g):
            for start in starts:
                here = pl.ds(pad + start, block)
                edge_ref[g, pl.ds(start, block), :] = edges_of(
                    ssrc[g, here, :], ssrc[groups + g, here, :]
                )
                for side in (0, 1) if not last else ():
                    coef = [sw_ref[side, i, pl.ds(start, block), :] for i in chosen]
                    update(
                        ssrc, sdst, srhs_ref, side * groups + g, start, coef, None, explicit,
                        to(sdst),
                    )

        @pl.loop(0, groups)
        def _(g):
            for start in range(HALO, HALO + rows, block) if last else starts:
                coef = [w_ref[i, pl.ds(start, block), :] for i in chosen]
                edge = edge_ref[g, pl.ds(start, block), :]
                for q in range(8):
                    rolled = pltpu.roll(edge, (lanes - HALO - SEG * q) % lanes, axis=1)
                    update(
                        src, dst, rhs_ref, 8 * g + q, start, coef, rolled, explicit,
                        to_out if last else to(dst),
                    )

    now, later = (a_ref, sa_ref), (b_ref, sb_ref)
    for step in range(STEPS):
        for stage in range(SWEEPS + 1):
            last = step == STEPS - 1 and stage == SWEEPS
            sweep(now[0], later[0], now[1], later[1], stage == 0, last)
            now, later = later, now


def extract_kernel(owner_share, me_ref, record_ref, state_ref, out_ref, meta_ref):
    members, rows, lanes = state_ref.shape
    ncol, height, _ = record_ref.shape
    fields = FIELDS * BATCH_COUNT
    base = height - fields
    capacity = lanes // ncol
    me = me_ref[1]
    stacked = jnp.concatenate([record_ref[p, base:, :] for p in range(ncol)], axis=0)
    pieces = [
        stacked[i * lanes : (i + 1) * lanes, :].T[0:owner_share]
        for i in range(ncol * fields // lanes)
    ]
    lane = iota((owner_share, lanes), 1)
    square = (owner_share, owner_share)
    triangle = (iota(square, 1) < iota(square, 0)).astype(BF16)
    slot = (lane % capacity).astype(F32)

    def spread(f, k):
        index = (lane // capacity) * fields + f * BATCH_COUNT + k
        out = None
        for i, piece in enumerate(pieces):
            got = jnp.take_along_axis(piece, jnp.clip(index - i * lanes, 0, lanes - 1), axis=1)
            out = got if out is None else jnp.where(index >= i * lanes, got, out)
        return out

    base = BATCH_COUNT * members
    out_ref[base + 3 * BATCH_COUNT :, :] = jnp.zeros((BATCH_COUNT, lanes), F32)
    for k in range(BATCH_COUNT):
        mine = spread(0, k) == me.astype(F32)
        rank = jnp.dot(triangle, mine.astype(BF16), preferred_element_type=F32)
        hot = mine & (rank == slot)

        def slotted(values):
            return jnp.sum(jnp.where(hot, values, 0.0), axis=0, keepdims=True)

        cell = spread(1, k).astype(jnp.int32)
        x = cell // lanes
        error = slotted(spread(3, k))
        taken = error > 0.0
        weight = jnp.where(taken, 1.0 / jnp.where(taken, error, 1.0), 0.0)
        place = slotted((x + 1).astype(F32)) - 1.0
        for n, values in enumerate((weight, slotted(spread(2, k)), place)):
            row = base + n * BATCH_COUNT + k
            out_ref[row : row + 1, :] = values
        meta_ref[k : k + 1, :] = slotted((cell - x * lanes).astype(F32))

    level = iota((8, lanes), 0)
    place = base + 2 * BATCH_COUNT
    for k in range(BATCH_COUNT):
        xs = jnp.broadcast_to(out_ref[place + k : place + k + 1, :], (8, lanes)).astype(jnp.int32)
        ys = jnp.broadcast_to(meta_ref[k : k + 1, :], (8, lanes)).astype(jnp.int32)

        @pl.loop(0, members // 8)
        def _(g):
            totals = []
            for q in range(8):
                total = jnp.zeros((8, lanes), F32)
                for s in range(0, rows, 8):
                    block = state_ref[8 * g + q, pl.ds(s, 8), :]
                    got = jnp.take_along_axis(block, ys, axis=1)
                    total = total + jnp.where(xs == level + s, got, 0.0)
                totals.append(jnp.sum(total, axis=0, keepdims=True))
            row = pl.multiple_of(k * members + 8 * g, 8)
            out_ref[pl.ds(row, 8), :] = jnp.concatenate(totals, axis=0)


def band_sums(ncol, parts):
    lanes = LANES
    mask = (iota((ncol, lanes), 1) // (lanes // ncol) == iota((ncol, lanes), 0)).astype(F32)
    row = iota((8, lanes), 0)
    lefts, rights = [], []
    for z, w, value in parts:
        members = z.shape[0]
        mean = jnp.mean(z, axis=0, keepdims=True)
        anomaly = z - mean
        innov = value - mean
        scaled = anomaly * w

        def masked(values):
            return jnp.concatenate(
                [values[m : m + 1, :] * mask for m in range(members)], axis=0
            ).astype(BF16)

        hi, lo, _ = split3(scaled)
        hi, lo = masked(hi), masked(lo)
        lefts += [hi, lo, hi]
        right = jnp.concatenate([anomaly, jnp.where(row == 0, innov, 0.0)], axis=0)
        hi, lo, _ = split3(right)
        hi, lo = hi.astype(BF16), lo.astype(BF16)
        rights += [hi, hi, lo]
    return nt(jnp.concatenate(rights, axis=1), jnp.concatenate(lefts, axis=1), None)


def seen_rows(seen_refs, p):
    half = seen_refs[0].shape[0]
    return seen_refs[p // half].at[p % half]


def first_kernel(members, low_ref, high_ref, out_ref):
    seen = (low_ref, high_ref)
    ncol = 2 * low_ref.shape[0]
    parts = []
    for p in range(ncol):
        rows = seen_rows(seen, p)
        meta = BATCH_COUNT * members
        parts.append(
            (
                rows[0:members, :],
                rows[meta : meta + 1, :],
                rows[meta + BATCH_COUNT : meta + BATCH_COUNT + 1, :],
            )
        )
    out_ref[...] = band_sums(ncol, parts)


def bands_of(row_strides, me, low_ref, high_ref):
    half = low_ref.shape[0]
    out = []
    for r in range(2 * half):
        at = position_of(jnp.bitwise_xor(me, r), row_strides)
        out.append(
            jnp.where(at < half, low_ref[at % half], high_ref[at % half])
        )
    return out


def spread_steps(bands, spread_ref, ncol):
    height, width = bands[0].shape
    nrow = len(bands)
    members = width // ncol
    devices = nrow * ncol
    lanes = LANES
    lane = iota((height, lanes), 1)
    owner = lane % devices
    which = lane // devices
    per = max(1, lanes // devices)
    for first in range(0, members, per):
        tile, start = divmod(first * ncol, lanes)
        index = start + which * ncol + owner % ncol
        group = None
        for r in range(nrow):
            piece = bands[r][:, tile * lanes : (tile + 1) * lanes]
            got = jnp.take_along_axis(piece, index, axis=1)
            group = got if group is None else jnp.where(owner // ncol == r, got, group)
        for n in range(per):
            m = first + n
            if per > 1:
                value = jnp.take_along_axis(group, n * devices + owner, axis=1)
                hi, mid, lo = split3(value)
                value = jnp.where(which == 0, hi, jnp.where(which == 1, mid, lo))
            else:
                value = jnp.concatenate(split3(group), axis=1)
            spread_ref[pl.ds(m * height, height), :] = value.astype(BF16)
        yield


def stacked(scaled):
    devices = scaled.shape[0]
    copies = max(3, LANES // devices)
    return jnp.concatenate([scaled] * 3 + [jnp.zeros_like(scaled)] * (copies - 3), axis=0)


def copies_of(levels):
    return stacked((levels * 0.125).astype(BF16))


def solve_steps(bands, ncol, result):
    height, width = bands[0].shape
    members = width // ncol
    lanes = LANES
    total = bands[0]
    for band in bands[1:]:
        total = total + band
    pick = (iota((width, lanes), 0) // ncol == iota((width, lanes), 1)).astype(BF16)
    a = sum(
        jnp.dot(part.astype(BF16), pick, preferred_element_type=F32)
        for part in reversed(split3(total))
    )
    row = iota((height, lanes), 0)
    lane = iota((height, lanes), 1)
    a = a + jnp.where((row == lane) & (row < members), members - 1.0, 0.0)
    lane1 = iota((1, lanes), 1)
    block = 8
    for start in range(0, members, block):
        columns = [
            jnp.broadcast_to(a[:, k : k + 1], (height, lanes))
            for k in range(start, start + block)
        ]
        for s in range(block):
            k, column = start + s, columns[s]
            inverse = 1.0 / column[k : k + 1, :]
            scaled = jnp.where(lane1 == k, inverse, a[k : k + 1, :] * inverse)
            a = jnp.where(row == k, scaled, jnp.where(lane == k, 0.0, a) - column * scaled)
            for t in range(s + 1, block):
                part = columns[t][k : k + 1, :] * inverse
                columns[t] = jnp.where(row == k, part, columns[t] - column * part)
        yield
    gain = a[members : members + 1, :] * (1.0 / (members - 1))
    out = jnp.where(lane1 < members, -0.5 * a[0:members, :] + gain, 0.0)
    out = jnp.where(lane1 == members, 1.0 / (members - 1), out)
    hi, lo, _ = split3(out)
    deep = height + 8
    stack = jnp.concatenate(
        [hi[:, 0:deep], hi[:, 0:deep], lo[:, 0:deep], jnp.zeros((members, 2 * lanes - 3 * deep), F32)],
        axis=1,
    )
    result.append(stack.astype(BF16))


def together(long, short, every):
    for n, _ in enumerate(long):
        if n % every == every - 1:
            next(short, None)
    for _ in short:
        pass


def product3(stack, right):
    height, width = right.shape
    hi, lo, _ = split3(right)
    zero = jnp.zeros((8, width), F32)
    hi, lo = (jnp.concatenate([part, zero], axis=0).astype(BF16) for part in (hi, lo))
    deep = 3 * (height + 8)
    return jnp.dot(
        stack[:, 0:deep], jnp.concatenate([hi, lo, hi], axis=0), preferred_element_type=F32
    )


def apply_sums(spread, levels, z, height):
    at = jnp.dot(spread, levels, preferred_element_type=F32)
    total = None
    for m in range(z.shape[0]):
        term = at[m * height : (m + 1) * height, :] * z[m : m + 1, :]
        total = term if total is None else total + term
    return total


def levels_kernel(strides, me_ref, record_ref, low_ref, high_ref, *out_refs):
    seen = (low_ref, high_ref)
    ncol, height, lanes = record_ref.shape
    devices = (height - FIELDS * BATCH_COUNT) // BATCH_COUNT
    members = (low_ref.shape[1] - FIELDS * BATCH_COUNT) // BATCH_COUNT
    base = BATCH_COUNT * members + 2 * BATCH_COUNT
    for p in range(ncol):
        offset = sum(((p >> bit) & 1) * stride for bit, stride in enumerate(strides))
        rows = record_ref.at[jnp.bitwise_xor(me_ref[1], offset)]
        at = 0
        for target in range(1, BATCH_COUNT):
            place = seen_rows(seen, p)[base + target : base + target + 1, :]
            hot = (iota((lanes, lanes), 0) == place.astype(jnp.int32)).astype(BF16)
            table = (rows[0 : target * devices, :] * 0.125).astype(BF16)
            found = jnp.dot(table, hot, preferred_element_type=F32)
            for batch in range(target):
                part = found[batch * devices : (batch + 1) * devices, :].astype(BF16)
                out_refs[at][p // 2, :, (p % 2) * lanes : (p % 2 + 1) * lanes] = stacked(part)
                at += 1


def sums_steps(levels_ref, spread_ref, read, found):
    for p in range(levels_ref.shape[0]):
        z = jnp.concatenate([read(2 * p), read(2 * p + 1)], axis=1)
        found.append((z, apply_sums(spread_ref[...], levels_ref[p], z, z.shape[0] + 8)))
        yield


def moved(found, solved):
    out = []
    for z, sums in found:
        z = z + product3(solved, sums)
        out += [z[:, 0:LANES], z[:, LANES:]]
    return out


def reader(seen, z_ref, members, target):
    if z_ref is not None:
        return lambda i: z_ref[i]
    return lambda i: seen_rows(seen, i)[target * members : (target + 1) * members, :]


def next_kernel(row_strides, batch, *refs):
    me_ref, lows_ref, highs_ref, levels_ref = refs[:4]
    seen = refs[4:6]
    z_ref = refs[6] if batch else None
    out_ref, spread_ref, solved_ref = refs[-3:]
    ncol = 2 * seen[0].shape[0]
    members = solved_ref.shape[0]
    bands = bands_of(row_strides, me_ref[0], lows_ref, highs_ref)
    target = batch + 1
    result, found = [], []
    together(
        itertools.chain(
            spread_steps(bands, spread_ref, ncol),
            sums_steps(levels_ref, spread_ref, reader(seen, z_ref, members, target), found),
        ),
        solve_steps(bands, ncol, result),
        2,
    )
    solved = result[0]
    solved_ref[...] = solved
    zs = moved(found, solved)
    parts = []
    meta = BATCH_COUNT * members + target
    for p in range(ncol):
        rows = seen_rows(seen, p)
        parts.append(
            (
                zs[p],
                rows[meta : meta + 1, :],
                rows[meta + BATCH_COUNT : meta + BATCH_COUNT + 1, :],
            )
        )
    out_ref[...] = band_sums(ncol, parts)


def moved_kernel(target, levels_ref, spread_ref, solved_ref, *refs):
    out_ref = refs[-1]
    z_ref = refs[0] if len(refs) == 2 else None
    read = reader(refs[0:2], z_ref, solved_ref.shape[0], target)
    found = []
    for _ in sums_steps(levels_ref, spread_ref, read, found):
        pass
    for p, z in enumerate(moved(found, solved_ref[...])):
        out_ref[p] = z


def compose_sums(spread_ref, levels, batch, trans_ref, height, members, found):
    at = jnp.dot(spread_ref[...], levels, preferred_element_type=F32)
    for j in range(0, members, 2):
        sums = []
        for i in (j, j + 1):
            if batch == 0:
                sums.append(at[i * height : (i + 1) * height, :])
            else:
                total = None
                for m in range(members):
                    term = at[m * height : (m + 1) * height, :] * trans_ref[i, m : m + 1, :]
                    total = term if total is None else total + term
                sums.append(total)
        found.append(jnp.concatenate(sums, axis=1))
        yield


def compose_end(found, solved, batch, trans_ref, dst_ref):
    members, lanes = solved.shape[0], LANES
    for j, sums in enumerate(found):
        change = product3(solved, sums)
        for n in range(2):
            i = 2 * j + n
            part = change[:, n * lanes : (n + 1) * lanes]
            if batch == 0:
                dst_ref[i] = part + (iota((members, lanes), 0) == i).astype(F32)
            else:
                dst_ref[i] = part + trans_ref[i]


def compose_kernel(batches, me_ref, record_ref, *refs):
    given = refs[: 2 * len(batches)]
    trans_ref = refs[2 * len(batches)] if batches[0] else None
    out_ref = refs[-1]
    members = given[1].shape[0]
    devices = (record_ref.shape[1] - FIELDS * BATCH_COUNT) // BATCH_COUNT
    for n, batch in enumerate(batches):
        levels = copies_of(record_ref[me_ref[1], batch * devices : (batch + 1) * devices, :])
        source = trans_ref if n == 0 else out_ref
        found = []
        for _ in compose_sums(given[2 * n], levels, batch, source, members + 8, members, found):
            pass
        compose_end(found, given[2 * n + 1][...], batch, source, out_ref)


def split_kernel(state_ref, out_ref):
    members, rows, _ = state_ref.shape

    @pl.loop(0, rows // 8)
    def _(b):
        start = pl.multiple_of(b * 8, 8)
        turned = jnp.swapaxes(state_ref[:, pl.ds(start, 8), :], 0, 1)
        for i in range(8):
            hi, lo, _ = split3(turned[i])
            out_ref[start + i] = jnp.concatenate([hi, lo], axis=0).astype(BF16)


def final_kernel(
    row_strides, me_ref, lows_ref, highs_ref, record_ref, trans_ref, state_ref, out_hbm,
    spread_ref, whole_ref, turned_ref, out_ref, sems,
):
    rows, lanes = state_ref.shape[0], state_ref.shape[2]
    members = state_ref.shape[1] // 2
    height, width = lows_ref.shape[1:]
    ncol = width // members
    devices = 2 * lows_ref.shape[0] * ncol
    batch = BATCH_COUNT - 1
    bands = bands_of(row_strides, me_ref[0], lows_ref, highs_ref)
    levels = copies_of(record_ref[me_ref[1], batch * devices : (batch + 1) * devices, :])
    result, found = [], []
    together(
        itertools.chain(
            spread_steps(bands, spread_ref, ncol),
            compose_sums(spread_ref, levels, batch, trans_ref, height, members, found),
        ),
        solve_steps(bands, ncol, result),
        2,
    )
    compose_end(found, result[0], batch, trans_ref, whole_ref)
    for i in range(members):
        hi, lo, _ = split3(whole_ref[:, i, :])
        turned_ref[i] = jnp.concatenate([hi, hi, lo, jnp.zeros_like(hi)], axis=0).T

    share = rows // sems.shape[0]
    copies = []
    for c in range(sems.shape[0]):

        @pl.loop(c * share // 8, (c + 1) * share // 8, unroll=2)
        def _(b):
            start = pl.multiple_of(b * 8, 8)
            lefts = jnp.swapaxes(turned_ref[:, pl.ds(start, 8), :], 0, 1).astype(BF16)
            done = []
            for i in range(8):
                both = state_ref[start + i]
                right = jnp.concatenate([both, both[0:members]], axis=0)
                done.append(
                    jnp.dot(lefts[i][:, 0 : 3 * members], right, preferred_element_type=F32)
                )
            out_ref[:, pl.ds(start, 8), :] = jnp.swapaxes(jnp.stack(done), 0, 1)

        part = pl.ds(c * share, share)
        copies.append(
            pltpu.make_async_copy(out_ref.at[:, part, :], out_hbm.at[:, part, :], sems.at[c])
        )
        copies[-1].start()
    for copy in copies:
        copy.wait()


def call(kernel, out_shape, in_specs, scratch=(), limit=48, out_specs=None):
    return pl.pallas_call(
        kernel,
        out_shape=out_shape,
        in_specs=in_specs,
        out_specs=out_specs or jax.tree.map(lambda _: VMEM, out_shape),
        scratch_shapes=list(scratch),
        compiler_params=pltpu.CompilerParams(vmem_limit_bytes=limit * 1024 * 1024),
    )


def body(
    sample_heights, depth, land_sea, batch_order, obs_value, obs_error, obs_tile, obs_cell, loc_level
):
    members, rows, cols = sample_heights.shape
    ncol = lax.axis_size("col")
    nrow = lax.axis_size("row")
    devices = nrow * ncol
    strides, row_strides = strides_of(ncol), strides_of(nrow)
    groups = members // 8
    half = groups // 2
    height = members + 8
    me = jnp.stack([lax.axis_index("row"), lax.axis_index("col")]).astype(jnp.int32)

    def out(*shape, dtype=F32):
        return jax.ShapeDtypeStruct(shape, dtype)

    record_rows = BATCH_COUNT * devices + FIELDS * BATCH_COUNT
    share = obs_cell.shape[1]
    to_right, to_left, record, coef = call(
        prep_kernel,
        (out(half + 1, rows, cols), out(half + 1, rows, cols), out(record_rows, cols), out(2, rows, cols)),
        [ANY] * 9,
        [
            pltpu.VMEM((members, rows, cols), F32),
            pltpu.VMEM((rows, cols), jnp.int32),
            pltpu.VMEM((rows, cols), jnp.int32),
            pltpu.VMEM((BATCH_COUNT, devices, rows), jnp.int32),
            pltpu.VMEM((BATCH_COUNT, share), jnp.int32),
            pltpu.VMEM((BATCH_COUNT, share), jnp.int32),
            pltpu.VMEM((BATCH_COUNT, share), F32),
            pltpu.VMEM((BATCH_COUNT, share), F32),
            pltpu.SMEM((BATCH_COUNT,), jnp.int32),
            pltpu.SemaphoreType.DMA((8 + groups,)),
        ],
        limit=58,
    )(
        sample_heights, depth, land_sea, jnp.transpose(loc_level[:, :, 0, :], (0, 2, 1)), obs_tile[:, :, 0], obs_cell,
        obs_value, obs_error, batch_order,
    )
    left, right = shift_pair(to_left, to_right, "col")

    def slab(start):
        cut = lambda a: lax.slice_in_dim(a, start, start + HALO, axis=1)
        return jnp.concatenate([cut(a) for a in (sample_heights, coef, left, right)], axis=0)

    up, down = shift_pair(slab(0), slab(rows - HALO), "row")
    records = lax.all_to_all(
        jnp.broadcast_to(record, (ncol, *record.shape)), "col", split_axis=0, concat_axis=0, tiled=True
    )

    ext = rows + 2 * HALO
    tall = ext + 2 * HALO
    own, own_k, held = call(
        strips_kernel,
        (out(2 * groups, rows, cols), out(4, rows, cols), out(members, rows, cols)),
        [VMEM] * 4,
    )(sample_heights, coef, left, right)
    state = call(
        forecast_kernel,
        out(members, rows, cols),
        [VMEM] * 6,
        [
            pltpu.VMEM((members, tall, cols), F32),
            pltpu.VMEM((members, tall, cols), F32),
            pltpu.VMEM((members, ext, cols), F32),
            pltpu.VMEM((2 * groups, tall, cols), F32),
            pltpu.VMEM((2 * groups, tall, cols), F32),
            pltpu.VMEM((2 * groups, ext, cols), F32),
            pltpu.VMEM((2, tall, cols), F32),
            pltpu.VMEM((4, tall, cols), F32),
            pltpu.VMEM((10, ext, cols), F32),
            pltpu.VMEM((2, 10, ext, cols), F32),
            pltpu.VMEM((groups, ext, cols), F32),
        ],
    )(held, coef, own, own_k, up, down)
    mine = call(
        functools.partial(extract_kernel, share),
        out(BATCH_COUNT * members + FIELDS * BATCH_COUNT, cols),
        [SMEM, VMEM, VMEM],
        [pltpu.VMEM((8, cols), F32)],
    )(me, records, state)
    seen, _, _ = gather_over(mine, "col")
    parts = call(split_kernel, out(rows, 2 * members, cols, dtype=BF16), [VMEM])(state)

    sums = call(
        functools.partial(first_kernel, members), out(height, members * ncol), [VMEM] * 2
    )(*seen)
    wide = max(LANES, 3 * devices)

    def compose_of(batches, given, trans):
        args = (me, records, *given) + (() if trans is None else (trans,))
        return call(
            functools.partial(compose_kernel, batches),
            out(members, members, cols),
            [SMEM] + [VMEM] * (len(args) - 1),
        )(*args)

    def moved_of(batch, target, given, z):
        args = (levels[(batch, target)], *given) + (seen if z is None else (z,))
        return call(
            functools.partial(moved_kernel, target),
            out(ncol, members, cols),
            [VMEM] * len(args),
        )(*args)

    def next_of(batch, every, z):
        args = (me, *every, levels[(batch, batch + 1)], *seen) + (() if z is None else (z,))
        got = call(
            functools.partial(next_kernel, row_strides, batch),
            (
                out(height, members * ncol),
                out(members * height, wide, dtype=BF16),
                out(members, 2 * LANES, dtype=BF16),
            ),
            [SMEM] + [VMEM] * (len(args) - 1),
        )(*args)
        return got[0], got[1:]

    pairs = [(b, k) for k in range(1, BATCH_COUNT) for b in range(k)]
    found = call(
        functools.partial(levels_kernel, strides),
        tuple(out(ncol // 2, wide, 2 * LANES, dtype=BF16) for _ in pairs),
        [SMEM] + [VMEM] * 3,
    )(me, records, *seen)
    every, (found, parts), _ = gather_over(sums, "row", (found, parts))
    levels = dict(zip(pairs, found))
    sums, first = next_of(0, every, None)
    every, (z2, z3), trans = gather_over(
        sums,
        "row",
        (moved_of(0, 2, first, None), moved_of(0, 3, first, None)),
        compose_of((0,), first, None),
    )
    sums, second = next_of(1, every, z2)
    every, trans, z3 = gather_over(
        sums, "row", compose_of((1,), second, trans), moved_of(1, 3, second, z3)
    )
    sums, third = next_of(2, every, z3)
    every, trans, _ = gather_over(sums, "row", compose_of((2,), third, trans))
    return call(
        functools.partial(final_kernel, row_strides),
        out(members, rows, cols),
        [SMEM] + [VMEM] * 5,
        [
            pltpu.VMEM((members * height, wide), BF16),
            pltpu.VMEM((members, members, cols), F32),
            pltpu.VMEM((members, rows, cols), F32),
            pltpu.VMEM((members, rows, cols), F32),
            pltpu.SemaphoreType.DMA((4,)),
        ],
        out_specs=ANY,
    )(me, *every, records, trans, parts)


def solution(mesh):
    return jax.shard_map(
        body,
        mesh=mesh,
        in_specs=(
            P(None, "row", "col"),
            P("row", "col"),
            P("row", "col"),
            P(),
            P(None, ("row", "col")),
            P(None, ("row", "col")),
            P(None, ("row", "col"), None),
            P(None, ("row", "col")),
            P(None, "row", "col", None),
        ),
        out_specs=P(None, "row", "col"),
        check_vma=False,
    )
```
